256 devices in a mesh: py: 8 (over x, z_hi), pz: 32 (over z_lo, y, core).
Axes of the slice: x: 4, y: 4, z: 8 (z_hi: 2, z_lo: 4; z = z_hi * 4 + z_lo), core: 2. Of those that a mesh axis runs over, the one named last changes fastest.
Arguments:
- wavefunction: float32 [2, 512, 512, 512], P(None, 'pz', 'py'), may hold values from -4 to 4
- potential: float32 [512, 512, 512], P('pz', 'py'), may hold values from 0 to 400
Outputs:
- evolved: float32 [2, 512, 512, 512], P(None, 'pz', 'py')
The draws below stay inside these ranges and needn't reach their ends.
All inputs are finite; a program needn't handle non-finite values.
Results may differ from the reference program's by a relative error of at most 0.017.
Values may be sent and summed in bfloat16 or wider, within the bound.
A program may use at most 128 MiB of HBM per device.

```python
import jax
import jax.numpy as jnp
from jax import lax

NX = 512
NY = 512
NZ = 512


def block_levels(rng, shape, shards, smallest, high):
    def one(axis_at, blocks):
        heights = jax.random.uniform(jax.random.fold_in(jax.random.fold_in(rng, 6), axis_at), (blocks,), jnp.float32, smallest / len(shards), high / len(shards))
        return jnp.repeat(jnp.exp(heights), shape[axis_at] // blocks).reshape((-1,) + (1,) * (len(shape) - axis_at - 1))

    gain = one(*shards[0])
    for cut in shards[1:]:
        gain = gain * one(*cut)
    return gain


def normal_values(key, dims, deviation, reach, split=(), kind=jnp.bfloat16):
    array = jax.random.normal(key, dims, jnp.float32) * deviation
    if len(split) > 0:
        array = block_levels(key, dims, split, -0.22, 0.18) * array
    return jnp.clip(array, min=-reach, max=reach).astype(kind)


def setup_inputs(seed: int = 0) -> dict:
    key_of = jax.random.split(jax.random.key(seed), 3)
    wavefunction = normal_values(key_of[0], (2, NZ, NY, NX), 0.5, 4.0, ((1, 32), (2, 8)), jnp.float32)
    potential = jnp.clip(400.0 * jax.random.uniform(key_of[1], (NZ, NY, NX), jnp.float32) ** block_levels(key_of[1], (NZ, NY, NX), ((0, 32), (1, 8)), -0.2, 0.2), 0.0, 400.0)
    return dict(wavefunction=wavefunction, potential=potential)


time_step = 0.005
rotation = 0.9
coupling = 100.0
grid_spacing = 0.05
slab_count = 8


def spectral_tables(length):
    counter = jnp.arange(length, dtype=jnp.int32)
    product = (counter[:, None] * counter[None, :]) % length
    angles = product.astype(jnp.float32) * (2.0 * jnp.pi / length)
    return jnp.cos(angles).astype(jnp.bfloat16), jnp.sin(angles).astype(jnp.bfloat16)


def positions(length, offset, amount):
    counter = offset + jnp.arange(amount, dtype=jnp.int32) - length // 2
    return counter.astype(jnp.float32) * grid_spacing


def crank_factor(length, coefficient):
    spacing = grid_spacing
    angles = jnp.arange(length, dtype=jnp.int32).astype(jnp.float32) * (2.0 * jnp.pi / length)
    phase_rate = 0.5 * time_step * ((1.0 - jnp.cos(angles))[None, :] / (spacing * spacing) + coefficient[:, None] * jnp.sin(angles)[None, :] / spacing)
    denominator = 1.0 + phase_rate * phase_rate
    return (1.0 - phase_rate * phase_rate) / denominator, -2.0 * phase_rate / denominator


def potential_kick(field, potential):
    real_part = field[0].astype(jnp.float32)
    imag_part = field[1].astype(jnp.float32)
    angle = -0.5 * time_step * (potential + coupling * (real_part * real_part + imag_part * imag_part))
    cosine = jnp.cos(angle)
    sine = jnp.sin(angle)
    return jnp.stack([real_part * cosine - imag_part * sine, real_part * sine + imag_part * cosine])


def forward_last(field, cosines, sines):
    cos_part = jnp.dot(field, cosines, preferred_element_type=jnp.float32)
    sin_part = jnp.dot(field, sines, preferred_element_type=jnp.float32)
    return cos_part[0] + sin_part[1], cos_part[1] - sin_part[0]


def scale_modes(real_part, imag_part, fac_real, fac_imag):
    return jnp.stack([real_part * fac_real - imag_part * fac_imag, real_part * fac_imag + imag_part * fac_real]).astype(jnp.bfloat16)


def inverse_last(spectrum, cosines, sines, length):
    cos_part = jnp.dot(spectrum, cosines, preferred_element_type=jnp.float32)
    sin_part = jnp.dot(spectrum, sines, preferred_element_type=jnp.float32)
    return (jnp.stack([cos_part[0] - sin_part[1], cos_part[1] + sin_part[0]]) / length).astype(jnp.bfloat16)


def sweep_last(field, cosines, sines, fac_real, fac_imag, length):
    real_part, imag_part = forward_last(field, cosines, sines)
    return inverse_last(scale_modes(real_part, imag_part, fac_real, fac_imag), cosines, sines, length)


def reference(wavefunction, potential):
    kicked = potential_kick(wavefunction, potential).astype(jnp.bfloat16)
    cos_x, sin_x = spectral_tables(NX)
    cos_y, sin_y = spectral_tables(NY)
    cos_z, sin_z = spectral_tables(NZ)
    real_x, imag_x = crank_factor(NX, rotation * positions(NY, 0, NY))
    real_y, imag_y = crank_factor(NY, -rotation * positions(NX, 0, NX))
    real_z, imag_z = crank_factor(NZ, jnp.zeros((1,), jnp.float32))

    def first_block(block_index):
        slab = lax.dynamic_slice_in_dim(kicked, block_index * slab_count, slab_count, 1)
        return sweep_last(slab, cos_x, sin_x, real_x, imag_x, NX)

    swept = lax.map(first_block, jnp.arange(NZ // slab_count, dtype=jnp.int32))
    swept_first = jnp.moveaxis(swept, 0, 1).reshape(2, NZ, NY, NX)

    def second_block(block_index):
        slab = lax.dynamic_slice_in_dim(swept_first, block_index * slab_count, slab_count, 1)
        turned = jnp.swapaxes(slab, 2, 3)
        return jnp.swapaxes(sweep_last(turned, cos_y, sin_y, real_y, imag_y, NY), 2, 3)

    swept = lax.map(second_block, jnp.arange(NZ // slab_count, dtype=jnp.int32))
    swept_second = jnp.moveaxis(swept, 0, 1).reshape(2, NZ, NY, NX)

    def third_block(block_index):
        slab = lax.dynamic_slice_in_dim(swept_second, block_index * slab_count, slab_count, 2)
        turned = jnp.transpose(slab, (0, 2, 3, 1))
        result = sweep_last(turned, cos_z, sin_z, real_z, imag_z, NZ)
        return jnp.transpose(result, (0, 3, 1, 2))

    swept = lax.map(third_block, jnp.arange(NY // slab_count, dtype=jnp.int32))
    swept_third = jnp.moveaxis(swept, 0, 2).reshape(2, NZ, NY, NX)
    return potential_kick(swept_third.astype(jnp.float32), potential)
```

```python
import functools

import jax
import jax.numpy as jnp
import numpy as np
from jax import lax
from jax.experimental import pallas as pl
from jax.experimental.pallas import tpu as pltpu
from jax.sharding import PartitionSpec as P

time_step = 0.005
rotation = 0.9
coupling = 100.0
grid_spacing = 0.05

NX = 512
BY = 64
BZ = 16
QX = 128
GROUPS = BY // 8
TILES_Z = GROUPS * 4
TILES_Y = 8
ROWS = 2 * BZ * 8
CARRY = 32

MESH = pl.DeviceIdType.MESH
f32 = jnp.float32
bf16 = jnp.bfloat16


def line_roots(beta):
    beta = np.asarray(beta, np.float64)
    half = (beta - 1j) / 2
    spread = np.sqrt((1 + 1j) ** 2 - (beta - 1j) * (-beta - 1j))
    first = (-(1 + 1j) + spread) / (beta - 1j)
    second = (-(1 + 1j) - spread) / (beta - 1j)
    swap = np.abs(first) > np.abs(second)
    inner = np.where(swap, second, first)
    outer = np.where(swap, first, second)
    return inner, 1 / outer, half * (inner - outer)


def real_form(matrix):
    return np.stack(
        [
            np.stack([matrix.real, -matrix.imag], 1),
            np.stack([matrix.imag, matrix.real], 1),
        ],
        0,
    )


def x_tables():
    forward, inverse = [], []
    cells = np.arange(QX)
    for residue in range(4):
        modes = 4 * np.arange(QX) + residue
        angles = 2 * np.pi * ((cells[:, None] * modes[None, :]) % NX) / NX
        cosines, sines = np.cos(angles), np.sin(angles)
        forward.append(np.block([[cosines, -sines], [sines, cosines]]))
        inverse.append(np.block([[cosines.T, sines.T], [-sines.T, cosines.T]]) / NX)
    modes = 4 * np.arange(QX)[None, :] + np.arange(4)[:, None]
    theta = 2 * np.pi * modes / NX
    trig = np.stack([1 - np.cos(theta), np.sin(theta)], 1).reshape(8, QX)
    return np.stack(forward), np.stack(inverse), trig


def z_tables():
    lam, _, scale = line_roots(0.0)
    lam, scale = complex(lam), complex(scale)
    cells = np.arange(BZ)
    local = (2 / scale) * lam ** np.abs(cells[:, None] - cells[None, :]) - np.eye(BZ)
    carry = (2 / scale) * np.stack([lam ** (cells + 1), lam ** (BZ - cells)], 1)
    states = np.stack([lam ** (BZ - 1 - cells), lam**cells], 0)
    eye = np.eye(8)
    apply_field = np.einsum("azbw,ij->azibwj", real_form(local), eye)
    apply_field = apply_field.reshape(ROWS, ROWS)
    apply_carry = np.einsum("azbs,ij->azisbj", real_form(carry), eye).reshape(ROWS, CARRY)
    state_rows = np.einsum("asbz,ij->saibzj", real_form(states), eye).reshape(CARRY, ROWS)
    turn = np.zeros((BZ, 16, 3, 4, 8))
    fields, carries = real_form(local), real_form(carry)
    for end in range(2):
        for out in range(2):
            for part in range(2):
                row, column = 2 * end + out, 2 * end + part
                for half in range(2):
                    turn[:, row, half, column, :] = fields[out, :, part, 8 * half : 8 * half + 8]
                turn[:, row, 2, column, 0:2] = carries[out, :, part, :]
    turn = turn.reshape(BZ * 16, 3 * CARRY)
    return np.concatenate([apply_field, apply_carry], 1), state_rows, turn, lam**BZ


def y_tables(blocks):
    cells = np.arange(BY)
    angles = 2 * np.pi * ((cells[:, None] * cells[None, :]) % BY) / BY
    modes = np.exp(-1j * angles)
    forward = real_form(modes).reshape(2 * BY, 2 * BY)
    inverse = real_form(np.conj(modes) / BY).reshape(2 * BY, 2 * BY)
    beta = -0.5 * time_step * rotation * (np.arange(NX) - NX // 2)
    theta = 2 * np.pi * cells / BY
    rate = (1 - np.cos(theta))[:, None] + np.sin(theta)[:, None] * beta[None, :]
    solve = 1 / (1 + 1j * rate)
    edge = real_form((np.conj(modes) / BY)[[0, BY - 1]])
    edge_rows = np.einsum("asbk,ij->saijbk", edge, np.eye(8)).reshape(CARRY, 8 * 2 * BY)
    ends = np.zeros((BY, 2))
    ends[0, 0] = 1
    ends[BY - 1, 1] = 1
    spread = np.einsum("akbs->aksb", real_form(modes @ ends)).reshape(2 * BY, 4)
    keep = np.einsum("akbs->aksb", real_form(ends.astype(complex))).reshape(2 * BY, 4)
    none = np.zeros((2 * BY, 12))
    forward_ext = np.concatenate([forward, spread, none], 1)
    inverse_ext = np.concatenate([inverse, keep, none], 1)
    lam1, lam2, scale = line_roots(beta)
    whole1, whole2 = lam1**BY, lam2**BY
    up, down = (beta - 1j) / 2, (-beta - 1j) / 2
    rows = [
        scale / (1 - lam1 * lam2),
        lam1,
        lam2,
        whole1,
        whole2,
        1 / (1 - whole1**blocks),
        1 / (1 - whole2**blocks),
        down / scale * (whole1 - 1),
        down * lam2 / scale * (1 - whole2),
        up * lam1 / scale * (1 - whole1),
        up / scale * (whole2 - 1),
    ]
    table = np.stack([part for row in rows for part in (row.real, row.imag)])
    table = np.concatenate([table, np.zeros((24 - len(table), NX))]).reshape(24, 4, QX)
    return (
        forward,
        forward_ext,
        inverse_ext,
        np.stack([solve.real, solve.imag]),
        edge_rows,
        table.transpose(1, 0, 2),
    )


def kick(real_part, imag_part, potential):
    turn = -0.5 * time_step / (2 * np.pi)
    density = real_part * real_part + imag_part * imag_part
    turns = potential * turn + density * (turn * coupling)
    rest = turns - jnp.round(turns)
    square = rest * rest
    sine = rest * (
        4.44288283
        + square
        * (-7.30824115 + square * (3.60628896 + square * (-0.84576359 + square * 0.10920575)))
    )
    cosine = 1.4142135 + square * (
        -6.97885099 + square * (5.73946123 + square * (-1.88356328 + square * 0.31069871))
    )
    whole_cos = 1.0 - sine * sine
    whole_sin = sine * cosine
    return (
        real_part * whole_cos - imag_part * whole_sin,
        real_part * whole_sin + imag_part * whole_cos,
    )


def cmul(a, b):
    return a[0] * b[0] - a[1] * b[1], a[0] * b[1] + a[1] * b[0]


def cadd(a, b):
    return a[0] + b[0], a[1] + b[1]


def csub(a, b):
    return a[0] - b[0], a[1] - b[1]


def split_modes(real_part, imag_part):
    quarter = [
        (real_part[:, QX * p : QX * (p + 1)], imag_part[:, QX * p : QX * (p + 1)])
        for p in range(4)
    ]
    t0, t1 = cadd(quarter[0], quarter[2]), csub(quarter[0], quarter[2])
    t2, t3 = cadd(quarter[1], quarter[3]), csub(quarter[1], quarter[3])
    return [
        cadd(t0, t2),
        (t1[0] + t3[1], t1[1] - t3[0]),
        csub(t0, t2),
        (t1[0] - t3[1], t1[1] + t3[0]),
    ]


def join_modes(back):
    t0, t1 = cadd(back[0], back[2]), csub(back[0], back[2])
    t2, t3 = cadd(back[1], back[3]), csub(back[1], back[3])
    return [
        cadd(t0, t2),
        (t1[0] - t3[1], t1[1] + t3[0]),
        csub(t0, t2),
        (t1[0] + t3[1], t1[1] - t3[0]),
    ]


def x_sweep(count, load, factors, store, left, cells, forward_ref, inverse_ref):
    rows = 16 * count
    for n in range(count):
        mixed = split_modes(*load(n))
        for residue in range(4):
            left[residue, 16 * n : 16 * n + 16, :] = jnp.concatenate(
                mixed[residue], axis=1
            ).astype(bf16)
    for residue in range(4):
        modes = jnp.dot(left[residue, 0:rows, :], forward_ref[residue], preferred_element_type=f32)
        for n in range(count):
            some = modes[16 * n : 16 * n + 16]
            scaled = cmul((some[:, :QX], some[:, QX:]), factors(n)[residue])
            left[residue, 16 * n : 16 * n + 16, :] = jnp.concatenate(scaled, axis=1).astype(bf16)
    for residue in range(4):
        cells[residue, 0:rows, :] = jnp.dot(
            left[residue, 0:rows, :], inverse_ref[residue], preferred_element_type=f32
        )
    for n in range(0, count, 2):
        done = []
        for at in range(2):
            lines = slice(16 * (n + at), 16 * (n + at) + 16)
            some = [cells[residue, lines, :] for residue in range(4)]
            out = join_modes([(one[:, :QX], one[:, QX:]) for one in some])
            done.append([jnp.concatenate([one[part] for one in out], axis=1) for part in range(2)])
        store(n, done)


def main_kernel(
    count_py,
    count_pz,
    z_step,
    wave_hbm,
    pot_hbm,
    xf_hbm,
    xi_hbm,
    trig_ref,
    zapply_ref,
    zstate_ref,
    yf_ref,
    solve_ref,
    edge_ref,
    turn_ref,
    ytab_ref,
    field_hbm,
    change_hbm,
    wave,
    pot,
    xf,
    xi,
    grid,
    field,
    swept,
    left_buf,
    cells_buf,
    modes_buf,
    z_states,
    z_partner,
    z_send,
    z_recv,
    z_back,
    z_chip,
    z_give,
    z_carry,
    y_send,
    y_recv,
    y_back,
    y_carry,
    c_send,
    c_recv,
    c_back,
    c_carry,
    change,
    in_sem,
    tab_sem,
    out_sem,
    pair_sems,
    z_sems,
    z_back_sems,
    y_sems,
    c_sems,
):
    me_y = lax.axis_index("py")
    me_z = lax.axis_index("pz")
    core = lax.rem(me_z, 2)
    chip = me_z // 2
    partner = me_z + 1 - 2 * core
    chips = count_pz // 2
    half_z = TILES_Z // 2
    tiles_z = half_z // chips
    mine = core * half_z
    theirs = half_z - mine

    def load(group):
        rows = pl.ds(pl.multiple_of(group * 8, 8), 8)
        return (
            pltpu.make_async_copy(wave_hbm.at[:, :, rows, :], wave.at[group], in_sem.at[0, group]),
            pltpu.make_async_copy(pot_hbm.at[:, rows, :], pot.at[group], in_sem.at[1, group]),
        )

    for group in range(GROUPS):
        for copy in load(group):
            copy.start()
    table_copies = (
        pltpu.make_async_copy(xf_hbm, xf, tab_sem.at[0]),
        pltpu.make_async_copy(xi_hbm, xi, tab_sem.at[1]),
    )
    for copy in table_copies:
        copy.start()

    barrier = pltpu.get_barrier_semaphore()

    def twin(other):
        return {"pz": other * 2 + core}

    pl.semaphore_signal(barrier, inc=1, device_id={"pz": partner}, device_id_type=MESH)

    @pl.loop(1, chips)
    def _(step):
        pl.semaphore_signal(
            barrier, inc=1, device_id=twin(lax.rem(chip + step, chips)), device_id_type=MESH
        )

    @pl.loop(1, count_py)
    def _(step):
        pl.semaphore_signal(
            barrier, inc=1, device_id={"py": lax.rem(me_y + step, count_py)}, device_id_type=MESH
        )

    def kick_group(group):
        for copy in load(group):
            copy.wait()
        for some in range(BZ // 2):
            planes = slice(2 * some, 2 * some + 2)
            new = kick(wave[group, 0, planes], wave[group, 1, planes], pot[group, planes])
            for part in range(2):
                start = ROWS // 2 * part + 16 * some
                grid[group, start : start + 16, :] = new[part].reshape(16, NX).astype(bf16)
        states = jnp.dot(
            zstate_ref[...], grid[group, 0:ROWS, :], preferred_element_type=f32
        ).astype(bf16)
        for quarter in range(4):
            z_states[group * 4 + quarter] = states[:, QX * quarter : QX * (quarter + 1)].reshape(
                2, 16, QX
            )

    def pair_out(step):
        return pltpu.make_async_remote_copy(
            src_ref=z_states.at[pl.ds(theirs + 4 * step, 4)],
            dst_ref=z_partner.at[pl.ds(4 * step, 4)],
            send_sem=pair_sems.at[0, step],
            recv_sem=pair_sems.at[1, step],
            device_id={"pz": partner},
            device_id_type=MESH,
        )

    def pair_back():
        return pltpu.make_async_remote_copy(
            src_ref=z_give,
            dst_ref=z_carry.at[pl.ds(mine, half_z)],
            send_sem=pair_sems.at[0, 4],
            recv_sem=pair_sems.at[1, 4],
            device_id={"pz": partner},
            device_id_type=MESH,
        )

    def pair_returned():
        return pltpu.make_async_remote_copy(
            src_ref=z_give,
            dst_ref=z_carry.at[pl.ds(theirs, half_z)],
            send_sem=pair_sems.at[0, 4],
            recv_sem=pair_sems.at[1, 4],
            device_id={"pz": partner},
            device_id_type=MESH,
        )

    def z_out(tile):
        return pltpu.make_async_remote_copy(
            src_ref=z_send.at[tile],
            dst_ref=z_recv.at[chip, lax.rem(tile, tiles_z)],
            send_sem=z_sems.at[0, tile],
            recv_sem=z_sems.at[1, chip * tiles_z + lax.rem(tile, tiles_z)],
            device_id=twin(tile // tiles_z),
            device_id_type=MESH,
        )

    def z_in(step, tile):
        peer = lax.rem(chip + step, chips)
        return pltpu.make_async_remote_copy(
            src_ref=z_send.at[tile],
            dst_ref=z_recv.at[peer, tile],
            send_sem=z_sems.at[0, tile],
            recv_sem=z_sems.at[1, peer * tiles_z + tile],
            device_id=twin(peer),
            device_id_type=MESH,
        )

    def z_return(step):
        peer = lax.rem(chip + step, chips)
        return pltpu.make_async_remote_copy(
            src_ref=z_back.at[peer],
            dst_ref=z_chip.at[pl.ds(chip * tiles_z, tiles_z)],
            send_sem=z_back_sems.at[0, peer],
            recv_sem=z_back_sems.at[1, chip],
            device_id=twin(peer),
            device_id_type=MESH,
        )

    def z_returned(step):
        peer = lax.rem(chip + step, chips)
        return pltpu.make_async_remote_copy(
            src_ref=z_back.at[chip],
            dst_ref=z_chip.at[pl.ds(peer * tiles_z, tiles_z)],
            send_sem=z_back_sems.at[0, chip],
            recv_sem=z_back_sems.at[1, peer],
            device_id=twin(peer),
            device_id_type=MESH,
        )

    lead = core == 0
    block_step = (z_step.real, z_step.imag)
    chip_step = z_step * z_step

    def parts(array):
        array = array.astype(f32)
        return array[0:8], array[8:16]

    def choose(first, second):
        return jnp.where(lead, first[0], second[0]), jnp.where(lead, first[1], second[1])

    def joined(value):
        return jnp.concatenate(value, axis=0).astype(bf16)

    @pl.loop(0, GROUPS // 2)
    def _(step):
        kick_group(theirs // 4 + step)

        @pl.when(step == 0)
        def _():
            pl.semaphore_wait(barrier, chips + count_py - 1)

        pair_out(step).start()

    @pl.loop(0, GROUPS // 2)
    def _(count):
        step = lax.rem(count + chip // 4, GROUPS // 2)
        kick_group(mine // 4 + step)
        pair_out(step).wait_recv()
        for at in range(4):
            tile = step * 4 + at
            own = [parts(z_states[mine + tile, side]) for side in range(2)]
            other = [parts(z_partner[tile, side]) for side in range(2)]
            left = cadd(choose(other[0], own[0]), cmul(choose(own[0], other[0]), block_step))
            right = cadd(choose(own[1], other[1]), cmul(choose(other[1], own[1]), block_step))
            z_send[tile, 0] = joined(left)
            z_send[tile, 1] = joined(right)
            owner = tile // tiles_z

            @pl.when(owner != chip)
            def _():
                z_out(tile).start()

            @pl.when(owner == chip)
            def _():
                z_recv[chip, lax.rem(tile, tiles_z)] = z_send[tile]

    for copy in table_copies:
        copy.wait()

    def factors_of(group):
        cell = lax.broadcasted_iota(jnp.int32, (8, QX), 0) + (
            me_y * BY + group * 8 - count_py * BY // 2
        )
        beta = cell.astype(f32) * (0.5 * time_step * rotation)
        out = []
        for residue in range(4):
            rate = trig_ref[2 * residue : 2 * residue + 1] + beta * trig_ref[
                2 * residue + 1 : 2 * residue + 2
            ]
            scale = 1.0 / (1.0 + rate * rate)
            out.append(((1.0 - rate * rate) * scale, -2.0 * rate * scale))
        return out

    def twice(factors):
        return [tuple(jnp.concatenate([part, part], axis=0) for part in one) for one in factors]

    all_factors = [twice(factors_of(group)) for group in range(GROUPS)]

    def sweep_half(half):
        def place(n):
            return n // 8 * 2 + n % 2, half * 4 + n // 2 % 4

        def fetch(n):
            group, some = place(n)
            return tuple(
                grid[group, start : start + 16, :].astype(f32)
                for start in (16 * some, 16 * some + ROWS // 2)
            )

        def put(n, done):
            group, some = place(n)
            for part in range(2):
                start = 16 * some + part * ROWS // 2
                for at in range(2):
                    grid[group + at, start : start + 16, :] = done[at][part].astype(bf16)
                for plane in range(2):
                    lines = slice(8 * plane, 8 * plane + 8)
                    swept[part, 2 * some + plane, 8 * group : 8 * group + 16, :] = jnp.concatenate(
                        [done[0][part][lines], done[1][part][lines]], axis=0
                    ).astype(bf16)

        x_sweep(
            GROUPS * 4, fetch, lambda n: all_factors[place(n)[0]], put, left_buf, cells_buf, xf, xi
        )

    def y_edges(planes, matrix):
        for at, plane in enumerate(planes):
            for side in range(2):
                lanes = slice(side * NX // 2, (side + 1) * NX // 2)
                block = jnp.concatenate(
                    [swept[part, plane, :, lanes] for part in range(2)], axis=0
                )
                modes = jnp.dot(yf_ref[...], block, preferred_element_type=f32)
                for some in range(0, BY, 32):
                    scaled = cmul(
                        (modes[some : some + 32], modes[BY + some : BY + some + 32]),
                        (
                            solve_ref[0, some : some + 32, lanes],
                            solve_ref[1, some : some + 32, lanes],
                        ),
                    )
                    for part in range(2):
                        start = at * 2 * BY + part * BY + some
                        modes_buf[start : start + 32, lanes] = scaled[part].astype(bf16)
        rows = len(planes) * 2 * BY
        return jnp.dot(matrix, modes_buf[0:rows, :], preferred_element_type=f32).astype(bf16)

    class Exchange:
        def __init__(self, send, recv, back, carry, sems, tiles, stride):
            self.send, self.recv, self.back, self.carry = send, recv, back, carry
            self.sems, self.tiles, self.stride = sems, tiles, stride

        def mine(self):
            return pl.ds(me_y // self.stride * self.tiles, self.tiles)

        def own(self):
            return lax.rem(me_y, self.stride) == 0

        def out(self, peer):
            return pltpu.make_async_remote_copy(
                src_ref=self.send.at[pl.ds(peer // self.stride * self.tiles, self.tiles)],
                dst_ref=self.recv.at[me_y],
                send_sem=self.sems.at[0, peer],
                recv_sem=self.sems.at[1, me_y],
                device_id={"py": peer},
                device_id_type=MESH,
            )

        def arrived(self, peer):
            return pltpu.make_async_remote_copy(
                src_ref=self.send.at[self.mine()],
                dst_ref=self.recv.at[peer],
                send_sem=self.sems.at[0, me_y],
                recv_sem=self.sems.at[1, peer],
                device_id={"py": peer},
                device_id_type=MESH,
            )

        def give(self, peer):
            return pltpu.make_async_remote_copy(
                src_ref=self.back.at[peer],
                dst_ref=self.carry.at[self.mine()],
                send_sem=self.sems.at[2, peer],
                recv_sem=self.sems.at[3, me_y],
                device_id={"py": peer},
                device_id_type=MESH,
            )

        def given(self, peer):
            return pltpu.make_async_remote_copy(
                src_ref=self.back.at[me_y],
                dst_ref=self.carry.at[pl.ds(peer // self.stride * self.tiles, self.tiles)],
                send_sem=self.sems.at[2, me_y],
                recv_sem=self.sems.at[3, peer],
                device_id={"py": peer},
                device_id_type=MESH,
            )

        def post(self, peers):
            for peer in peers:

                @pl.when(peer != me_y)
                def _():
                    self.out(peer).start()

        def answer(self):
            @pl.when(self.own())
            def _():
                self.recv[me_y] = self.send[self.mine()]

                @pl.loop(1, count_py)
                def _(step):
                    self.arrived(lax.rem(me_y + step, count_py)).wait_recv()

                for tile in range(self.tiles):
                    solve_tile(
                        self.recv,
                        self.back,
                        tile,
                        lax.rem(me_y // self.stride * self.tiles + tile, 4),
                    )

                @pl.loop(1, count_py)
                def _(step):
                    self.give(lax.rem(me_y + step, count_py)).start()

                self.carry[self.mine()] = self.back[me_y]

        def receive(self):
            for peer in range(0, count_py, self.stride):

                @pl.when(peer != me_y)
                def _():
                    self.given(peer).wait_recv()

        def close(self):
            for peer in range(0, count_py, self.stride):

                @pl.when(peer != me_y)
                def _():
                    self.out(peer).wait_send()

            @pl.when(self.own())
            def _():
                @pl.loop(1, count_py)
                def _(step):
                    self.give(lax.rem(me_y + step, count_py)).wait_send()

        def rows(self, tiles):
            return jnp.concatenate(
                [self.carry[tile].reshape(CARRY, QX) for tile in tiles], axis=1
            )

    def solve_tile(recv, back, tile, quarter):
        table = ytab_ref[quarter]
        value = [(table[2 * n : 2 * n + 1], table[2 * n + 1 : 2 * n + 2]) for n in range(11)]
        gain, lam1, lam2, whole1, whole2, wrap1, wrap2, d0l, d0r, d63l, d63r = value
        left_own, right_own = [], []
        for block in range(count_py):
            first, last = parts(recv[block, tile, 0]), parts(recv[block, tile, 1])
            left_own.append(cmul(csub(last, cmul(first, lam2)), gain))
            right_own.append(cmul(csub(first, cmul(last, lam1)), gain))
        left_state = [csub(one, cmul(one, whole1)) for one in left_own]
        right_state = [csub(one, cmul(one, whole2)) for one in right_own]
        left, right = left_state[0], right_state[count_py - 1]
        for block in range(1, count_py):
            left = cadd(left_state[block], cmul(left, whole1))
            right = cadd(right_state[count_py - 1 - block], cmul(right, whole2))
        left, right = cmul(left, wrap1), cmul(right, wrap2)
        lefts, rights = [None] * count_py, [None] * count_py
        for block in range(count_py):
            other = count_py - 1 - block
            lefts[block], rights[other] = left, right
            left = cadd(left_state[block], cmul(left, whole1))
            right = cadd(right_state[other], cmul(right, whole2))
        for block in range(count_py):
            from_left = csub(lefts[block], left_own[block])
            from_right = csub(rights[block], right_own[block])
            back[block, tile, 0] = joined(cadd(cmul(from_left, d0l), cmul(from_right, d0r)))
            back[block, tile, 1] = joined(cadd(cmul(from_left, d63l), cmul(from_right, d63r)))

    planes_y = Exchange(y_send, y_recv, y_back, y_carry, y_sems, TILES_Y // count_py, 1)
    carry_stride = max(1, count_py // 4)
    carry_y = Exchange(
        c_send, c_recv, c_back, c_carry, c_sems, max(1, 4 // count_py), carry_stride
    )

    def post_half(half):
        edges = y_edges(range(half * 8, half * 8 + 8), edge_ref[...])
        for quarter in range(4):
            y_send[half * 4 + quarter] = edges[:, QX * quarter : QX * (quarter + 1)].reshape(
                2, 16, QX
            )
        planes_y.post(range(half * count_py // 2, (half + 1) * count_py // 2))

    sweep_half(0)
    post_half(0)

    @pl.loop(1, chips)
    def _(step):
        for tile in range(tiles_z):
            z_in(step, tile).wait_recv()

    for tile in range(tiles_z):

        def state(block, side):
            return parts(z_recv[block, tile, side])

        def advance(total, value):
            return cadd(cmul(total, (chip_step.real, chip_step.imag)), value)

        def gather(step, carry):
            left, right = carry
            return (
                advance(left, state(step, 0)),
                advance(right, state(chips - 1 - step, 1)),
            )

        zero = (jnp.zeros((8, QX), f32), jnp.zeros((8, QX), f32))
        left, right = lax.fori_loop(0, chips, gather, (zero, zero), unroll=2)
        wrap = 1 / (1 - chip_step**chips)
        left = cmul(left, (wrap.real, wrap.imag))
        right = cmul(right, (wrap.real, wrap.imag))

        def hand_out(step, carry):
            left, right = carry
            last = chips - 1 - step
            z_back[step, tile, 0] = joined(left)
            z_back[last, tile, 1] = joined(right)
            return advance(left, state(step, 0)), advance(right, state(last, 1))

        lax.fori_loop(0, chips, hand_out, (left, right), unroll=2)

    @pl.loop(1, chips)
    def _(step):
        z_return(step).start()

    z_chip[pl.ds(chip * tiles_z, tiles_z)] = z_back[chip]

    sweep_half(1)
    post_half(1)

    @pl.loop(1, chips)
    def _(step):
        z_returned(step).wait_recv()

    @pl.loop(0, half_z)
    def _(tile):
        own = [parts(z_states[mine + tile, side]) for side in range(2)]
        other = [parts(z_partner[tile, side]) for side in range(2)]
        whole = [parts(z_chip[tile, side]) for side in range(2)]
        inner_left = cadd(choose(own[0], other[0]), cmul(whole[0], block_step))
        inner_right = cadd(choose(other[1], own[1]), cmul(whole[1], block_step))
        z_give[tile, 0] = joined(choose(inner_left, whole[0]))
        z_give[tile, 1] = joined(choose(whole[1], inner_right))
        z_carry[mine + tile, 0] = joined(choose(whole[0], inner_left))
        z_carry[mine + tile, 1] = joined(choose(inner_right, whole[1]))

    pair_back().start()

    pair_returned().wait_recv()

    def fetch(n):
        sides = [
            jnp.concatenate([z_carry[n * 4 + quarter, side] for quarter in range(4)], axis=1)
            for side in range(2)
        ]
        sides = [side.astype(f32) for side in sides]
        return tuple(
            jnp.concatenate([side[8 * part : 8 * part + 8] for side in sides], axis=0)
            for part in range(2)
        )

    def put(n, done):
        for side in range(2):
            lines = slice(8 * side, 8 * side + 8)
            start = ROWS + 16 * side
            for at in range(2):
                grid[n + at, start : start + 16, :] = jnp.concatenate(
                    [done[at][part][lines] for part in range(2)], axis=0
                ).astype(bf16)
            for part in range(2):
                swept[part, BZ + side, 8 * n : 8 * n + 16, :] = jnp.concatenate(
                    [done[at][part][lines] for at in range(2)], axis=0
                ).astype(bf16)

    x_sweep(GROUPS, fetch, lambda n: all_factors[n], put, left_buf, cells_buf, xf, xi)
    edges = y_edges((BZ, BZ + 1), edge_ref[:, 0 : 4 * BY])
    for quarter in range(4):
        c_send[quarter] = edges[:, QX * quarter : QX * (quarter + 1)].reshape(2, 16, QX)
    carry_y.post(range(0, count_py, carry_stride))
    planes_y.answer()

    def store(pair):
        rows = pl.ds(pl.multiple_of(pair * 16, 16), 16)
        return pltpu.make_async_copy(
            field.at[:, :, rows, :], field_hbm.at[:, :, rows, :], out_sem.at[pair]
        )

    @pl.loop(0, GROUPS // 2)
    def _(pair):
        rows = pl.ds(pl.multiple_of(pair * 16, 16), 16)
        for side in range(2):
            lanes = slice(side * NX // 2, (side + 1) * NX // 2)
            halves = [
                jnp.dot(
                    zapply_ref[...], grid[2 * pair + at, :, lanes], preferred_element_type=f32
                ).reshape(2, BZ, 8, NX // 2)
                for at in range(2)
            ]
            for part in range(2):
                for plane in range(BZ):
                    field[part, plane, rows, lanes] = jnp.concatenate(
                        [half[part, plane] for half in halves], axis=0
                    ).astype(bf16)
        store(pair).start()

    carry_y.answer()
    planes_y.receive()
    carry_y.receive()
    rows = [planes_y.rows(range(4)), planes_y.rows(range(4, 8)), carry_y.rows(range(4))]
    change[...] = (
        jnp.dot(turn_ref[...], jnp.concatenate(rows, axis=0), preferred_element_type=f32)
        .astype(bf16)
        .reshape(BZ, 16, NX)
    )
    last = pltpu.make_async_copy(change, change_hbm, out_sem.at[GROUPS // 2])
    last.start()

    @pl.loop(0, half_z)
    def _(tile):
        @pl.when(tile // tiles_z != chip)
        def _():
            z_out(tile).wait_send()

    @pl.loop(1, chips)
    def _(step):
        z_return(step).wait_send()

    @pl.loop(0, GROUPS // 2)
    def _(step):
        pair_out(step).wait_send()

    pair_back().wait_send()

    planes_y.close()
    carry_y.close()

    @pl.loop(0, GROUPS // 2)
    def _(pair):
        store(pair).wait()

    last.wait()


PLANES = 2


def finish_kernel(
    field_hbm,
    change_hbm,
    pot_hbm,
    factor_hbm,
    yf_ref,
    yi_ref,
    out_hbm,
    field,
    change,
    pot,
    factor,
    out,
    in_sem,
    tab_sem,
    out_sem,
):
    steps = BZ // PLANES

    def load(step):
        planes = pl.ds(step * PLANES, PLANES)
        return (
            pltpu.make_async_copy(field_hbm.at[:, planes], field.at[:, planes], in_sem.at[0, step]),
            pltpu.make_async_copy(pot_hbm.at[planes], pot.at[planes], in_sem.at[1, step]),
        )

    def save(step):
        planes = pl.ds(step * PLANES, PLANES)
        return pltpu.make_async_copy(out.at[:, planes], out_hbm.at[:, planes], out_sem.at[step])

    tables = (
        pltpu.make_async_copy(change_hbm, change, tab_sem.at[0]),
        pltpu.make_async_copy(factor_hbm, factor, tab_sem.at[1]),
    )
    for copy in tables:
        copy.start()
    for step in range(steps):
        for copy in load(step):
            copy.start()
    for copy in tables:
        copy.wait()

    def finish(at, lanes):
        rows = jnp.concatenate(
            [field[0, at, :, lanes], field[1, at, :, lanes], change[at, :, lanes]], axis=0
        )
        modes = jnp.dot(yf_ref[...], rows, preferred_element_type=f32)
        scaled = [
            cmul(
                (modes[some : some + 32], modes[BY + some : BY + some + 32]),
                (factor[0, some : some + 32, lanes], factor[1, some : some + 32, lanes]),
            )
            for some in range(0, BY, 32)
        ]
        rows = jnp.concatenate(
            [one[part].astype(bf16) for part in range(2) for one in scaled]
            + [change[at, :, lanes]],
            axis=0,
        )
        cells = jnp.dot(yi_ref[...], rows, preferred_element_type=f32)
        for some in range(0, BY, 32):
            new = kick(
                cells[some : some + 32],
                cells[BY + some : BY + some + 32],
                pot[at, some : some + 32, lanes],
            )
            for part in range(2):
                out[part, at, some : some + 32, lanes] = new[part]

    @pl.loop(0, steps)
    def _(step):
        for copy in load(step):
            copy.wait()
        for one in range(PLANES):
            for side in range(2):
                finish(step * PLANES + one, slice(side * NX // 2, (side + 1) * NX // 2))
        save(step).start()

    @pl.loop(0, steps)
    def _(step):
        save(step).wait()


def shards(count_py, count_pz, wavefunction, potential):
    forward_x, inverse_x, trig = x_tables()
    z_apply, z_states, turn, z_step = z_tables()
    forward_y, forward_ext, inverse_ext, solve, edges, y_table = y_tables(count_py)
    factor = np.stack([2 * solve[0] - 1, 2 * solve[1]])

    def low(array):
        return jnp.asarray(array.astype(np.float32)).astype(bf16)

    def full(array):
        return jnp.asarray(array.astype(np.float32))

    chips = count_pz // 2
    tiles_z = TILES_Z // 2 // chips
    tiles_y = TILES_Y // count_py
    tiles_c = max(1, 4 // count_py)
    anywhere = pl.BlockSpec(memory_space=pl.ANY)
    inside = pl.BlockSpec(memory_space=pltpu.VMEM)
    field, change = pl.pallas_call(
        functools.partial(main_kernel, count_py, count_pz, z_step),
        out_shape=(
            jax.ShapeDtypeStruct((2, BZ, BY, NX), bf16),
            jax.ShapeDtypeStruct((BZ, 16, NX), bf16),
        ),
        in_specs=[anywhere] * 4 + [inside] * 8,
        out_specs=(anywhere, anywhere),
        scratch_shapes=[
            pltpu.VMEM((GROUPS, 2, BZ, 8, NX), f32),
            pltpu.VMEM((GROUPS, BZ, 8, NX), f32),
            pltpu.VMEM((4, 2 * QX, 2 * QX), bf16),
            pltpu.VMEM((4, 2 * QX, 2 * QX), bf16),
            pltpu.VMEM((GROUPS, ROWS + CARRY, NX), bf16),
            pltpu.VMEM((2, BZ, BY, NX), bf16),
            pltpu.VMEM((2, BZ + 2, BY, NX), bf16),
            pltpu.VMEM((4, GROUPS * BZ * 4, 2 * QX), bf16),
            pltpu.VMEM((4, GROUPS * BZ * 4, 2 * QX), f32),
            pltpu.VMEM((8 * 2 * BY, NX), bf16),
            pltpu.VMEM((TILES_Z, 2, 16, QX), bf16),
            pltpu.VMEM((TILES_Z // 2, 2, 16, QX), bf16),
            pltpu.VMEM((TILES_Z // 2, 2, 16, QX), bf16),
            pltpu.VMEM((chips, tiles_z, 2, 16, QX), bf16),
            pltpu.VMEM((chips, tiles_z, 2, 16, QX), bf16),
            pltpu.VMEM((TILES_Z // 2, 2, 16, QX), bf16),
            pltpu.VMEM((TILES_Z // 2, 2, 16, QX), bf16),
            pltpu.VMEM((TILES_Z, 2, 16, QX), bf16),
            pltpu.VMEM((TILES_Y, 2, 16, QX), bf16),
            pltpu.VMEM((count_py, tiles_y, 2, 16, QX), bf16),
            pltpu.VMEM((count_py, tiles_y, 2, 16, QX), bf16),
            pltpu.VMEM((TILES_Y, 2, 16, QX), bf16),
            pltpu.VMEM((4, 2, 16, QX), bf16),
            pltpu.VMEM((count_py, tiles_c, 2, 16, QX), bf16),
            pltpu.VMEM((count_py, tiles_c, 2, 16, QX), bf16),
            pltpu.VMEM((4, 2, 16, QX), bf16),
            pltpu.VMEM((BZ, 16, NX), bf16),
            pltpu.SemaphoreType.DMA((2, GROUPS)),
            pltpu.SemaphoreType.DMA((2,)),
            pltpu.SemaphoreType.DMA((GROUPS // 2 + 1,)),
            pltpu.SemaphoreType.DMA((2, 5)),
            pltpu.SemaphoreType.DMA((2, TILES_Z // 2)),
            pltpu.SemaphoreType.DMA((2, chips)),
            pltpu.SemaphoreType.DMA((4, count_py)),
            pltpu.SemaphoreType.DMA((4, count_py)),
        ],
        compiler_params=pltpu.CompilerParams(
            collective_id=0, has_side_effects=True, vmem_limit_bytes=56 * 2**20
        ),
        cost_estimate=pl.CostEstimate(
            flops=3_000_000_000, bytes_accessed=10_000_000, transcendentals=0
        ),
        name="sweeps",
    )(
        wavefunction,
        potential,
        low(forward_x),
        low(inverse_x),
        full(trig),
        low(z_apply),
        low(z_states),
        low(forward_y),
        full(solve),
        low(edges),
        low(turn),
        full(y_table),
    )
    return pl.pallas_call(
        finish_kernel,
        out_shape=jax.ShapeDtypeStruct((2, BZ, BY, NX), f32),
        in_specs=[anywhere] * 4 + [inside] * 2,
        out_specs=anywhere,
        scratch_shapes=[
            pltpu.VMEM((2, BZ, BY, NX), bf16),
            pltpu.VMEM((BZ, 16, NX), bf16),
            pltpu.VMEM((BZ, BY, NX), f32),
            pltpu.VMEM(factor.shape, f32),
            pltpu.VMEM((2, BZ, BY, NX), f32),
            pltpu.SemaphoreType.DMA((2, BZ // PLANES)),
            pltpu.SemaphoreType.DMA((2,)),
            pltpu.SemaphoreType.DMA((BZ // PLANES,)),
        ],
        compiler_params=pltpu.CompilerParams(vmem_limit_bytes=60 * 2**20),
        cost_estimate=pl.CostEstimate(
            flops=800_000_000, bytes_accessed=9_000_000, transcendentals=0
        ),
        name="finish",
    )(field, change, potential, full(factor), low(forward_ext), low(inverse_ext))


def solution(mesh):
    return jax.shard_map(
        functools.partial(shards, mesh.shape["py"], mesh.shape["pz"]),
        mesh=mesh,
        in_specs=(P(None, "pz", "py", None), P("pz", "py", None)),
        out_specs=P(None, "pz", "py", None),
        check_vma=False,
    )
```

```python
import functools

import jax
import jax.numpy as jnp
import numpy as np
from jax import lax
from jax.experimental import pallas as pl
from jax.experimental.pallas import tpu as pltpu
from jax.sharding import PartitionSpec as P

time_step = 0.005
rotation = 0.9
coupling = 100.0
grid_spacing = 0.05

NX = 512
BY = 64
BZ = 16
QX = 128
GROUPS = BY // 8
TILES_Z = GROUPS * 4
TILES_Y = 8
ROWS = 2 * BZ * 8
CARRY = 32

MESH = pl.DeviceIdType.MESH
f32 = jnp.float32
bf16 = jnp.bfloat16


def line_roots(beta):
    beta = np.asarray(beta, np.float64)
    half = (beta - 1j) / 2
    spread = np.sqrt((1 + 1j) ** 2 - (beta - 1j) * (-beta - 1j))
    first = (-(1 + 1j) + spread) / (beta - 1j)
    second = (-(1 + 1j) - spread) / (beta - 1j)
    swap = np.abs(first) > np.abs(second)
    inner = np.where(swap, second, first)
    outer = np.where(swap, first, second)
    return inner, 1 / outer, half * (inner - outer)


def real_form(matrix):
    return np.stack(
        [
            np.stack([matrix.real, -matrix.imag], 1),
            np.stack([matrix.imag, matrix.real], 1),
        ],
        0,
    )


def x_tables():
    forward, inverse = [], []
    cells = np.arange(QX)
    for residue in range(4):
        modes = 4 * np.arange(QX) + residue
        angles = 2 * np.pi * ((cells[:, None] * modes[None, :]) % NX) / NX
        cosines, sines = np.cos(angles), np.sin(angles)
        forward.append(np.block([[cosines, -sines], [sines, cosines]]))
        inverse.append(np.block([[cosines.T, sines.T], [-sines.T, cosines.T]]) / NX)
    modes = 4 * np.arange(QX)[None, :] + np.arange(4)[:, None]
    theta = 2 * np.pi * modes / NX
    trig = np.stack([1 - np.cos(theta), np.sin(theta)], 1).reshape(8, QX)
    return np.stack(forward), np.stack(inverse), trig


def z_tables():
    lam, _, scale = line_roots(0.0)
    lam, scale = complex(lam), complex(scale)
    cells = np.arange(BZ)
    local = (2 / scale) * lam ** np.abs(cells[:, None] - cells[None, :]) - np.eye(BZ)
    carry = (2 / scale) * np.stack([lam ** (cells + 1), lam ** (BZ - cells)], 1)
    states = np.stack([lam ** (BZ - 1 - cells), lam**cells], 0)
    eye = np.eye(8)
    apply_field = np.einsum("azbw,ij->aizbwj", real_form(local), eye).reshape(ROWS, ROWS)
    state_rows = np.einsum("asbz,ij->saibzj", real_form(states), eye).reshape(CARRY, ROWS)
    turn = np.zeros((4, BZ, 8, 3, 4, 8))
    fields, carries = real_form(np.eye(BZ).astype(complex)), real_form(carry)
    for end in range(2):
        for out in range(2):
            for part in range(2):
                row, column = 2 * end + out, 2 * end + part
                for half in range(2):
                    turn[:, :, row, half, column, :] = fields[
                        out, :, part, 8 * half : 8 * half + 8
                    ]
                for quarter in range(4):
                    lines = slice(2 * quarter, 2 * quarter + 2)
                    turn[quarter, :, row, 2, column, lines] = carries[out, :, part, :]
    turn = turn.reshape(4, BZ * 8, 3 * CARRY)
    return np.concatenate([apply_field, state_rows], 0), turn, carry, lam**BZ


def y_tables(blocks):
    cells = np.arange(BY)
    angles = 2 * np.pi * ((cells[:, None] * cells[None, :]) % BY) / BY
    modes = np.exp(-1j * angles)
    forward = real_form(modes).reshape(2 * BY, 2 * BY)
    inverse = real_form(np.conj(modes) / BY).reshape(2 * BY, 2 * BY)
    beta = -0.5 * time_step * rotation * (np.arange(NX) - NX // 2)
    theta = 2 * np.pi * cells / BY
    rate = (1 - np.cos(theta))[:, None] + np.sin(theta)[:, None] * beta[None, :]
    factor = (1 - 1j * rate) / (1 + 1j * rate)
    lam1, lam2, scale = line_roots(beta)
    whole1, whole2 = lam1**BY, lam2**BY
    rows = [
        whole1,
        whole2,
        1 / (1 - whole1),
        1 / (1 - whole2),
        1 / (1 - whole1**blocks),
        1 / (1 - whole2**blocks),
        2 * lam1 / scale,
        2 * lam2 / scale,
    ]
    apart = 1 - lam1 * lam2
    steps = [lam1, lam2, lam1 / apart, 2 * apart / scale]
    table = np.stack([part for row in rows for part in (row.real, row.imag)])
    down, up = np.arange(BY)[:, None], BY - 1 - np.arange(BY)[:, None]
    states = [lam1**up, lam2**down]
    homogeneous = [lam1**down, lam2**up]
    add = np.zeros((4, 4, 8, 4, 2, 8))
    for quarter in range(4):
        for plane in range(2):
            for part in range(4):
                add[quarter, part, 2 * quarter + plane, part, plane, :] = 1
    add = add.reshape(4, CARRY, 64)
    table = table.reshape(len(table), 4, QX)
    packed = np.repeat(table, 2, axis=1)
    table = table.transpose(1, 0, 2)

    def parts(values):
        return np.stack([part for value in values for part in (value.real, value.imag)])

    return (
        forward,
        inverse,
        parts([factor]),
        parts(states),
        parts(homogeneous),
        parts(steps),
        add,
        table,
        packed,
    )


def kick(real_part, imag_part, potential):
    turn = -0.5 * time_step / (2 * np.pi)
    density = real_part * real_part + imag_part * imag_part
    turns = potential * turn + density * (turn * coupling)
    rest = turns - jnp.round(turns)
    square = rest * rest
    sine = rest * (
        4.4428679 + square * (-7.30744342 + square * (3.59478806 + square * -0.78437396))
    )
    cosine = 1.4142135 + square * (
        -6.97885099 + square * (5.73946123 + square * (-1.88356328 + square * 0.31069871))
    )
    whole_cos = 1.0 - sine * sine
    whole_sin = sine * cosine
    return (
        real_part * whole_cos - imag_part * whole_sin,
        real_part * whole_sin + imag_part * whole_cos,
    )


def cmul(a, b):
    return a[0] * b[0] - a[1] * b[1], a[0] * b[1] + a[1] * b[0]


def cadd(a, b):
    return a[0] + b[0], a[1] + b[1]


def csub(a, b):
    return a[0] - b[0], a[1] - b[1]


def split_modes(real_part, imag_part):
    quarter = [
        (real_part[:, QX * p : QX * (p + 1)], imag_part[:, QX * p : QX * (p + 1)])
        for p in range(4)
    ]
    t0, t1 = cadd(quarter[0], quarter[2]), csub(quarter[0], quarter[2])
    t2, t3 = cadd(quarter[1], quarter[3]), csub(quarter[1], quarter[3])
    return [
        cadd(t0, t2),
        (t1[0] + t3[1], t1[1] - t3[0]),
        csub(t0, t2),
        (t1[0] - t3[1], t1[1] + t3[0]),
    ]


def join_modes(back):
    t0, t1 = cadd(back[0], back[2]), csub(back[0], back[2])
    t2, t3 = cadd(back[1], back[3]), csub(back[1], back[3])
    return [
        cadd(t0, t2),
        (t1[0] - t3[1], t1[1] + t3[0]),
        csub(t0, t2),
        (t1[0] + t3[1], t1[1] - t3[0]),
    ]


def x_sweep(count, load, factors, store, left, cells, forward_ref, inverse_ref):
    rows = 16 * count
    for n in range(count):
        mixed = split_modes(*load(n))
        for residue in range(4):
            left[residue, 16 * n : 16 * n + 16, :] = jnp.concatenate(
                mixed[residue], axis=1
            ).astype(bf16)
    for residue in range(4):
        modes = jnp.dot(left[residue, 0:rows, :], forward_ref[residue], preferred_element_type=f32)
        for n in range(count):
            some = modes[16 * n : 16 * n + 16]
            scaled = cmul((some[:, :QX], some[:, QX:]), factors(n)[residue])
            left[residue, 16 * n : 16 * n + 16, :] = jnp.concatenate(scaled, axis=1).astype(bf16)
    for residue in range(4):
        cells[residue, 0:rows, :] = jnp.dot(
            left[residue, 0:rows, :], inverse_ref[residue], preferred_element_type=f32
        )
    for n in range(0, count, 2):
        done = []
        for at in range(2):
            lines = slice(16 * (n + at), 16 * (n + at) + 16)
            some = [cells[residue, lines, :] for residue in range(4)]
            out = join_modes([(one[:, :QX], one[:, QX:]) for one in some])
            done.append([jnp.concatenate([one[part] for one in out], axis=1) for part in range(2)])
        store(n, done)


def main_kernel(
    count_py,
    count_pz,
    z_step,
    z_profile,
    wave_hbm,
    pot_hbm,
    xf_hbm,
    xi_hbm,
    weight_hbm,
    factor_hbm,
    trig_ref,
    z_ref,
    yf_ref,
    yi_ref,
    add_ref,
    turn_ref,
    ytab_ref,
    step_ref,
    packed_ref,
    field_hbm,
    change_hbm,
    wave,
    pot,
    xf,
    xi,
    weight,
    factor,
    fresh_a,
    fresh_b,
    gains,
    grid,
    swept,
    solved,
    planes,
    result,
    left_buf,
    cells_buf,
    sums,
    z_states,
    z_partner,
    z_send,
    z_recv,
    z_back,
    z_chip,
    z_give,
    z_carry,
    y_send,
    y_recv,
    y_back,
    y_carry,
    c_send,
    c_recv,
    change,
    in_sem,
    tab_sem,
    out_sem,
    pair_sems,
    z_sems,
    z_back_sems,
    y_sems,
    c_sems,
):
    me_y = lax.axis_index("py")
    me_z = lax.axis_index("pz")
    core = lax.rem(me_z, 2)
    chip = me_z // 2
    partner = me_z + 1 - 2 * core
    chips = count_pz // 2
    half_z = TILES_Z // 2
    tiles_z = half_z // chips
    mine = core * half_z
    theirs = half_z - mine

    def load(group):
        rows = pl.ds(pl.multiple_of(group * 8, 8), 8)
        return (
            pltpu.make_async_copy(wave_hbm.at[:, :, rows, :], wave.at[group], in_sem.at[0, group]),
            pltpu.make_async_copy(pot_hbm.at[:, rows, :], pot.at[group], in_sem.at[1, group]),
        )

    for group in range(GROUPS):
        for copy in load(group):
            copy.start()
    table_copies = (
        pltpu.make_async_copy(xf_hbm, xf, tab_sem.at[0]),
        pltpu.make_async_copy(xi_hbm, xi, tab_sem.at[1]),
        pltpu.make_async_copy(weight_hbm, weight, tab_sem.at[2]),
        pltpu.make_async_copy(factor_hbm, factor, tab_sem.at[3]),
    )
    for copy in table_copies:
        copy.start()

    barrier = pltpu.get_barrier_semaphore()

    def twin(other):
        return {"pz": other * 2 + core}

    pl.semaphore_signal(barrier, inc=1, device_id={"pz": partner}, device_id_type=MESH)

    @pl.loop(1, chips)
    def _(step):
        pl.semaphore_signal(
            barrier, inc=1, device_id=twin(lax.rem(chip + step, chips)), device_id_type=MESH
        )

    @pl.loop(1, count_py)
    def _(step):
        pl.semaphore_signal(
            barrier, inc=1, device_id={"py": lax.rem(me_y + step, count_py)}, device_id_type=MESH
        )

    def kick_group(group, fresh):
        for some in range(BZ // 2):
            rows = slice(2 * some, 2 * some + 2)
            new = kick(wave[group, 0, rows], wave[group, 1, rows], pot[group, rows])
            for part in range(2):
                start = ROWS // 2 * part + 16 * some
                fresh[start : start + 16, :] = new[part].reshape(16, NX).astype(bf16)

    def solve_group(group, fresh):
        for side in range(2):
            lanes = slice(side * NX // 2, (side + 1) * NX // 2)
            rows = jnp.dot(z_ref[...], fresh[:, lanes], preferred_element_type=f32)
            for start in range(0, ROWS, 16):
                grid[group, start : start + 16, lanes] = rows[start : start + 16].astype(bf16)
            states = rows[ROWS:].astype(bf16)
            for quarter in range(2):
                z_states[group * 4 + 2 * side + quarter] = states[
                    :, QX * quarter : QX * (quarter + 1)
                ].reshape(2, 16, QX)

    def pair_out(step):
        return pltpu.make_async_remote_copy(
            src_ref=z_states.at[pl.ds(theirs + 4 * step, 4)],
            dst_ref=z_partner.at[pl.ds(4 * step, 4)],
            send_sem=pair_sems.at[0, step],
            recv_sem=pair_sems.at[1, step],
            device_id={"pz": partner},
            device_id_type=MESH,
        )

    def pair_back():
        return pltpu.make_async_remote_copy(
            src_ref=z_give,
            dst_ref=z_carry.at[pl.ds(mine, half_z)],
            send_sem=pair_sems.at[0, 4],
            recv_sem=pair_sems.at[1, 4],
            device_id={"pz": partner},
            device_id_type=MESH,
        )

    def pair_returned():
        return pltpu.make_async_remote_copy(
            src_ref=z_give,
            dst_ref=z_carry.at[pl.ds(theirs, half_z)],
            send_sem=pair_sems.at[0, 4],
            recv_sem=pair_sems.at[1, 4],
            device_id={"pz": partner},
            device_id_type=MESH,
        )

    def z_out(tile):
        return pltpu.make_async_remote_copy(
            src_ref=z_send.at[tile],
            dst_ref=z_recv.at[chip, lax.rem(tile, tiles_z)],
            send_sem=z_sems.at[0, tile],
            recv_sem=z_sems.at[1, chip * tiles_z + lax.rem(tile, tiles_z)],
            device_id=twin(tile // tiles_z),
            device_id_type=MESH,
        )

    def z_in(step, tile):
        peer = lax.rem(chip + step, chips)
        return pltpu.make_async_remote_copy(
            src_ref=z_send.at[tile],
            dst_ref=z_recv.at[peer, tile],
            send_sem=z_sems.at[0, tile],
            recv_sem=z_sems.at[1, peer * tiles_z + tile],
            device_id=twin(peer),
            device_id_type=MESH,
        )

    def z_return(step):
        peer = lax.rem(chip + step, chips)
        return pltpu.make_async_remote_copy(
            src_ref=z_back.at[peer],
            dst_ref=z_chip.at[pl.ds(chip * tiles_z, tiles_z)],
            send_sem=z_back_sems.at[0, peer],
            recv_sem=z_back_sems.at[1, chip],
            device_id=twin(peer),
            device_id_type=MESH,
        )

    def z_returned(step):
        peer = lax.rem(chip + step, chips)
        return pltpu.make_async_remote_copy(
            src_ref=z_back.at[chip],
            dst_ref=z_chip.at[pl.ds(peer * tiles_z, tiles_z)],
            send_sem=z_back_sems.at[0, chip],
            recv_sem=z_back_sems.at[1, peer],
            device_id=twin(peer),
            device_id_type=MESH,
        )

    lead = core == 0
    block_step = (z_step.real, z_step.imag)
    chip_step = z_step * z_step

    def parts(array):
        array = array.astype(f32)
        return array[0:8], array[8:16]

    def choose(first, second):
        return jnp.where(lead, first[0], second[0]), jnp.where(lead, first[1], second[1])

    def joined(value):
        return jnp.concatenate(value, axis=0).astype(bf16)

    def order(count):
        if count < GROUPS // 2:
            return theirs // 4 + count
        return mine // 4 + lax.rem(count + chip // 4, GROUPS // 2)

    def merge(step):
        pair_out(step).wait_recv()
        for at in range(4):
            tile = step * 4 + at
            own = [parts(z_states[mine + tile, side]) for side in range(2)]
            other = [parts(z_partner[tile, side]) for side in range(2)]
            left = cadd(choose(other[0], own[0]), cmul(choose(own[0], other[0]), block_step))
            right = cadd(choose(own[1], other[1]), cmul(choose(other[1], own[1]), block_step))
            z_send[tile, 0] = joined(left)
            z_send[tile, 1] = joined(right)
            owner = tile // tiles_z

            @pl.when(owner != chip)
            def _():
                z_out(tile).start()

            @pl.when(owner == chip)
            def _():
                z_recv[chip, lax.rem(tile, tiles_z)] = z_send[tile]

    def kicked(count, fresh):
        for copy in load(order(count)):
            copy.wait()
        kick_group(order(count), fresh)

    fresh = (fresh_a, fresh_b)
    kicked(0, fresh[0])
    for count in range(GROUPS):
        if count + 1 < GROUPS:
            for copy in load(order(count + 1)):
                copy.wait()
        solve_group(order(count), fresh[count % 2])
        if count + 1 < GROUPS:
            kick_group(order(count + 1), fresh[(count + 1) % 2])
        if count == 0:
            pl.semaphore_wait(barrier, chips + count_py - 1)
        if count < GROUPS // 2:
            pair_out(count).start()
        else:
            merge(order(count) - mine // 4)

    for copy in table_copies:
        copy.wait()

    for group in range(GROUPS):
        cell = lax.broadcasted_iota(jnp.int32, (8, QX), 0) + (
            me_y * BY + group * 8 - count_py * BY // 2
        )
        beta = cell.astype(f32) * (0.5 * time_step * rotation)
        for residue in range(4):
            rate = trig_ref[2 * residue : 2 * residue + 1] + beta * trig_ref[
                2 * residue + 1 : 2 * residue + 2
            ]
            scale = 1.0 / (1.0 + rate * rate)
            lines = slice(8 * group, 8 * group + 8)
            gains[2 * residue, lines, :] = (1.0 - rate * rate) * scale
            gains[2 * residue + 1, lines, :] = -2.0 * rate * scale

    def sweep_half(half):
        first = half * BY // 2

        def fetch(n):
            group, row = (first + n) // 8, (first + n) % 8 * BZ
            return tuple(
                grid[group, start : start + BZ, :].astype(f32)
                for start in (row, row + ROWS // 2)
            )

        def gain(n):
            line = slice(first + n, first + n + 1)
            return [
                (gains[2 * residue, line, :], gains[2 * residue + 1, line, :])
                for residue in range(4)
            ]

        def put(n, done):
            for at in range(2):
                start = (first + n + at) * BZ
                for part in range(2):
                    swept[part, start : start + BZ, :] = done[at][part].astype(bf16)

        x_sweep(BY // 2, fetch, gain, put, left_buf, cells_buf, xf, xi)

    steps_y = [(step_ref[2 * n : 2 * n + 1], step_ref[2 * n + 1 : 2 * n + 2]) for n in range(4)]
    forward_step, backward_step, turn_step, whole_gain = steps_y

    def y_rows(cell):
        return pl.ds(pl.multiple_of(cell * BZ, BZ), BZ)

    def save(rows, value):
        for part in range(2):
            for quarter in range(4):
                solved[part, quarter, rows, :] = value[part][
                    :, QX * quarter : QX * (quarter + 1)
                ]

    def y_forward():
        def advance(cell, totals):
            total, other = totals
            rows = y_rows(cell)
            value = tuple(swept[part, rows, :].astype(f32) for part in range(2))
            total = cadd(value, cmul(total, forward_step))
            save(rows, total)
            share = tuple(weight[2 + part, pl.ds(cell, 1), :] for part in range(2))
            return total, cadd(other, cmul(value, share))

        zero = jnp.zeros((BZ, NX), f32)
        return lax.fori_loop(0, BY, advance, ((zero, zero), (zero, zero)), unroll=4)

    def y_backward(state):
        def advance(count, total):
            rows = y_rows(BY - 1 - count)
            value = tuple(
                jnp.concatenate([solved[part, quarter, rows, :] for quarter in range(4)], axis=1)
                for part in range(2)
            )
            total = cadd(value, cmul(total, backward_step))
            out = cmul(total, whole_gain)
            save(rows, [out[part] - swept[part, rows, :].astype(f32) for part in range(2)])
            return total

        lax.fori_loop(0, BY, advance, cmul(state, turn_step), unroll=4)

    def y_states(count):
        @pl.loop(0, count)
        def _(at):
            for quarter in range(4):
                lanes = slice(QX * quarter, QX * (quarter + 1))
                total = [[0.0, 0.0], [0.0, 0.0]]
                for start in range(0, BY, 16):
                    rows = slice(start, start + 16)
                    value = [planes[part, at, rows, lanes].astype(f32) for part in range(2)]
                    for side in range(2):
                        some = cmul(
                            value, (weight[2 * side, rows, lanes], weight[2 * side + 1, rows, lanes])
                        )
                        for part in range(2):
                            total[side][part] += some[part][0:8] + some[part][8:16]
                for side in range(2):
                    for part in range(2):
                        row = pl.multiple_of((side * 2 + part) * 16 + at * 8, 8)
                        sums[pl.ds(row, 8), lanes] = total[side][part]

        rows = 0.0
        for quarter in range(4):
            some = sums[:, QX * quarter : QX * (quarter + 1)].astype(bf16)
            rows += jnp.dot(add_ref[quarter], some, preferred_element_type=f32)
        return rows.astype(bf16)

    def y_periodic(plane):
        for side in range(2):
            lanes = slice(side * NX // 2, (side + 1) * NX // 2)
            block = jnp.concatenate([planes[part, plane, :, lanes] for part in range(2)], axis=0)
            modes = jnp.dot(yf_ref[...], block, preferred_element_type=f32)
            scaled = [
                cmul(
                    (modes[some : some + 32], modes[BY + some : BY + some + 32]),
                    (factor[0, some : some + 32, lanes], factor[1, some : some + 32, lanes]),
                )
                for some in range(0, BY, 32)
            ]
            block = jnp.concatenate(
                [one[part].astype(bf16) for part in range(2) for one in scaled], axis=0
            )
            cells = jnp.dot(yi_ref[...], block, preferred_element_type=f32).astype(bf16)
            for part in range(2):
                planes[part, plane, :, lanes] = cells[part * BY : (part + 1) * BY]

    class Exchange:
        def __init__(self, send, recv, back, carry, sems, tiles):
            self.send, self.recv, self.back, self.carry = send, recv, back, carry
            self.sems, self.tiles = sems, tiles

        def mine(self):
            return pl.ds(me_y * self.tiles, self.tiles)

        def out(self, peer):
            return pltpu.make_async_remote_copy(
                src_ref=self.send.at[pl.ds(peer * self.tiles, self.tiles)],
                dst_ref=self.recv.at[me_y],
                send_sem=self.sems.at[0, peer],
                recv_sem=self.sems.at[1, me_y],
                device_id={"py": peer},
                device_id_type=MESH,
            )

        def arrived(self, peer):
            return pltpu.make_async_remote_copy(
                src_ref=self.send.at[self.mine()],
                dst_ref=self.recv.at[peer],
                send_sem=self.sems.at[0, me_y],
                recv_sem=self.sems.at[1, peer],
                device_id={"py": peer},
                device_id_type=MESH,
            )

        def give(self, peer):
            return pltpu.make_async_remote_copy(
                src_ref=self.back.at[peer],
                dst_ref=self.carry.at[self.mine()],
                send_sem=self.sems.at[2, peer],
                recv_sem=self.sems.at[3, me_y],
                device_id={"py": peer},
                device_id_type=MESH,
            )

        def given(self, peer):
            return pltpu.make_async_remote_copy(
                src_ref=self.back.at[me_y],
                dst_ref=self.carry.at[pl.ds(peer * self.tiles, self.tiles)],
                send_sem=self.sems.at[2, me_y],
                recv_sem=self.sems.at[3, peer],
                device_id={"py": peer},
                device_id_type=MESH,
            )

        def post(self):
            @pl.loop(1, count_py)
            def _(step):
                self.out(lax.rem(me_y + step, count_py)).start()

        def answer(self):
            self.recv[me_y] = self.send[self.mine()]

            @pl.loop(1, count_py)
            def _(step):
                self.arrived(lax.rem(me_y + step, count_py)).wait_recv()

            for tile in range(self.tiles):
                solve_tile(self.recv, self.back, tile, lax.rem(me_y * self.tiles + tile, 4))

            @pl.loop(1, count_py)
            def _(step):
                self.give(lax.rem(me_y + step, count_py)).start()

            self.carry[self.mine()] = self.back[me_y]

        def receive(self):
            @pl.loop(1, count_py)
            def _(step):
                self.given(lax.rem(me_y + step, count_py)).wait_recv()

        def close(self):
            @pl.loop(1, count_py)
            def _(step):
                peer = lax.rem(me_y + step, count_py)
                self.out(peer).wait_send()
                self.give(peer).wait_send()

        def rows(self, tiles):
            return [self.carry[tile].reshape(CARRY, QX) for tile in tiles]

    def solve_tile(recv, back, tile, quarter):
        table = ytab_ref[quarter]
        value = [(table[2 * n : 2 * n + 1], table[2 * n + 1 : 2 * n + 2]) for n in range(8)]
        whole1, whole2, _, _, wrap1, wrap2, out1, out2 = value
        left_state = [parts(recv[block, tile, 0]) for block in range(count_py)]
        right_state = [parts(recv[block, tile, 1]) for block in range(count_py)]
        left, right = left_state[0], right_state[count_py - 1]
        for block in range(1, count_py):
            left = cadd(left_state[block], cmul(left, whole1))
            right = cadd(right_state[count_py - 1 - block], cmul(right, whole2))
        left, right = cmul(left, wrap1), cmul(right, wrap2)
        for block in range(count_py):
            other = count_py - 1 - block
            back[block, tile, 0] = joined(cmul(left, out1))
            back[other, tile, 1] = joined(cmul(right, out2))
            left = cadd(left_state[block], cmul(left, whole1))
            right = cadd(right_state[other], cmul(right, whole2))

    planes_y = Exchange(y_send, y_recv, y_back, y_carry, y_sems, TILES_Y // count_py)
    def carry_out(step):
        return pltpu.make_async_remote_copy(
            src_ref=c_send,
            dst_ref=c_recv.at[me_y],
            send_sem=c_sems.at[0, lax.rem(me_y + step, count_py)],
            recv_sem=c_sems.at[1, me_y],
            device_id={"py": lax.rem(me_y + step, count_py)},
            device_id_type=MESH,
        )

    def carry_in(step):
        peer = lax.rem(me_y + step, count_py)
        return pltpu.make_async_remote_copy(
            src_ref=c_send,
            dst_ref=c_recv.at[peer],
            send_sem=c_sems.at[0, me_y],
            recv_sem=c_sems.at[1, peer],
            device_id={"py": peer},
            device_id_type=MESH,
        )

    def carry_solve():
        value = [(packed_ref[2 * n], packed_ref[2 * n + 1]) for n in range(8)]
        whole1, whole2, own1, own2, wrap1, wrap2, out1, out2 = value
        own = [parts(c_send[side]) for side in range(2)]
        left, right = own
        for step in range(1, count_py):
            left = cadd(parts(c_recv[lax.rem(me_y + step, count_py), 0]), cmul(left, whole1))
            back = lax.rem(me_y + count_py - step, count_py)
            right = cadd(parts(c_recv[back, 1]), cmul(right, whole2))
        left = csub(cmul(left, wrap1), cmul(own[0], own1))
        right = csub(cmul(right, wrap2), cmul(own[1], own2))
        return jnp.concatenate([joined(cmul(left, out1)), joined(cmul(right, out2))], axis=0)

    def post_planes(states):
        for half in range(2):
            lines = slice(8 * half, 8 * half + 8)
            for quarter in range(4):
                lanes = slice(QX * quarter, QX * (quarter + 1))
                for side in range(2):
                    y_send[half * 4 + quarter, side] = joined(
                        [states[side][part][lines, lanes] for part in range(2)]
                    )
        planes_y.post()

    sweep_half(0)
    sweep_half(1)

    @pl.loop(1, chips)
    def _(step):
        for tile in range(tiles_z):
            z_in(step, tile).wait_recv()

    for tile in range(tiles_z):

        def state(block, side):
            return parts(z_recv[block, tile, side])

        def advance(total, value):
            return cadd(cmul(total, (chip_step.real, chip_step.imag)), value)

        def gather(step, carry):
            left, right = carry
            return (
                advance(left, state(step, 0)),
                advance(right, state(chips - 1 - step, 1)),
            )

        zero = (jnp.zeros((8, QX), f32), jnp.zeros((8, QX), f32))
        left, right = lax.fori_loop(0, chips, gather, (zero, zero), unroll=2)
        wrap = 1 / (1 - chip_step**chips)
        left = cmul(left, (wrap.real, wrap.imag))
        right = cmul(right, (wrap.real, wrap.imag))

        def hand_out(step, carry):
            left, right = carry
            last = chips - 1 - step
            z_back[step, tile, 0] = joined(left)
            z_back[last, tile, 1] = joined(right)
            return advance(left, state(step, 0)), advance(right, state(last, 1))

        lax.fori_loop(0, chips, hand_out, (left, right), unroll=2)

    @pl.loop(1, chips)
    def _(step):
        z_return(step).start()

    z_chip[pl.ds(chip * tiles_z, tiles_z)] = z_back[chip]

    forward_state, backward_state = y_forward()
    post_planes((forward_state, backward_state))
    y_backward(forward_state)

    @pl.loop(1, chips)
    def _(step):
        z_returned(step).wait_recv()

    @pl.loop(0, half_z)
    def _(tile):
        own = [parts(z_states[mine + tile, side]) for side in range(2)]
        other = [parts(z_partner[tile, side]) for side in range(2)]
        whole = [parts(z_chip[tile, side]) for side in range(2)]
        inner_left = cadd(choose(own[0], other[0]), cmul(whole[0], block_step))
        inner_right = cadd(choose(other[1], own[1]), cmul(whole[1], block_step))
        z_give[tile, 0] = joined(choose(inner_left, whole[0]))
        z_give[tile, 1] = joined(choose(whole[1], inner_right))
        z_carry[mine + tile, 0] = joined(choose(whole[0], inner_left))
        z_carry[mine + tile, 1] = joined(choose(inner_right, whole[1]))

    pair_back().start()

    pair_returned().wait_recv()

    def fetch(n):
        sides = [
            jnp.concatenate([z_carry[n * 4 + quarter, side] for quarter in range(4)], axis=1)
            for side in range(2)
        ]
        sides = [side.astype(f32) for side in sides]
        return tuple(
            jnp.concatenate([side[8 * part : 8 * part + 8] for side in sides], axis=0)
            for part in range(2)
        )

    def put(n, done):
        for side in range(2):
            lines = slice(8 * side, 8 * side + 8)
            for part in range(2):
                planes[part, side, 8 * n : 8 * n + 16, :] = jnp.concatenate(
                    [done[at][part][lines] for at in range(2)], axis=0
                ).astype(bf16)

    def gain(n):
        lines = slice(8 * n, 8 * n + 8)
        return [
            tuple(
                jnp.concatenate([gains[2 * residue + part, lines, :]] * 2, axis=0)
                for part in range(2)
            )
            for residue in range(4)
        ]

    x_sweep(GROUPS, fetch, gain, put, left_buf, cells_buf, xf, xi)
    c_send[...] = y_states(2).reshape(2, 16, QX)

    @pl.loop(1, count_py)
    def _(step):
        carry_out(step).start()

    planes_y.answer()
    y_periodic(0)
    y_periodic(1)

    def store(pair):
        rows = pl.ds(pl.multiple_of(pair * 16, 16), 16)
        return pltpu.make_async_copy(
            result.at[:, :, rows, :], field_hbm.at[:, :, rows, :], out_sem.at[pair]
        )

    @pl.loop(0, BY // 16)
    def _(pair):
        rows = pl.ds(pl.multiple_of(pair * 16, 16), 16)
        for quarter in range(4):
            lanes = slice(QX * quarter, QX * (quarter + 1))
            left, right = [
                tuple(planes[part, one, rows, lanes].astype(f32) for part in range(2))
                for one in range(2)
            ]
            for plane in range(BZ):
                first, second = (complex(one) for one in z_profile[plane])
                lines = pl.ds(pair * 16 * BZ + plane, 16, stride=BZ)
                value = tuple(solved[part, quarter, lines, :] for part in range(2))
                value = cadd(value, cmul(left, (first.real, first.imag)))
                value = cadd(value, cmul(right, (second.real, second.imag)))
                for part in range(2):
                    result[part, plane, rows, lanes] = value[part].astype(bf16)
        store(pair).start()

    @pl.loop(1, count_py)
    def _(step):
        carry_in(step).wait_recv()

    carried = carry_solve()
    planes_y.receive()
    for quarter in range(4):
        rows = planes_y.rows((quarter, 4 + quarter)) + [carried]
        change[:, :, QX * quarter : QX * (quarter + 1)] = jnp.dot(
            turn_ref[quarter], jnp.concatenate(rows, axis=0), preferred_element_type=f32
        ).reshape(BZ, 8, QX)
    last = pltpu.make_async_copy(change, change_hbm, out_sem.at[GROUPS // 2])
    last.start()

    @pl.loop(0, half_z)
    def _(tile):
        @pl.when(tile // tiles_z != chip)
        def _():
            z_out(tile).wait_send()

    @pl.loop(1, chips)
    def _(step):
        z_return(step).wait_send()

    @pl.loop(0, GROUPS // 2)
    def _(step):
        pair_out(step).wait_send()

    pair_back().wait_send()

    planes_y.close()

    @pl.loop(1, count_py)
    def _(step):
        carry_out(step).wait_send()


    @pl.loop(0, GROUPS // 2)
    def _(pair):
        store(pair).wait()

    last.wait()


PLANES = 2


def finish_kernel(
    field_hbm,
    change_hbm,
    pot_hbm,
    table_hbm,
    out_hbm,
    field,
    change,
    pot,
    table,
    out,
    in_sem,
    tab_sem,
    out_sem,
):
    steps = BZ // PLANES

    def load(step):
        planes = pl.ds(step * PLANES, PLANES)
        return (
            pltpu.make_async_copy(field_hbm.at[:, planes], field.at[:, planes], in_sem.at[0, step]),
            pltpu.make_async_copy(pot_hbm.at[planes], pot.at[planes], in_sem.at[1, step]),
        )

    def save(step):
        planes = pl.ds(step * PLANES, PLANES)
        return pltpu.make_async_copy(out.at[:, planes], out_hbm.at[:, planes], out_sem.at[step])

    tables = (
        pltpu.make_async_copy(change_hbm, change, tab_sem.at[0]),
        pltpu.make_async_copy(table_hbm, table, tab_sem.at[1]),
    )
    for copy in tables:
        copy.start()
    for step in range(steps):
        for copy in load(step):
            copy.start()
    for copy in tables:
        copy.wait()

    def finish(at, lanes):
        ends = [change[at, row : row + 1, lanes] for row in range(4)]
        for start in range(0, BY, 16):
            rows = slice(start, start + 16)
            value = tuple(field[part, at, rows, lanes].astype(f32) for part in range(2))
            for side in range(2):
                profile = (table[2 * side, rows, lanes], table[2 * side + 1, rows, lanes])
                value = cadd(value, cmul(profile, (ends[2 * side], ends[2 * side + 1])))
            new = kick(value[0], value[1], pot[at, rows, lanes])
            for part in range(2):
                out[part, at, rows, lanes] = new[part]

    @pl.loop(0, steps)
    def _(step):
        for copy in load(step):
            copy.wait()
        for one in range(PLANES):
            for side in range(2):
                finish(step * PLANES + one, slice(side * NX // 2, (side + 1) * NX // 2))
        save(step).start()

    @pl.loop(0, steps)
    def _(step):
        save(step).wait()


def shards(count_py, count_pz, wavefunction, potential):
    forward_x, inverse_x, trig = x_tables()
    z_rows, turn, z_profile, z_step = z_tables()
    forward_y, inverse_y, factor, weight, homogeneous, steps_y, add, y_table, packed = y_tables(count_py)

    def low(array):
        return jnp.asarray(array.astype(np.float32)).astype(bf16)

    def full(array):
        return jnp.asarray(array.astype(np.float32))

    chips = count_pz // 2
    tiles_z = TILES_Z // 2 // chips
    tiles_y = TILES_Y // count_py
    anywhere = pl.BlockSpec(memory_space=pl.ANY)
    inside = pl.BlockSpec(memory_space=pltpu.VMEM)
    field, change = pl.pallas_call(
        functools.partial(main_kernel, count_py, count_pz, z_step, z_profile),
        out_shape=(
            jax.ShapeDtypeStruct((2, BZ, BY, NX), bf16),
            jax.ShapeDtypeStruct((BZ, 8, NX), f32),
        ),
        in_specs=[anywhere] * 6 + [inside] * 9,
        out_specs=(anywhere, anywhere),
        scratch_shapes=[
            pltpu.VMEM((GROUPS, 2, BZ, 8, NX), f32),
            pltpu.VMEM((GROUPS, BZ, 8, NX), f32),
            pltpu.VMEM((4, 2 * QX, 2 * QX), bf16),
            pltpu.VMEM((4, 2 * QX, 2 * QX), bf16),
            pltpu.VMEM(weight.shape, f32),
            pltpu.VMEM(factor.shape, f32),
            pltpu.VMEM((ROWS, NX), bf16),
            pltpu.VMEM((ROWS, NX), bf16),
            pltpu.VMEM((8, BY, QX), f32),
            pltpu.VMEM((GROUPS, ROWS, NX), bf16),
            pltpu.VMEM((2, BY * BZ, NX), bf16),
            pltpu.VMEM((2, 4, BY * BZ, QX), f32),
            pltpu.VMEM((2, 2, BY, NX), bf16),
            pltpu.VMEM((2, BZ, BY, NX), bf16),
            pltpu.VMEM((4, GROUPS * BZ * 4, 2 * QX), bf16),
            pltpu.VMEM((4, GROUPS * BZ * 4, 2 * QX), f32),
            pltpu.VMEM((64, NX), f32),
            pltpu.VMEM((TILES_Z, 2, 16, QX), bf16),
            pltpu.VMEM((TILES_Z // 2, 2, 16, QX), bf16),
            pltpu.VMEM((TILES_Z // 2, 2, 16, QX), bf16),
            pltpu.VMEM((chips, tiles_z, 2, 16, QX), bf16),
            pltpu.VMEM((chips, tiles_z, 2, 16, QX), bf16),
            pltpu.VMEM((TILES_Z // 2, 2, 16, QX), bf16),
            pltpu.VMEM((TILES_Z // 2, 2, 16, QX), bf16),
            pltpu.VMEM((TILES_Z, 2, 16, QX), bf16),
            pltpu.VMEM((TILES_Y, 2, 16, QX), bf16),
            pltpu.VMEM((count_py, tiles_y, 2, 16, QX), bf16),
            pltpu.VMEM((count_py, tiles_y, 2, 16, QX), bf16),
            pltpu.VMEM((TILES_Y, 2, 16, QX), bf16),
            pltpu.VMEM((2, 16, QX), bf16),
            pltpu.VMEM((count_py, 2, 16, QX), bf16),
            pltpu.VMEM((BZ, 8, NX), f32),
            pltpu.SemaphoreType.DMA((2, GROUPS)),
            pltpu.SemaphoreType.DMA((4,)),
            pltpu.SemaphoreType.DMA((GROUPS // 2 + 1,)),
            pltpu.SemaphoreType.DMA((2, 5)),
            pltpu.SemaphoreType.DMA((2, TILES_Z // 2)),
            pltpu.SemaphoreType.DMA((2, chips)),
            pltpu.SemaphoreType.DMA((4, count_py)),
            pltpu.SemaphoreType.DMA((2, count_py)),
        ],
        compiler_params=pltpu.CompilerParams(
            collective_id=0, has_side_effects=True, vmem_limit_bytes=56 * 2**20
        ),
        cost_estimate=pl.CostEstimate(
            flops=3_000_000_000, bytes_accessed=10_000_000, transcendentals=0
        ),
        name="sweeps",
    )(
        wavefunction,
        potential,
        low(forward_x),
        low(inverse_x),
        full(weight),
        full(factor),
        full(trig),
        low(z_rows),
        low(forward_y),
        low(inverse_y),
        low(add),
        low(turn),
        full(y_table),
        full(steps_y),
        full(packed),
    )
    return pl.pallas_call(
        finish_kernel,
        out_shape=jax.ShapeDtypeStruct((2, BZ, BY, NX), f32),
        in_specs=[anywhere] * 4,
        out_specs=anywhere,
        scratch_shapes=[
            pltpu.VMEM((2, BZ, BY, NX), bf16),
            pltpu.VMEM((BZ, 8, NX), f32),
            pltpu.VMEM((BZ, BY, NX), f32),
            pltpu.VMEM(homogeneous.shape, f32),
            pltpu.VMEM((2, BZ, BY, NX), f32),
            pltpu.SemaphoreType.DMA((2, BZ // PLANES)),
            pltpu.SemaphoreType.DMA((2,)),
            pltpu.SemaphoreType.DMA((BZ // PLANES,)),
        ],
        compiler_params=pltpu.CompilerParams(vmem_limit_bytes=60 * 2**20),
        cost_estimate=pl.CostEstimate(
            flops=800_000_000, bytes_accessed=9_000_000, transcendentals=0
        ),
        name="finish",
    )(field, change, potential, full(homogeneous))


def solution(mesh):
    return jax.shard_map(
        functools.partial(shards, mesh.shape["py"], mesh.shape["pz"]),
        mesh=mesh,
        in_specs=(P(None, "pz", "py", None), P("pz", "py", None)),
        out_specs=P(None, "pz", "py", None),
        check_vma=False,
    )
```

```python
import functools

import jax
import jax.numpy as jnp
import numpy as np
from jax import lax
from jax.experimental import pallas as pl
from jax.experimental.pallas import tpu as pltpu
from jax.sharding import PartitionSpec as P

time_step = 0.005
rotation = 0.9
coupling = 100.0
grid_spacing = 0.05

NX = 512
BY = 64
BZ = 16
QX = 128
GROUPS = BY // 8
TILES_Z = GROUPS * 4
TILES_Y = 8
ROWS = 2 * BZ * 8
CARRY = 32

MESH = pl.DeviceIdType.MESH
f32 = jnp.float32
bf16 = jnp.bfloat16


def line_roots(beta):
    beta = np.asarray(beta, np.float64)
    half = (beta - 1j) / 2
    spread = np.sqrt((1 + 1j) ** 2 - (beta - 1j) * (-beta - 1j))
    first = (-(1 + 1j) + spread) / (beta - 1j)
    second = (-(1 + 1j) - spread) / (beta - 1j)
    swap = np.abs(first) > np.abs(second)
    inner = np.where(swap, second, first)
    outer = np.where(swap, first, second)
    return inner, 1 / outer, half * (inner - outer)


def real_form(matrix):
    return np.stack(
        [
            np.stack([matrix.real, -matrix.imag], 1),
            np.stack([matrix.imag, matrix.real], 1),
        ],
        0,
    )


def x_tables():
    forward, inverse = [], []
    cells = np.arange(QX)
    for residue in range(4):
        modes = 4 * np.arange(QX) + residue
        angles = 2 * np.pi * ((cells[:, None] * modes[None, :]) % NX) / NX
        cosines, sines = np.cos(angles), np.sin(angles)
        forward.append(np.block([[cosines, -sines], [sines, cosines]]))
        inverse.append(np.block([[cosines.T, sines.T], [-sines.T, cosines.T]]) / NX)
    modes = 4 * np.arange(QX)[None, :] + np.arange(4)[:, None]
    theta = 2 * np.pi * modes / NX
    trig = np.stack([1 - np.cos(theta), np.sin(theta)], 1).reshape(8, QX)
    return np.stack(forward), np.stack(inverse), trig


def z_tables():
    lam, _, scale = line_roots(0.0)
    lam, scale = complex(lam), complex(scale)
    cells = np.arange(BZ)
    local = (2 / scale) * lam ** np.abs(cells[:, None] - cells[None, :]) - np.eye(BZ)
    carry = (2 / scale) * np.stack([lam ** (cells + 1), lam ** (BZ - cells)], 1)
    states = np.stack([lam ** (BZ - 1 - cells), lam**cells], 0)
    eye = np.eye(8)
    apply_field = np.einsum("azbw,ij->aizbwj", real_form(local), eye).reshape(ROWS, ROWS)
    state_rows = np.einsum("asbz,ij->saibzj", real_form(states), eye).reshape(CARRY, ROWS)
    turn = np.zeros((4, BZ, 8, 3, 4, 8))
    fields, carries = real_form(np.eye(BZ).astype(complex)), real_form(carry)
    for end in range(2):
        for out in range(2):
            for part in range(2):
                row, column = 2 * end + out, 2 * end + part
                for half in range(2):
                    turn[:, :, row, half, column, :] = fields[
                        out, :, part, 8 * half : 8 * half + 8
                    ]
                for quarter in range(4):
                    lines = slice(2 * quarter, 2 * quarter + 2)
                    turn[quarter, :, row, 2, column, lines] = carries[out, :, part, :]
    turn = turn.reshape(4, BZ * 8, 3 * CARRY)
    return np.concatenate([apply_field, state_rows], 0), turn, carry, lam**BZ


def y_tables(blocks):
    cells = np.arange(BY)
    angles = 2 * np.pi * ((cells[:, None] * cells[None, :]) % BY) / BY
    modes = np.exp(-1j * angles)
    forward = real_form(modes).reshape(2 * BY, 2 * BY)
    inverse = real_form(np.conj(modes) / BY).reshape(2 * BY, 2 * BY)
    beta = -0.5 * time_step * rotation * (np.arange(NX) - NX // 2)
    theta = 2 * np.pi * cells / BY
    rate = (1 - np.cos(theta))[:, None] + np.sin(theta)[:, None] * beta[None, :]
    factor = (1 - 1j * rate) / (1 + 1j * rate)
    lam1, lam2, scale = line_roots(beta)
    whole1, whole2 = lam1**BY, lam2**BY
    rows = [
        whole1,
        whole2,
        1 / (1 - whole1),
        1 / (1 - whole2),
        1 / (1 - whole1**blocks),
        1 / (1 - whole2**blocks),
        2 * lam1 / scale,
        2 * lam2 / scale,
    ]
    apart = 1 - lam1 * lam2
    steps = [lam1, lam2, lam1 / apart, 2 * apart / scale]
    table = np.stack([part for row in rows for part in (row.real, row.imag)])
    down, up = np.arange(BY)[:, None], BY - 1 - np.arange(BY)[:, None]
    states = [lam1**up, lam2**down]
    homogeneous = [lam1**down, lam2**up]
    add = np.zeros((4, 4, 8, 4, 2, 8))
    for quarter in range(4):
        for plane in range(2):
            for part in range(4):
                add[quarter, part, 2 * quarter + plane, part, plane, :] = 1
    add = add.reshape(4, CARRY, 64)
    table = table.reshape(len(table), 4, QX)
    packed = np.repeat(table, 2, axis=1)
    table = table.transpose(1, 0, 2)

    def parts(values):
        return np.stack([part for value in values for part in (value.real, value.imag)])

    return (
        forward,
        inverse,
        parts([factor]),
        parts(states),
        parts(homogeneous),
        parts(steps),
        add,
        table,
        packed,
    )


def kick(real_part, imag_part, potential):
    turn = -0.5 * time_step / (2 * np.pi)
    density = real_part * real_part + imag_part * imag_part
    turns = potential * turn + density * (turn * coupling)
    rest = turns - jnp.round(turns)
    square = rest * rest
    sine = rest * (
        4.4428679 + square * (-7.30744342 + square * (3.59478806 + square * -0.78437396))
    )
    cosine = 1.4142135 + square * (
        -6.97885099 + square * (5.73946123 + square * (-1.88356328 + square * 0.31069871))
    )
    whole_cos = 1.0 - sine * sine
    whole_sin = sine * cosine
    return (
        real_part * whole_cos - imag_part * whole_sin,
        real_part * whole_sin + imag_part * whole_cos,
    )


def cmul(a, b):
    return a[0] * b[0] - a[1] * b[1], a[0] * b[1] + a[1] * b[0]


def cadd(a, b):
    return a[0] + b[0], a[1] + b[1]


def csub(a, b):
    return a[0] - b[0], a[1] - b[1]


def split_modes(real_part, imag_part):
    quarter = [
        (real_part[:, QX * p : QX * (p + 1)], imag_part[:, QX * p : QX * (p + 1)])
        for p in range(4)
    ]
    t0, t1 = cadd(quarter[0], quarter[2]), csub(quarter[0], quarter[2])
    t2, t3 = cadd(quarter[1], quarter[3]), csub(quarter[1], quarter[3])
    return [
        cadd(t0, t2),
        (t1[0] + t3[1], t1[1] - t3[0]),
        csub(t0, t2),
        (t1[0] - t3[1], t1[1] + t3[0]),
    ]


def join_modes(back):
    t0, t1 = cadd(back[0], back[2]), csub(back[0], back[2])
    t2, t3 = cadd(back[1], back[3]), csub(back[1], back[3])
    return [
        cadd(t0, t2),
        (t1[0] - t3[1], t1[1] + t3[0]),
        csub(t0, t2),
        (t1[0] + t3[1], t1[1] - t3[0]),
    ]


def x_sweep(count, load, factors, store, left, cells, forward_ref, inverse_ref):
    rows = 16 * count
    for n in range(count):
        mixed = split_modes(*load(n))
        for residue in range(4):
            left[residue, 16 * n : 16 * n + 16, :] = jnp.concatenate(
                mixed[residue], axis=1
            ).astype(bf16)
    for residue in range(4):
        modes = jnp.dot(left[residue, 0:rows, :], forward_ref[residue], preferred_element_type=f32)
        for n in range(count):
            some = modes[16 * n : 16 * n + 16]
            scaled = cmul((some[:, :QX], some[:, QX:]), factors(n)[residue])
            left[residue, 16 * n : 16 * n + 16, :] = jnp.concatenate(scaled, axis=1).astype(bf16)
    for residue in range(4):
        cells[residue, 0:rows, :] = jnp.dot(
            left[residue, 0:rows, :], inverse_ref[residue], preferred_element_type=f32
        )
    for n in range(0, count, 2):
        done = []
        for at in range(2):
            lines = slice(16 * (n + at), 16 * (n + at) + 16)
            some = [cells[residue, lines, :] for residue in range(4)]
            out = join_modes([(one[:, :QX], one[:, QX:]) for one in some])
            done.append([jnp.concatenate([one[part] for one in out], axis=1) for part in range(2)])
        store(n, done)


def main_kernel(
    count_py,
    count_pz,
    z_step,
    z_profile,
    wave_hbm,
    pot_hbm,
    xf_hbm,
    xi_hbm,
    weight_hbm,
    factor_hbm,
    trig_ref,
    z_ref,
    yf_ref,
    yi_ref,
    add_ref,
    turn_ref,
    ytab_ref,
    step_ref,
    packed_ref,
    field_hbm,
    change_hbm,
    wave,
    pot,
    xf,
    xi,
    weight,
    factor,
    fresh_a,
    fresh_b,
    gains,
    grid,
    swept,
    solved,
    planes,
    result,
    left_buf,
    cells_buf,
    sums,
    z_states,
    z_partner,
    z_send,
    z_recv,
    z_back,
    z_chip,
    z_give,
    z_carry,
    y_send,
    y_recv,
    y_back,
    y_carry,
    c_send,
    c_recv,
    change,
    in_sem,
    tab_sem,
    out_sem,
    pair_sems,
    z_sems,
    z_back_sems,
    y_sems,
    c_sems,
):
    me_y = lax.axis_index("py")
    me_z = lax.axis_index("pz")
    core = lax.rem(me_z, 2)
    chip = me_z // 2
    partner = me_z + 1 - 2 * core
    chips = count_pz // 2
    half_z = TILES_Z // 2
    tiles_z = half_z // chips
    mine = core * half_z
    theirs = half_z - mine

    def load(group):
        rows = pl.ds(pl.multiple_of(group * 8, 8), 8)
        return (
            pltpu.make_async_copy(wave_hbm.at[:, :, rows, :], wave.at[group], in_sem.at[0, group]),
            pltpu.make_async_copy(pot_hbm.at[:, rows, :], pot.at[group], in_sem.at[1, group]),
        )

    for group in range(GROUPS):
        for copy in load(group):
            copy.start()
    table_copies = (
        pltpu.make_async_copy(xf_hbm, xf, tab_sem.at[0]),
        pltpu.make_async_copy(xi_hbm, xi, tab_sem.at[1]),
        pltpu.make_async_copy(weight_hbm, weight, tab_sem.at[2]),
        pltpu.make_async_copy(factor_hbm, factor, tab_sem.at[3]),
    )
    for copy in table_copies:
        copy.start()

    barrier = pltpu.get_barrier_semaphore()

    def twin(other):
        return {"pz": other * 2 + core}

    pl.semaphore_signal(barrier, inc=1, device_id={"pz": partner}, device_id_type=MESH)

    @pl.loop(1, chips)
    def _(step):
        pl.semaphore_signal(
            barrier, inc=1, device_id=twin(lax.rem(chip + step, chips)), device_id_type=MESH
        )

    @pl.loop(1, count_py)
    def _(step):
        pl.semaphore_signal(
            barrier, inc=1, device_id={"py": lax.rem(me_y + step, count_py)}, device_id_type=MESH
        )

    def kick_group(group, fresh):
        for some in range(BZ // 2):
            rows = slice(2 * some, 2 * some + 2)
            new = kick(wave[group, 0, rows], wave[group, 1, rows], pot[group, rows])
            for part in range(2):
                start = ROWS // 2 * part + 16 * some
                fresh[start : start + 16, :] = new[part].reshape(16, NX).astype(bf16)

    def solve_group(group, fresh):
        for side in range(2):
            lanes = slice(side * NX // 2, (side + 1) * NX // 2)
            rows = jnp.dot(z_ref[...], fresh[:, lanes], preferred_element_type=f32)
            for start in range(0, ROWS, 16):
                grid[group, start : start + 16, lanes] = rows[start : start + 16].astype(bf16)
            states = rows[ROWS:].astype(bf16)
            for quarter in range(2):
                z_states[group * 4 + 2 * side + quarter] = states[
                    :, QX * quarter : QX * (quarter + 1)
                ].reshape(2, 16, QX)

    def pair_out(step):
        return pltpu.make_async_remote_copy(
            src_ref=z_states.at[pl.ds(theirs + 4 * step, 4)],
            dst_ref=z_partner.at[pl.ds(4 * step, 4)],
            send_sem=pair_sems.at[0, step],
            recv_sem=pair_sems.at[1, step],
            device_id={"pz": partner},
            device_id_type=MESH,
        )

    def pair_back():
        return pltpu.make_async_remote_copy(
            src_ref=z_give,
            dst_ref=z_carry.at[pl.ds(mine, half_z)],
            send_sem=pair_sems.at[0, 4],
            recv_sem=pair_sems.at[1, 4],
            device_id={"pz": partner},
            device_id_type=MESH,
        )

    def pair_returned():
        return pltpu.make_async_remote_copy(
            src_ref=z_give,
            dst_ref=z_carry.at[pl.ds(theirs, half_z)],
            send_sem=pair_sems.at[0, 4],
            recv_sem=pair_sems.at[1, 4],
            device_id={"pz": partner},
            device_id_type=MESH,
        )

    def z_out(tile):
        return pltpu.make_async_remote_copy(
            src_ref=z_send.at[tile],
            dst_ref=z_recv.at[chip, lax.rem(tile, tiles_z)],
            send_sem=z_sems.at[0, tile],
            recv_sem=z_sems.at[1, chip * tiles_z + lax.rem(tile, tiles_z)],
            device_id=twin(tile // tiles_z),
            device_id_type=MESH,
        )

    def z_in(step, tile):
        peer = lax.rem(chip + step, chips)
        return pltpu.make_async_remote_copy(
            src_ref=z_send.at[tile],
            dst_ref=z_recv.at[peer, tile],
            send_sem=z_sems.at[0, tile],
            recv_sem=z_sems.at[1, peer * tiles_z + tile],
            device_id=twin(peer),
            device_id_type=MESH,
        )

    def z_return(step):
        peer = lax.rem(chip + step, chips)
        return pltpu.make_async_remote_copy(
            src_ref=z_back.at[peer],
            dst_ref=z_chip.at[pl.ds(chip * tiles_z, tiles_z)],
            send_sem=z_back_sems.at[0, peer],
            recv_sem=z_back_sems.at[1, chip],
            device_id=twin(peer),
            device_id_type=MESH,
        )

    def z_returned(step):
        peer = lax.rem(chip + step, chips)
        return pltpu.make_async_remote_copy(
            src_ref=z_back.at[chip],
            dst_ref=z_chip.at[pl.ds(peer * tiles_z, tiles_z)],
            send_sem=z_back_sems.at[0, chip],
            recv_sem=z_back_sems.at[1, peer],
            device_id=twin(peer),
            device_id_type=MESH,
        )

    lead = core == 0
    block_step = (z_step.real, z_step.imag)
    chip_step = z_step * z_step

    def parts(array):
        array = array.astype(f32)
        return array[0:8], array[8:16]

    def choose(first, second):
        return jnp.where(lead, first[0], second[0]), jnp.where(lead, first[1], second[1])

    def joined(value):
        return jnp.concatenate(value, axis=0).astype(bf16)

    def order(count):
        if count < GROUPS // 2:
            return theirs // 4 + count
        return mine // 4 + lax.rem(count + chip // 4, GROUPS // 2)

    def merge(step):
        pair_out(step).wait_recv()
        for at in range(4):
            tile = step * 4 + at
            own = [parts(z_states[mine + tile, side]) for side in range(2)]
            other = [parts(z_partner[tile, side]) for side in range(2)]
            left = cadd(choose(other[0], own[0]), cmul(choose(own[0], other[0]), block_step))
            right = cadd(choose(own[1], other[1]), cmul(choose(other[1], own[1]), block_step))
            z_send[tile, 0] = joined(left)
            z_send[tile, 1] = joined(right)
            owner = tile // tiles_z

            @pl.when(owner != chip)
            def _():
                z_out(tile).start()

            @pl.when(owner == chip)
            def _():
                z_recv[chip, lax.rem(tile, tiles_z)] = z_send[tile]

    def kicked(count, fresh):
        for copy in load(order(count)):
            copy.wait()
        kick_group(order(count), fresh)

    fresh = (fresh_a, fresh_b)
    kicked(0, fresh[0])
    for count in range(GROUPS):
        if count + 1 < GROUPS:
            for copy in load(order(count + 1)):
                copy.wait()
        solve_group(order(count), fresh[count % 2])
        if count + 1 < GROUPS:
            kick_group(order(count + 1), fresh[(count + 1) % 2])
        if count == 0:
            pl.semaphore_wait(barrier, chips + count_py - 1)
        if count < GROUPS // 2:
            pair_out(count).start()
        else:
            merge(order(count) - mine // 4)

    for copy in table_copies:
        copy.wait()

    for group in range(GROUPS):
        cell = lax.broadcasted_iota(jnp.int32, (8, QX), 0) + (
            me_y * BY + group * 8 - count_py * BY // 2
        )
        beta = cell.astype(f32) * (0.5 * time_step * rotation)
        for residue in range(4):
            rate = trig_ref[2 * residue : 2 * residue + 1] + beta * trig_ref[
                2 * residue + 1 : 2 * residue + 2
            ]
            scale = 1.0 / (1.0 + rate * rate)
            lines = slice(8 * group, 8 * group + 8)
            gains[2 * residue, lines, :] = (1.0 - rate * rate) * scale
            gains[2 * residue + 1, lines, :] = -2.0 * rate * scale

    def sweep_field():
        def fetch(n):
            group, row = n // 8, n % 8 * BZ
            return tuple(
                grid[group, start : start + BZ, :].astype(f32)
                for start in (row, row + ROWS // 2)
            )

        def gain(n):
            line = slice(n, n + 1)
            return [
                (gains[2 * residue, line, :], gains[2 * residue + 1, line, :])
                for residue in range(4)
            ]

        def put(n, done):
            for at in range(2):
                start = (n + at) * BZ
                for part in range(2):
                    swept[part, start : start + BZ, :] = done[at][part].astype(bf16)

        x_sweep(BY, fetch, gain, put, left_buf, cells_buf, xf, xi)

    steps_y = [(step_ref[2 * n : 2 * n + 1], step_ref[2 * n + 1 : 2 * n + 2]) for n in range(4)]
    forward_step, backward_step, turn_step, whole_gain = steps_y

    def y_rows(cell):
        return pl.ds(pl.multiple_of(cell * BZ, BZ), BZ)

    def save(rows, value):
        for part in range(2):
            for quarter in range(4):
                solved[part, quarter, rows, :] = value[part][
                    :, QX * quarter : QX * (quarter + 1)
                ]

    def y_forward():
        def advance(cell, totals):
            total, other = totals
            rows = y_rows(cell)
            value = tuple(swept[part, rows, :].astype(f32) for part in range(2))
            total = cadd(value, cmul(total, forward_step))
            save(rows, total)
            share = tuple(weight[2 + part, pl.ds(cell, 1), :] for part in range(2))
            return total, cadd(other, cmul(value, share))

        zero = jnp.zeros((BZ, NX), f32)
        return lax.fori_loop(0, BY, advance, ((zero, zero), (zero, zero)), unroll=4)

    def y_backward(first, last, total):
        def advance(count, total):
            rows = y_rows(BY - 1 - count)
            value = tuple(
                jnp.concatenate([solved[part, quarter, rows, :] for quarter in range(4)], axis=1)
                for part in range(2)
            )
            total = cadd(value, cmul(total, backward_step))
            out = cmul(total, whole_gain)
            save(rows, [out[part] - swept[part, rows, :].astype(f32) for part in range(2)])
            return total

        return lax.fori_loop(first, last, advance, total, unroll=4)

    def y_states(count):
        @pl.loop(0, count)
        def _(at):
            for quarter in range(4):
                lanes = slice(QX * quarter, QX * (quarter + 1))
                total = [[0.0, 0.0], [0.0, 0.0]]
                for start in range(0, BY, 16):
                    rows = slice(start, start + 16)
                    value = [planes[part, at, rows, lanes].astype(f32) for part in range(2)]
                    for side in range(2):
                        some = cmul(
                            value, (weight[2 * side, rows, lanes], weight[2 * side + 1, rows, lanes])
                        )
                        for part in range(2):
                            total[side][part] += some[part][0:8] + some[part][8:16]
                for side in range(2):
                    for part in range(2):
                        row = pl.multiple_of((side * 2 + part) * 16 + at * 8, 8)
                        sums[pl.ds(row, 8), lanes] = total[side][part]

        rows = 0.0
        for quarter in range(4):
            some = sums[:, QX * quarter : QX * (quarter + 1)].astype(bf16)
            rows += jnp.dot(add_ref[quarter], some, preferred_element_type=f32)
        return rows.astype(bf16)

    def y_periodic(plane):
        for side in range(2):
            lanes = slice(side * NX // 2, (side + 1) * NX // 2)
            block = jnp.concatenate([planes[part, plane, :, lanes] for part in range(2)], axis=0)
            modes = jnp.dot(yf_ref[...], block, preferred_element_type=f32)
            scaled = [
                cmul(
                    (modes[some : some + 32], modes[BY + some : BY + some + 32]),
                    (factor[0, some : some + 32, lanes], factor[1, some : some + 32, lanes]),
                )
                for some in range(0, BY, 32)
            ]
            block = jnp.concatenate(
                [one[part].astype(bf16) for part in range(2) for one in scaled], axis=0
            )
            cells = jnp.dot(yi_ref[...], block, preferred_element_type=f32).astype(bf16)
            for part in range(2):
                planes[part, plane, :, lanes] = cells[part * BY : (part + 1) * BY]

    class Exchange:
        def __init__(self, send, recv, back, carry, sems, tiles):
            self.send, self.recv, self.back, self.carry = send, recv, back, carry
            self.sems, self.tiles = sems, tiles

        def mine(self):
            return pl.ds(me_y * self.tiles, self.tiles)

        def out(self, peer):
            return pltpu.make_async_remote_copy(
                src_ref=self.send.at[pl.ds(peer * self.tiles, self.tiles)],
                dst_ref=self.recv.at[me_y],
                send_sem=self.sems.at[0, peer],
                recv_sem=self.sems.at[1, me_y],
                device_id={"py": peer},
                device_id_type=MESH,
            )

        def arrived(self, peer):
            return pltpu.make_async_remote_copy(
                src_ref=self.send.at[self.mine()],
                dst_ref=self.recv.at[peer],
                send_sem=self.sems.at[0, me_y],
                recv_sem=self.sems.at[1, peer],
                device_id={"py": peer},
                device_id_type=MESH,
            )

        def give(self, peer):
            return pltpu.make_async_remote_copy(
                src_ref=self.back.at[peer],
                dst_ref=self.carry.at[self.mine()],
                send_sem=self.sems.at[2, peer],
                recv_sem=self.sems.at[3, me_y],
                device_id={"py": peer},
                device_id_type=MESH,
            )

        def given(self, peer):
            return pltpu.make_async_remote_copy(
                src_ref=self.back.at[me_y],
                dst_ref=self.carry.at[pl.ds(peer * self.tiles, self.tiles)],
                send_sem=self.sems.at[2, me_y],
                recv_sem=self.sems.at[3, peer],
                device_id={"py": peer},
                device_id_type=MESH,
            )

        def post(self):
            @pl.loop(1, count_py)
            def _(step):
                self.out(lax.rem(me_y + step, count_py)).start()

        def answer(self):
            self.recv[me_y] = self.send[self.mine()]

            @pl.loop(1, count_py)
            def _(step):
                self.arrived(lax.rem(me_y + step, count_py)).wait_recv()

            for tile in range(self.tiles):
                solve_tile(self.recv, self.back, tile, lax.rem(me_y * self.tiles + tile, 4))

            @pl.loop(1, count_py)
            def _(step):
                self.give(lax.rem(me_y + step, count_py)).start()

            self.carry[self.mine()] = self.back[me_y]

        def receive(self):
            @pl.loop(1, count_py)
            def _(step):
                self.given(lax.rem(me_y + step, count_py)).wait_recv()

        def close(self):
            @pl.loop(1, count_py)
            def _(step):
                peer = lax.rem(me_y + step, count_py)
                self.out(peer).wait_send()
                self.give(peer).wait_send()

        def rows(self, tiles):
            return [self.carry[tile].reshape(CARRY, QX) for tile in tiles]

    def solve_tile(recv, back, tile, quarter):
        table = ytab_ref[quarter]
        value = [(table[2 * n : 2 * n + 1], table[2 * n + 1 : 2 * n + 2]) for n in range(8)]
        whole1, whole2, _, _, wrap1, wrap2, out1, out2 = value
        left_state = [parts(recv[block, tile, 0]) for block in range(count_py)]
        right_state = [parts(recv[block, tile, 1]) for block in range(count_py)]
        left, right = left_state[0], right_state[count_py - 1]
        for block in range(1, count_py):
            left = cadd(left_state[block], cmul(left, whole1))
            right = cadd(right_state[count_py - 1 - block], cmul(right, whole2))
        left, right = cmul(left, wrap1), cmul(right, wrap2)
        for block in range(count_py):
            other = count_py - 1 - block
            back[block, tile, 0] = joined(cmul(left, out1))
            back[other, tile, 1] = joined(cmul(right, out2))
            left = cadd(left_state[block], cmul(left, whole1))
            right = cadd(right_state[other], cmul(right, whole2))

    planes_y = Exchange(y_send, y_recv, y_back, y_carry, y_sems, TILES_Y // count_py)
    def carry_out(step):
        return pltpu.make_async_remote_copy(
            src_ref=c_send,
            dst_ref=c_recv.at[me_y],
            send_sem=c_sems.at[0, lax.rem(me_y + step, count_py)],
            recv_sem=c_sems.at[1, me_y],
            device_id={"py": lax.rem(me_y + step, count_py)},
            device_id_type=MESH,
        )

    def carry_in(step):
        peer = lax.rem(me_y + step, count_py)
        return pltpu.make_async_remote_copy(
            src_ref=c_send,
            dst_ref=c_recv.at[peer],
            send_sem=c_sems.at[0, me_y],
            recv_sem=c_sems.at[1, peer],
            device_id={"py": peer},
            device_id_type=MESH,
        )

    def carry_solve():
        value = [(packed_ref[2 * n], packed_ref[2 * n + 1]) for n in range(8)]
        whole1, whole2, own1, own2, wrap1, wrap2, out1, out2 = value
        own = [parts(c_send[side]) for side in range(2)]
        left, right = own
        for step in range(1, count_py):
            left = cadd(parts(c_recv[lax.rem(me_y + step, count_py), 0]), cmul(left, whole1))
            back = lax.rem(me_y + count_py - step, count_py)
            right = cadd(parts(c_recv[back, 1]), cmul(right, whole2))
        left = csub(cmul(left, wrap1), cmul(own[0], own1))
        right = csub(cmul(right, wrap2), cmul(own[1], own2))
        return jnp.concatenate([joined(cmul(left, out1)), joined(cmul(right, out2))], axis=0)

    def post_planes(states):
        for half in range(2):
            lines = slice(8 * half, 8 * half + 8)
            for quarter in range(4):
                lanes = slice(QX * quarter, QX * (quarter + 1))
                for side in range(2):
                    y_send[half * 4 + quarter, side] = joined(
                        [states[side][part][lines, lanes] for part in range(2)]
                    )
        planes_y.post()

    sweep_field()

    @pl.loop(1, chips)
    def _(step):
        for tile in range(tiles_z):
            z_in(step, tile).wait_recv()

    for tile in range(tiles_z):

        def state(block, side):
            return parts(z_recv[block, tile, side])

        def advance(total, value):
            return cadd(cmul(total, (chip_step.real, chip_step.imag)), value)

        def gather(step, carry):
            left, right = carry
            return (
                advance(left, state(step, 0)),
                advance(right, state(chips - 1 - step, 1)),
            )

        zero = (jnp.zeros((8, QX), f32), jnp.zeros((8, QX), f32))
        left, right = lax.fori_loop(0, chips, gather, (zero, zero), unroll=8)
        wrap = 1 / (1 - chip_step**chips)
        left = cmul(left, (wrap.real, wrap.imag))
        right = cmul(right, (wrap.real, wrap.imag))

        def hand_out(step, carry):
            left, right = carry
            last = chips - 1 - step
            z_back[step, tile, 0] = joined(left)
            z_back[last, tile, 1] = joined(right)
            return advance(left, state(step, 0)), advance(right, state(last, 1))

        lax.fori_loop(0, chips, hand_out, (left, right), unroll=8)

    @pl.loop(1, chips)
    def _(step):
        z_return(step).start()

    z_chip[pl.ds(chip * tiles_z, tiles_z)] = z_back[chip]

    forward_state, backward_state = y_forward()
    post_planes((forward_state, backward_state))
    back_total = y_backward(0, BY // 2, cmul(forward_state, turn_step))

    @pl.loop(1, chips)
    def _(step):
        z_returned(step).wait_recv()

    @pl.loop(0, half_z)
    def _(tile):
        own = [parts(z_states[mine + tile, side]) for side in range(2)]
        other = [parts(z_partner[tile, side]) for side in range(2)]
        whole = [parts(z_chip[tile, side]) for side in range(2)]
        inner_left = cadd(choose(own[0], other[0]), cmul(whole[0], block_step))
        inner_right = cadd(choose(other[1], own[1]), cmul(whole[1], block_step))
        z_give[tile, 0] = joined(choose(inner_left, whole[0]))
        z_give[tile, 1] = joined(choose(whole[1], inner_right))
        z_carry[mine + tile, 0] = joined(choose(whole[0], inner_left))
        z_carry[mine + tile, 1] = joined(choose(inner_right, whole[1]))

    pair_back().start()

    y_backward(BY // 2, BY, back_total)
    pair_returned().wait_recv()

    def fetch(n):
        sides = [
            jnp.concatenate([z_carry[n * 4 + quarter, side] for quarter in range(4)], axis=1)
            for side in range(2)
        ]
        sides = [side.astype(f32) for side in sides]
        return tuple(
            jnp.concatenate([side[8 * part : 8 * part + 8] for side in sides], axis=0)
            for part in range(2)
        )

    def put(n, done):
        for side in range(2):
            lines = slice(8 * side, 8 * side + 8)
            for part in range(2):
                planes[part, side, 8 * n : 8 * n + 16, :] = jnp.concatenate(
                    [done[at][part][lines] for at in range(2)], axis=0
                ).astype(bf16)

    def gain(n):
        lines = slice(8 * n, 8 * n + 8)
        return [
            tuple(
                jnp.concatenate([gains[2 * residue + part, lines, :]] * 2, axis=0)
                for part in range(2)
            )
            for residue in range(4)
        ]

    x_sweep(GROUPS, fetch, gain, put, left_buf, cells_buf, xf, xi)
    c_send[...] = y_states(2).reshape(2, 16, QX)

    @pl.loop(1, count_py)
    def _(step):
        carry_out(step).start()

    planes_y.answer()
    y_periodic(0)
    y_periodic(1)

    def store(pair):
        rows = pl.ds(pl.multiple_of(pair * 16, 16), 16)
        return pltpu.make_async_copy(
            result.at[:, :, rows, :], field_hbm.at[:, :, rows, :], out_sem.at[pair]
        )

    @pl.loop(0, BY // 16)
    def _(pair):
        rows = pl.ds(pl.multiple_of(pair * 16, 16), 16)
        for quarter in range(4):
            lanes = slice(QX * quarter, QX * (quarter + 1))
            left, right = [
                tuple(planes[part, one, rows, lanes].astype(f32) for part in range(2))
                for one in range(2)
            ]
            for plane in range(BZ):
                first, second = (complex(one) for one in z_profile[plane])
                lines = pl.ds(pair * 16 * BZ + plane, 16, stride=BZ)
                value = tuple(solved[part, quarter, lines, :] for part in range(2))
                value = cadd(value, cmul(left, (first.real, first.imag)))
                value = cadd(value, cmul(right, (second.real, second.imag)))
                for part in range(2):
                    result[part, plane, rows, lanes] = value[part].astype(bf16)
        store(pair).start()

    @pl.loop(1, count_py)
    def _(step):
        carry_in(step).wait_recv()

    carried = carry_solve()
    planes_y.receive()
    for quarter in range(4):
        rows = planes_y.rows((quarter, 4 + quarter)) + [carried]
        change[:, :, QX * quarter : QX * (quarter + 1)] = jnp.dot(
            turn_ref[quarter], jnp.concatenate(rows, axis=0), preferred_element_type=f32
        ).reshape(BZ, 8, QX)
    last = pltpu.make_async_copy(change, change_hbm, out_sem.at[GROUPS // 2])
    last.start()

    @pl.loop(0, half_z)
    def _(tile):
        @pl.when(tile // tiles_z != chip)
        def _():
            z_out(tile).wait_send()

    @pl.loop(1, chips)
    def _(step):
        z_return(step).wait_send()

    @pl.loop(0, GROUPS // 2)
    def _(step):
        pair_out(step).wait_send()

    pair_back().wait_send()

    planes_y.close()

    @pl.loop(1, count_py)
    def _(step):
        carry_out(step).wait_send()


    @pl.loop(0, GROUPS // 2)
    def _(pair):
        store(pair).wait()

    last.wait()


PLANES = 2


def finish_kernel(
    field_hbm,
    change_hbm,
    pot_hbm,
    table_hbm,
    out_hbm,
    field,
    change,
    pot,
    table,
    out,
    in_sem,
    tab_sem,
    out_sem,
):
    steps = BZ // PLANES

    def load(step):
        planes = pl.ds(step * PLANES, PLANES)
        return (
            pltpu.make_async_copy(field_hbm.at[:, planes], field.at[:, planes], in_sem.at[0, step]),
            pltpu.make_async_copy(pot_hbm.at[planes], pot.at[planes], in_sem.at[1, step]),
        )

    def save(step):
        planes = pl.ds(step * PLANES, PLANES)
        return pltpu.make_async_copy(out.at[:, planes], out_hbm.at[:, planes], out_sem.at[step])

    tables = (
        pltpu.make_async_copy(change_hbm, change, tab_sem.at[0]),
        pltpu.make_async_copy(table_hbm, table, tab_sem.at[1]),
    )
    for copy in tables:
        copy.start()
    for step in range(steps):
        for copy in load(step):
            copy.start()
    for copy in tables:
        copy.wait()

    def finish(at, lanes):
        ends = [change[at, row : row + 1, lanes] for row in range(4)]
        for start in range(0, BY, 16):
            rows = slice(start, start + 16)
            value = tuple(field[part, at, rows, lanes].astype(f32) for part in range(2))
            for side in range(2):
                profile = (table[2 * side, rows, lanes], table[2 * side + 1, rows, lanes])
                value = cadd(value, cmul(profile, (ends[2 * side], ends[2 * side + 1])))
            new = kick(value[0], value[1], pot[at, rows, lanes])
            for part in range(2):
                out[part, at, rows, lanes] = new[part]

    @pl.loop(0, steps)
    def _(step):
        for copy in load(step):
            copy.wait()
        for one in range(PLANES):
            for side in range(2):
                finish(step * PLANES + one, slice(side * NX // 2, (side + 1) * NX // 2))
        save(step).start()

    @pl.loop(0, steps)
    def _(step):
        save(step).wait()


def shards(count_py, count_pz, wavefunction, potential):
    forward_x, inverse_x, trig = x_tables()
    z_rows, turn, z_profile, z_step = z_tables()
    forward_y, inverse_y, factor, weight, homogeneous, steps_y, add, y_table, packed = y_tables(count_py)

    def low(array):
        return jnp.asarray(array.astype(np.float32)).astype(bf16)

    def full(array):
        return jnp.asarray(array.astype(np.float32))

    chips = count_pz // 2
    tiles_z = TILES_Z // 2 // chips
    tiles_y = TILES_Y // count_py
    anywhere = pl.BlockSpec(memory_space=pl.ANY)
    inside = pl.BlockSpec(memory_space=pltpu.VMEM)
    field, change = pl.pallas_call(
        functools.partial(main_kernel, count_py, count_pz, z_step, z_profile),
        out_shape=(
            pltpu.VMEM((2, BZ, BY, NX), bf16),
            pltpu.VMEM((BZ, 8, NX), f32),
        ),
        in_specs=[anywhere] * 6 + [inside] * 9,
        out_specs=(anywhere, anywhere),
        scratch_shapes=[
            pltpu.VMEM((GROUPS, 2, BZ, 8, NX), f32),
            pltpu.VMEM((GROUPS, BZ, 8, NX), f32),
            pltpu.VMEM((4, 2 * QX, 2 * QX), bf16),
            pltpu.VMEM((4, 2 * QX, 2 * QX), bf16),
            pltpu.VMEM(weight.shape, f32),
            pltpu.VMEM(factor.shape, f32),
            pltpu.VMEM((ROWS, NX), bf16),
            pltpu.VMEM((ROWS, NX), bf16),
            pltpu.VMEM((8, BY, QX), f32),
            pltpu.VMEM((GROUPS, ROWS, NX), bf16),
            pltpu.VMEM((2, BY * BZ, NX), bf16),
            pltpu.VMEM((2, 4, BY * BZ, QX), f32),
            pltpu.VMEM((2, 2, BY, NX), bf16),
            pltpu.VMEM((2, BZ, BY, NX), bf16),
            pltpu.VMEM((4, BY * BZ, 2 * QX), bf16),
            pltpu.VMEM((4, BY * BZ, 2 * QX), f32),
            pltpu.VMEM((64, NX), f32),
            pltpu.VMEM((TILES_Z, 2, 16, QX), bf16),
            pltpu.VMEM((TILES_Z // 2, 2, 16, QX), bf16),
            pltpu.VMEM((TILES_Z // 2, 2, 16, QX), bf16),
            pltpu.VMEM((chips, tiles_z, 2, 16, QX), bf16),
            pltpu.VMEM((chips, tiles_z, 2, 16, QX), bf16),
            pltpu.VMEM((TILES_Z // 2, 2, 16, QX), bf16),
            pltpu.VMEM((TILES_Z // 2, 2, 16, QX), bf16),
            pltpu.VMEM((TILES_Z, 2, 16, QX), bf16),
            pltpu.VMEM((TILES_Y, 2, 16, QX), bf16),
            pltpu.VMEM((count_py, tiles_y, 2, 16, QX), bf16),
            pltpu.VMEM((count_py, tiles_y, 2, 16, QX), bf16),
            pltpu.VMEM((TILES_Y, 2, 16, QX), bf16),
            pltpu.VMEM((2, 16, QX), bf16),
            pltpu.VMEM((count_py, 2, 16, QX), bf16),
            pltpu.VMEM((BZ, 8, NX), f32),
            pltpu.SemaphoreType.DMA((2, GROUPS)),
            pltpu.SemaphoreType.DMA((4,)),
            pltpu.SemaphoreType.DMA((GROUPS // 2 + 1,)),
            pltpu.SemaphoreType.DMA((2, 5)),
            pltpu.SemaphoreType.DMA((2, TILES_Z // 2)),
            pltpu.SemaphoreType.DMA((2, chips)),
            pltpu.SemaphoreType.DMA((4, count_py)),
            pltpu.SemaphoreType.DMA((2, count_py)),
        ],
        compiler_params=pltpu.CompilerParams(
            collective_id=0, has_side_effects=True, vmem_limit_bytes=57 * 2**20
        ),
        cost_estimate=pl.CostEstimate(
            flops=3_000_000_000, bytes_accessed=10_000_000, transcendentals=0
        ),
        name="sweeps",
    )(
        wavefunction,
        potential,
        low(forward_x),
        low(inverse_x),
        full(weight),
        full(factor),
        full(trig),
        low(z_rows),
        low(forward_y),
        low(inverse_y),
        low(add),
        low(turn),
        full(y_table),
        full(steps_y),
        full(packed),
    )
    return pl.pallas_call(
        finish_kernel,
        out_shape=jax.ShapeDtypeStruct((2, BZ, BY, NX), f32),
        in_specs=[anywhere] * 4,
        out_specs=anywhere,
        scratch_shapes=[
            pltpu.VMEM((2, BZ, BY, NX), bf16),
            pltpu.VMEM((BZ, 8, NX), f32),
            pltpu.VMEM((BZ, BY, NX), f32),
            pltpu.VMEM(homogeneous.shape, f32),
            pltpu.VMEM((2, BZ, BY, NX), f32),
            pltpu.SemaphoreType.DMA((2, BZ // PLANES)),
            pltpu.SemaphoreType.DMA((2,)),
            pltpu.SemaphoreType.DMA((BZ // PLANES,)),
        ],
        compiler_params=pltpu.CompilerParams(vmem_limit_bytes=16 * 2**20),
        cost_estimate=pl.CostEstimate(
            flops=800_000_000, bytes_accessed=9_000_000, transcendentals=0
        ),
        name="finish",
    )(field, change, potential, full(homogeneous))


def solution(mesh):
    return jax.shard_map(
        functools.partial(shards, mesh.shape["py"], mesh.shape["pz"]),
        mesh=mesh,
        in_specs=(P(None, "pz", "py", None), P("pz", "py", None)),
        out_specs=P(None, "pz", "py", None),
        check_vma=False,
    )
```

```python
import functools

import jax
import jax.numpy as jnp
import numpy as np
from jax import lax
from jax.experimental import pallas as pl
from jax.experimental.pallas import tpu as pltpu
from jax.sharding import PartitionSpec as P

time_step = 0.005
rotation = 0.9
coupling = 100.0
grid_spacing = 0.05

NX = 512
BY = 64
BZ = 16
QX = 128
GROUPS = BY // 8
TILES_Z = GROUPS * 4
TILES_Y = 8
ROWS = 2 * BZ * 8
CARRY = 32

MESH = pl.DeviceIdType.MESH
f32 = jnp.float32
bf16 = jnp.bfloat16


def line_roots(beta):
    beta = np.asarray(beta, np.float64)
    half = (beta - 1j) / 2
    spread = np.sqrt((1 + 1j) ** 2 - (beta - 1j) * (-beta - 1j))
    first = (-(1 + 1j) + spread) / (beta - 1j)
    second = (-(1 + 1j) - spread) / (beta - 1j)
    swap = np.abs(first) > np.abs(second)
    inner = np.where(swap, second, first)
    outer = np.where(swap, first, second)
    return inner, 1 / outer, half * (inner - outer)


def real_form(matrix):
    return np.stack(
        [
            np.stack([matrix.real, -matrix.imag], 1),
            np.stack([matrix.imag, matrix.real], 1),
        ],
        0,
    )


def x_tables():
    forward, inverse = [], []
    cells = np.arange(QX)
    for residue in range(4):
        modes = 4 * np.arange(QX) + residue
        angles = 2 * np.pi * ((cells[:, None] * modes[None, :]) % NX) / NX
        cosines, sines = np.cos(angles), np.sin(angles)
        forward.append(np.block([[cosines, -sines], [sines, cosines]]))
        inverse.append(np.block([[cosines.T, sines.T], [-sines.T, cosines.T]]) / NX)
    modes = 4 * np.arange(QX)[None, :] + np.arange(4)[:, None]
    theta = 2 * np.pi * modes / NX
    trig = np.stack([1 - np.cos(theta), np.sin(theta)], 1).reshape(8, QX)
    return np.stack(forward), np.stack(inverse), trig


def z_tables():
    lam, _, scale = line_roots(0.0)
    lam, scale = complex(lam), complex(scale)
    cells = np.arange(BZ)
    local = (2 / scale) * lam ** np.abs(cells[:, None] - cells[None, :]) - np.eye(BZ)
    carry = (2 / scale) * np.stack([lam ** (cells + 1), lam ** (BZ - cells)], 1)
    states = np.stack([lam ** (BZ - 1 - cells), lam**cells], 0)
    eye = np.eye(8)
    apply_field = np.einsum("azbw,ij->aizbwj", real_form(local), eye).reshape(ROWS, ROWS)
    state_rows = np.einsum("asbz,ij->saibzj", real_form(states), eye).reshape(CARRY, ROWS)
    turn = np.zeros((4, BZ, 8, 3, 4, 8))
    fields, carries = real_form(np.eye(BZ).astype(complex)), real_form(carry)
    for end in range(2):
        for out in range(2):
            for part in range(2):
                row, column = 2 * end + out, 2 * end + part
                for half in range(2):
                    turn[:, :, row, half, column, :] = fields[
                        out, :, part, 8 * half : 8 * half + 8
                    ]
                for quarter in range(4):
                    lines = slice(2 * quarter, 2 * quarter + 2)
                    turn[quarter, :, row, 2, column, lines] = carries[out, :, part, :]
    turn = turn.reshape(4, BZ * 8, 3 * CARRY)
    return np.concatenate([apply_field, state_rows], 0), turn, carry, lam**BZ


def y_tables(blocks):
    cells = np.arange(BY)
    angles = 2 * np.pi * ((cells[:, None] * cells[None, :]) % BY) / BY
    modes = np.exp(-1j * angles)
    forward = real_form(modes).reshape(2 * BY, 2 * BY)
    inverse = real_form(np.conj(modes) / BY).reshape(2 * BY, 2 * BY)
    beta = -0.5 * time_step * rotation * (np.arange(NX) - NX // 2)
    theta = 2 * np.pi * cells / BY
    rate = (1 - np.cos(theta))[:, None] + np.sin(theta)[:, None] * beta[None, :]
    factor = (1 - 1j * rate) / (1 + 1j * rate)
    lam1, lam2, scale = line_roots(beta)
    whole1, whole2 = lam1**BY, lam2**BY
    rows = [
        whole1,
        whole2,
        1 / (1 - whole1),
        1 / (1 - whole2),
        1 / (1 - whole1**blocks),
        1 / (1 - whole2**blocks),
        2 * lam1 / scale,
        2 * lam2 / scale,
    ]
    apart = 1 - lam1 * lam2
    steps = [lam1, lam2, lam1 / apart, 2 * apart / scale]
    table = np.stack([part for row in rows for part in (row.real, row.imag)])
    down, up = np.arange(BY)[:, None], BY - 1 - np.arange(BY)[:, None]
    states = [lam1**up, lam2**down]
    homogeneous = [lam1**down, lam2**up]
    add = np.zeros((4, 4, 8, 4, 2, 8))
    for quarter in range(4):
        for plane in range(2):
            for part in range(4):
                add[quarter, part, 2 * quarter + plane, part, plane, :] = 1
    add = add.reshape(4, CARRY, 64)
    table = table.reshape(len(table), 4, QX)
    packed = np.repeat(table, 2, axis=1)
    table = table.transpose(1, 0, 2)

    def parts(values):
        return np.stack([part for value in values for part in (value.real, value.imag)])

    return (
        forward,
        inverse,
        parts([factor]),
        parts(states),
        parts(homogeneous),
        parts(steps),
        add,
        table,
        packed,
    )


def kick(real_part, imag_part, potential):
    turn = -0.5 * time_step / (2 * np.pi)
    density = real_part * real_part + imag_part * imag_part
    turns = potential * turn + density * (turn * coupling)
    rest = turns - jnp.round(turns)
    square = rest * rest
    sine = rest * (
        4.4428679 + square * (-7.30744342 + square * (3.59478806 + square * -0.78437396))
    )
    cosine = 1.4142135 + square * (
        -6.97885099 + square * (5.73946123 + square * (-1.88356328 + square * 0.31069871))
    )
    whole_cos = 1.0 - sine * sine
    whole_sin = sine * cosine
    return (
        real_part * whole_cos - imag_part * whole_sin,
        real_part * whole_sin + imag_part * whole_cos,
    )


def cmul(a, b):
    return a[0] * b[0] - a[1] * b[1], a[0] * b[1] + a[1] * b[0]


def cadd(a, b):
    return a[0] + b[0], a[1] + b[1]


def csub(a, b):
    return a[0] - b[0], a[1] - b[1]


def split_modes(real_part, imag_part):
    quarter = [
        (real_part[:, QX * p : QX * (p + 1)], imag_part[:, QX * p : QX * (p + 1)])
        for p in range(4)
    ]
    t0, t1 = cadd(quarter[0], quarter[2]), csub(quarter[0], quarter[2])
    t2, t3 = cadd(quarter[1], quarter[3]), csub(quarter[1], quarter[3])
    return [
        cadd(t0, t2),
        (t1[0] + t3[1], t1[1] - t3[0]),
        csub(t0, t2),
        (t1[0] - t3[1], t1[1] + t3[0]),
    ]


def join_modes(back):
    t0, t1 = cadd(back[0], back[2]), csub(back[0], back[2])
    t2, t3 = cadd(back[1], back[3]), csub(back[1], back[3])
    return [
        cadd(t0, t2),
        (t1[0] - t3[1], t1[1] + t3[0]),
        csub(t0, t2),
        (t1[0] + t3[1], t1[1] - t3[0]),
    ]


def x_sweep(count, load, factors, store, left, cells, forward_ref, inverse_ref):
    rows = 16 * count
    for n in range(count):
        mixed = split_modes(*load(n))
        for residue in range(4):
            left[residue, 16 * n : 16 * n + 16, :] = jnp.concatenate(mixed[residue], axis=1)
    for residue in range(4):
        modes = jnp.dot(left[residue, 0:rows, :], forward_ref[residue], preferred_element_type=f32)
        for n in range(count):
            some = modes[16 * n : 16 * n + 16]
            scaled = cmul((some[:, :QX], some[:, QX:]), factors(n)[residue])
            left[residue, 16 * n : 16 * n + 16, :] = jnp.concatenate(scaled, axis=1).astype(bf16)
    for residue in range(4):
        cells[residue, 0:rows, :] = jnp.dot(
            left[residue, 0:rows, :], inverse_ref[residue], preferred_element_type=f32
        )
    for n in range(0, count, 2):
        done = []
        for at in range(2):
            lines = slice(16 * (n + at), 16 * (n + at) + 16)
            some = [cells[residue, lines, :] for residue in range(4)]
            out = join_modes([(one[:, :QX], one[:, QX:]) for one in some])
            done.append([jnp.concatenate([one[part] for one in out], axis=1) for part in range(2)])
        store(n, done)


def main_kernel(
    count_py,
    count_pz,
    z_step,
    z_profile,
    wave_hbm,
    pot_hbm,
    xf_hbm,
    xi_hbm,
    weight_hbm,
    factor_hbm,
    trig_ref,
    z_ref,
    yf_ref,
    yi_ref,
    add_ref,
    turn_ref,
    ytab_ref,
    step_ref,
    packed_ref,
    field_hbm,
    change_hbm,
    wave,
    pot,
    xf,
    xi,
    weight,
    factor,
    fresh_a,
    fresh_b,
    gains,
    grid,
    swept,
    solved,
    planes,
    result,
    left_buf,
    cells_buf,
    sums,
    z_states,
    z_partner,
    z_send,
    z_recv,
    z_back,
    z_chip,
    z_give,
    z_carry,
    y_send,
    y_recv,
    y_back,
    y_carry,
    c_send,
    c_recv,
    change,
    in_sem,
    tab_sem,
    out_sem,
    pair_sems,
    z_sems,
    z_back_sems,
    y_sems,
    c_sems,
):
    me_y = lax.axis_index("py")
    me_z = lax.axis_index("pz")
    core = lax.rem(me_z, 2)
    chip = me_z // 2
    partner = me_z + 1 - 2 * core
    chips = count_pz // 2
    half_z = TILES_Z // 2
    tiles_z = half_z // chips
    mine = core * half_z
    theirs = half_z - mine

    def load(group):
        rows = pl.ds(pl.multiple_of(group * 8, 8), 8)
        return (
            pltpu.make_async_copy(wave_hbm.at[:, :, rows, :], wave.at[group], in_sem.at[0, group]),
            pltpu.make_async_copy(pot_hbm.at[:, rows, :], pot.at[group], in_sem.at[1, group]),
        )

    for group in range(GROUPS):
        for copy in load(group):
            copy.start()
    table_copies = (
        pltpu.make_async_copy(xf_hbm, xf, tab_sem.at[0]),
        pltpu.make_async_copy(xi_hbm, xi, tab_sem.at[1]),
        pltpu.make_async_copy(weight_hbm, weight, tab_sem.at[2]),
        pltpu.make_async_copy(factor_hbm, factor, tab_sem.at[3]),
    )
    for copy in table_copies:
        copy.start()

    barrier = pltpu.get_barrier_semaphore()

    def twin(other):
        return {"pz": other * 2 + core}

    pl.semaphore_signal(barrier, inc=1, device_id={"pz": partner}, device_id_type=MESH)

    @pl.loop(1, chips)
    def _(step):
        pl.semaphore_signal(
            barrier, inc=1, device_id=twin(lax.rem(chip + step, chips)), device_id_type=MESH
        )

    @pl.loop(1, count_py)
    def _(step):
        pl.semaphore_signal(
            barrier, inc=1, device_id={"py": lax.rem(me_y + step, count_py)}, device_id_type=MESH
        )

    for group in range(GROUPS):
        cell = lax.broadcasted_iota(jnp.int32, (8, QX), 0) + (
            me_y * BY + group * 8 - count_py * BY // 2
        )
        beta = cell.astype(f32) * (0.5 * time_step * rotation)
        for residue in range(4):
            rate = trig_ref[2 * residue : 2 * residue + 1] + beta * trig_ref[
                2 * residue + 1 : 2 * residue + 2
            ]
            scale = 1.0 / (1.0 + rate * rate)
            lines = slice(8 * group, 8 * group + 8)
            gains[2 * residue, lines, :] = (1.0 - rate * rate) * scale
            gains[2 * residue + 1, lines, :] = -2.0 * rate * scale

    def kick_group(group, fresh):
        for some in range(BZ // 2):
            rows = slice(2 * some, 2 * some + 2)
            new = kick(wave[group, 0, rows], wave[group, 1, rows], pot[group, rows])
            for part in range(2):
                start = ROWS // 2 * part + 16 * some
                fresh[start : start + 16, :] = new[part].reshape(16, NX).astype(bf16)

    def solve_group(group, fresh):
        for side in range(2):
            lanes = slice(side * NX // 2, (side + 1) * NX // 2)
            rows = jnp.dot(z_ref[...], fresh[:, lanes], preferred_element_type=f32)
            for start in range(0, ROWS, 16):
                grid[group, start : start + 16, lanes] = rows[start : start + 16].astype(bf16)
            states = rows[ROWS:].astype(bf16)
            for quarter in range(2):
                z_states[group * 4 + 2 * side + quarter] = states[
                    :, QX * quarter : QX * (quarter + 1)
                ].reshape(2, 16, QX)

    def pair_out(step):
        return pltpu.make_async_remote_copy(
            src_ref=z_states.at[pl.ds(theirs + 4 * step, 4)],
            dst_ref=z_partner.at[pl.ds(4 * step, 4)],
            send_sem=pair_sems.at[0, step],
            recv_sem=pair_sems.at[1, step],
            device_id={"pz": partner},
            device_id_type=MESH,
        )

    def pair_back():
        return pltpu.make_async_remote_copy(
            src_ref=z_give,
            dst_ref=z_carry.at[pl.ds(mine, half_z)],
            send_sem=pair_sems.at[0, 4],
            recv_sem=pair_sems.at[1, 4],
            device_id={"pz": partner},
            device_id_type=MESH,
        )

    def pair_returned():
        return pltpu.make_async_remote_copy(
            src_ref=z_give,
            dst_ref=z_carry.at[pl.ds(theirs, half_z)],
            send_sem=pair_sems.at[0, 4],
            recv_sem=pair_sems.at[1, 4],
            device_id={"pz": partner},
            device_id_type=MESH,
        )

    def z_out(tile):
        return pltpu.make_async_remote_copy(
            src_ref=z_send.at[tile],
            dst_ref=z_recv.at[chip, lax.rem(tile, tiles_z)],
            send_sem=z_sems.at[0, tile],
            recv_sem=z_sems.at[1, chip * tiles_z + lax.rem(tile, tiles_z)],
            device_id=twin(tile // tiles_z),
            device_id_type=MESH,
        )

    def z_in(step, tile):
        peer = lax.rem(chip + step, chips)
        return pltpu.make_async_remote_copy(
            src_ref=z_send.at[tile],
            dst_ref=z_recv.at[peer, tile],
            send_sem=z_sems.at[0, tile],
            recv_sem=z_sems.at[1, peer * tiles_z + tile],
            device_id=twin(peer),
            device_id_type=MESH,
        )

    def z_return(step):
        peer = lax.rem(chip + step, chips)
        return pltpu.make_async_remote_copy(
            src_ref=z_back.at[peer],
            dst_ref=z_chip.at[pl.ds(chip * tiles_z, tiles_z)],
            send_sem=z_back_sems.at[0, peer],
            recv_sem=z_back_sems.at[1, chip],
            device_id=twin(peer),
            device_id_type=MESH,
        )

    def z_returned(step):
        peer = lax.rem(chip + step, chips)
        return pltpu.make_async_remote_copy(
            src_ref=z_back.at[chip],
            dst_ref=z_chip.at[pl.ds(peer * tiles_z, tiles_z)],
            send_sem=z_back_sems.at[0, chip],
            recv_sem=z_back_sems.at[1, peer],
            device_id=twin(peer),
            device_id_type=MESH,
        )

    lead = core == 0
    block_step = (z_step.real, z_step.imag)
    chip_step = z_step * z_step

    def parts(array):
        array = array.astype(f32)
        return array[0:8], array[8:16]

    def choose(first, second):
        return jnp.where(lead, first[0], second[0]), jnp.where(lead, first[1], second[1])

    def joined(value):
        return jnp.concatenate(value, axis=0).astype(bf16)

    def order(count):
        if count < GROUPS // 2:
            return theirs // 4 + count
        return mine // 4 + lax.rem(count + chip // 4, GROUPS // 2)

    def merge(step):
        pair_out(step).wait_recv()
        for at in range(4):
            tile = step * 4 + at
            own = [parts(z_states[mine + tile, side]) for side in range(2)]
            other = [parts(z_partner[tile, side]) for side in range(2)]
            left = cadd(choose(other[0], own[0]), cmul(choose(own[0], other[0]), block_step))
            right = cadd(choose(own[1], other[1]), cmul(choose(other[1], own[1]), block_step))
            z_send[tile, 0] = joined(left)
            z_send[tile, 1] = joined(right)
        for at in range(4):
            tile = step * 4 + at
            owner = tile // tiles_z

            @pl.when(owner != chip)
            def _():
                z_out(tile).start()

            @pl.when(owner == chip)
            def _():
                z_recv[chip, lax.rem(tile, tiles_z)] = z_send[tile]

    def kicked(count, fresh):
        for copy in load(order(count)):
            copy.wait()
        kick_group(order(count), fresh)

    fresh = (fresh_a, fresh_b)
    kicked(0, fresh[0])
    for count in range(GROUPS):
        if count + 1 < GROUPS:
            for copy in load(order(count + 1)):
                copy.wait()
        solve_group(order(count), fresh[count % 2])
        if count + 1 < GROUPS:
            kick_group(order(count + 1), fresh[(count + 1) % 2])
        if count == 0:
            pl.semaphore_wait(barrier, chips + count_py - 1)
        if count < GROUPS // 2:
            pair_out(count).start()
        else:
            merge(order(count) - mine // 4)

    for copy in table_copies:
        copy.wait()

    def sweep_field():
        def fetch(n):
            group, row = n // 8, n % 8 * BZ
            return tuple(
                grid[group, start : start + BZ, :] for start in (row, row + ROWS // 2)
            )

        def gain(n):
            line = slice(n, n + 1)
            return [
                (gains[2 * residue, line, :], gains[2 * residue + 1, line, :])
                for residue in range(4)
            ]

        def put(n, done):
            for at in range(2):
                start = (n + at) * BZ
                for part in range(2):
                    swept[part, start : start + BZ, :] = done[at][part].astype(bf16)

        x_sweep(BY, fetch, gain, put, left_buf, cells_buf, xf, xi)

    steps_y = [(step_ref[2 * n : 2 * n + 1], step_ref[2 * n + 1 : 2 * n + 2]) for n in range(4)]
    forward_step, backward_step, turn_step, whole_gain = steps_y

    def y_rows(cell):
        return pl.ds(pl.multiple_of(cell * BZ, BZ), BZ)

    def save(rows, value):
        for part in range(2):
            for quarter in range(4):
                solved[part, quarter, rows, :] = value[part][
                    :, QX * quarter : QX * (quarter + 1)
                ]

    def y_forward():
        def advance(cell, totals):
            total, other = totals
            rows = y_rows(cell)
            value = tuple(swept[part, rows, :].astype(f32) for part in range(2))
            total = cadd(value, cmul(total, forward_step))
            save(rows, total)
            share = tuple(weight[2 + part, pl.ds(cell, 1), :] for part in range(2))
            return total, cadd(other, cmul(value, share))

        zero = jnp.zeros((BZ, NX), f32)
        return lax.fori_loop(0, BY, advance, ((zero, zero), (zero, zero)), unroll=4)

    def y_backward(first, last, total):
        def advance(count, total):
            rows = y_rows(BY - 1 - count)
            value = tuple(
                jnp.concatenate([solved[part, quarter, rows, :] for quarter in range(4)], axis=1)
                for part in range(2)
            )
            total = cadd(value, cmul(total, backward_step))
            out = cmul(total, whole_gain)
            save(rows, [out[part] - swept[part, rows, :].astype(f32) for part in range(2)])
            return total

        return lax.fori_loop(first, last, advance, total, unroll=4)

    def y_states(count):
        @pl.loop(0, count)
        def _(at):
            for quarter in range(4):
                lanes = slice(QX * quarter, QX * (quarter + 1))
                total = [[0.0, 0.0], [0.0, 0.0]]
                for start in range(0, BY, 16):
                    rows = slice(start, start + 16)
                    value = [planes[part, at, rows, lanes].astype(f32) for part in range(2)]
                    for side in range(2):
                        some = cmul(
                            value, (weight[2 * side, rows, lanes], weight[2 * side + 1, rows, lanes])
                        )
                        for part in range(2):
                            total[side][part] += some[part][0:8] + some[part][8:16]
                for side in range(2):
                    for part in range(2):
                        row = pl.multiple_of((side * 2 + part) * 16 + at * 8, 8)
                        sums[pl.ds(row, 8), lanes] = total[side][part]

        rows = 0.0
        for quarter in range(4):
            some = sums[:, QX * quarter : QX * (quarter + 1)].astype(bf16)
            rows += jnp.dot(add_ref[quarter], some, preferred_element_type=f32)
        return rows.astype(bf16)

    def y_periodic(plane):
        for side in range(2):
            lanes = slice(side * NX // 2, (side + 1) * NX // 2)
            block = jnp.concatenate([planes[part, plane, :, lanes] for part in range(2)], axis=0)
            modes = jnp.dot(yf_ref[...], block, preferred_element_type=f32)
            scaled = [
                cmul(
                    (modes[some : some + 32], modes[BY + some : BY + some + 32]),
                    (factor[0, some : some + 32, lanes], factor[1, some : some + 32, lanes]),
                )
                for some in range(0, BY, 32)
            ]
            block = jnp.concatenate(
                [one[part].astype(bf16) for part in range(2) for one in scaled], axis=0
            )
            cells = jnp.dot(yi_ref[...], block, preferred_element_type=f32).astype(bf16)
            for part in range(2):
                planes[part, plane, :, lanes] = cells[part * BY : (part + 1) * BY]

    class Exchange:
        def __init__(self, send, recv, back, carry, sems, tiles):
            self.send, self.recv, self.back, self.carry = send, recv, back, carry
            self.sems, self.tiles = sems, tiles

        def mine(self):
            return pl.ds(me_y * self.tiles, self.tiles)

        def out(self, peer):
            return pltpu.make_async_remote_copy(
                src_ref=self.send.at[pl.ds(peer * self.tiles, self.tiles)],
                dst_ref=self.recv.at[me_y],
                send_sem=self.sems.at[0, peer],
                recv_sem=self.sems.at[1, me_y],
                device_id={"py": peer},
                device_id_type=MESH,
            )

        def arrived(self, peer):
            return pltpu.make_async_remote_copy(
                src_ref=self.send.at[self.mine()],
                dst_ref=self.recv.at[peer],
                send_sem=self.sems.at[0, me_y],
                recv_sem=self.sems.at[1, peer],
                device_id={"py": peer},
                device_id_type=MESH,
            )

        def give(self, peer):
            return pltpu.make_async_remote_copy(
                src_ref=self.back.at[peer],
                dst_ref=self.carry.at[self.mine()],
                send_sem=self.sems.at[2, peer],
                recv_sem=self.sems.at[3, me_y],
                device_id={"py": peer},
                device_id_type=MESH,
            )

        def given(self, peer):
            return pltpu.make_async_remote_copy(
                src_ref=self.back.at[me_y],
                dst_ref=self.carry.at[pl.ds(peer * self.tiles, self.tiles)],
                send_sem=self.sems.at[2, me_y],
                recv_sem=self.sems.at[3, peer],
                device_id={"py": peer},
                device_id_type=MESH,
            )

        def post(self):
            @pl.loop(1, count_py)
            def _(step):
                self.out(lax.rem(me_y + step, count_py)).start()

        def answer(self):
            self.recv[me_y] = self.send[self.mine()]

            @pl.loop(1, count_py)
            def _(step):
                self.arrived(lax.rem(me_y + step, count_py)).wait_recv()

            for tile in range(self.tiles):
                solve_tile(self.recv, self.back, tile, lax.rem(me_y * self.tiles + tile, 4))

            @pl.loop(1, count_py)
            def _(step):
                self.give(lax.rem(me_y + step, count_py)).start()

            self.carry[self.mine()] = self.back[me_y]

        def receive(self):
            @pl.loop(1, count_py)
            def _(step):
                self.given(lax.rem(me_y + step, count_py)).wait_recv()

        def close(self):
            @pl.loop(1, count_py)
            def _(step):
                peer = lax.rem(me_y + step, count_py)
                self.out(peer).wait_send()
                self.give(peer).wait_send()

        def rows(self, tiles):
            return [self.carry[tile].reshape(CARRY, QX) for tile in tiles]

    def solve_tile(recv, back, tile, quarter):
        table = ytab_ref[quarter]
        value = [(table[2 * n : 2 * n + 1], table[2 * n + 1 : 2 * n + 2]) for n in range(8)]
        whole1, whole2, _, _, wrap1, wrap2, out1, out2 = value
        left_state = [parts(recv[block, tile, 0]) for block in range(count_py)]
        right_state = [parts(recv[block, tile, 1]) for block in range(count_py)]
        left, right = left_state[0], right_state[count_py - 1]
        for block in range(1, count_py):
            left = cadd(left_state[block], cmul(left, whole1))
            right = cadd(right_state[count_py - 1 - block], cmul(right, whole2))
        left, right = cmul(left, wrap1), cmul(right, wrap2)
        for block in range(count_py):
            other = count_py - 1 - block
            back[block, tile, 0] = joined(cmul(left, out1))
            back[other, tile, 1] = joined(cmul(right, out2))
            left = cadd(left_state[block], cmul(left, whole1))
            right = cadd(right_state[other], cmul(right, whole2))

    planes_y = Exchange(y_send, y_recv, y_back, y_carry, y_sems, TILES_Y // count_py)
    def carry_out(step):
        return pltpu.make_async_remote_copy(
            src_ref=c_send,
            dst_ref=c_recv.at[me_y],
            send_sem=c_sems.at[0, lax.rem(me_y + step, count_py)],
            recv_sem=c_sems.at[1, me_y],
            device_id={"py": lax.rem(me_y + step, count_py)},
            device_id_type=MESH,
        )

    def carry_in(step):
        peer = lax.rem(me_y + step, count_py)
        return pltpu.make_async_remote_copy(
            src_ref=c_send,
            dst_ref=c_recv.at[peer],
            send_sem=c_sems.at[0, me_y],
            recv_sem=c_sems.at[1, peer],
            device_id={"py": peer},
            device_id_type=MESH,
        )

    def carry_solve():
        value = [(packed_ref[2 * n], packed_ref[2 * n + 1]) for n in range(8)]
        whole1, whole2, own1, own2, wrap1, wrap2, out1, out2 = value
        own = [parts(c_send[side]) for side in range(2)]
        left, right = own
        for step in range(1, count_py):
            left = cadd(parts(c_recv[lax.rem(me_y + step, count_py), 0]), cmul(left, whole1))
            back = lax.rem(me_y + count_py - step, count_py)
            right = cadd(parts(c_recv[back, 1]), cmul(right, whole2))
        left = csub(cmul(left, wrap1), cmul(own[0], own1))
        right = csub(cmul(right, wrap2), cmul(own[1], own2))
        return jnp.concatenate([joined(cmul(left, out1)), joined(cmul(right, out2))], axis=0)

    def post_planes(states):
        for half in range(2):
            lines = slice(8 * half, 8 * half + 8)
            for quarter in range(4):
                lanes = slice(QX * quarter, QX * (quarter + 1))
                for side in range(2):
                    y_send[half * 4 + quarter, side] = joined(
                        [states[side][part][lines, lanes] for part in range(2)]
                    )
        planes_y.post()

    sweep_field()

    @pl.loop(1, chips)
    def _(step):
        for tile in range(tiles_z):
            z_in(step, tile).wait_recv()

    for tile in range(tiles_z):

        def state(block, side):
            return parts(z_recv[block, tile, side])

        def advance(total, value):
            return cadd(cmul(total, (chip_step.real, chip_step.imag)), value)

        def gather(step, carry):
            left, right = carry
            return (
                advance(left, state(step, 0)),
                advance(right, state(chips - 1 - step, 1)),
            )

        zero = (jnp.zeros((8, QX), f32), jnp.zeros((8, QX), f32))
        left, right = lax.fori_loop(0, chips, gather, (zero, zero), unroll=8)
        wrap = 1 / (1 - chip_step**chips)
        left = cmul(left, (wrap.real, wrap.imag))
        right = cmul(right, (wrap.real, wrap.imag))

        def hand_out(step, carry):
            left, right = carry
            last = chips - 1 - step
            z_back[step, tile, 0] = joined(left)
            z_back[last, tile, 1] = joined(right)
            return advance(left, state(step, 0)), advance(right, state(last, 1))

        lax.fori_loop(0, chips, hand_out, (left, right), unroll=8)

    @pl.loop(1, chips)
    def _(step):
        z_return(step).start()

    z_chip[pl.ds(chip * tiles_z, tiles_z)] = z_back[chip]

    forward_state, backward_state = y_forward()
    post_planes((forward_state, backward_state))
    back_total = y_backward(0, BY // 2, cmul(forward_state, turn_step))

    @pl.loop(1, chips)
    def _(step):
        z_returned(step).wait_recv()

    def split_carry(tile, _):
        own = [parts(z_states[mine + tile, side]) for side in range(2)]
        other = [parts(z_partner[tile, side]) for side in range(2)]
        whole = [parts(z_chip[tile, side]) for side in range(2)]
        inner_left = cadd(choose(own[0], other[0]), cmul(whole[0], block_step))
        inner_right = cadd(choose(other[1], own[1]), cmul(whole[1], block_step))
        z_give[tile, 0] = joined(choose(inner_left, whole[0]))
        z_give[tile, 1] = joined(choose(whole[1], inner_right))
        z_carry[mine + tile, 0] = joined(choose(whole[0], inner_left))
        z_carry[mine + tile, 1] = joined(choose(inner_right, whole[1]))
        return 0

    lax.fori_loop(0, half_z, split_carry, 0, unroll=4)
    pair_back().start()

    y_backward(BY // 2, BY, back_total)
    pair_returned().wait_recv()

    def fetch(n):
        sides = [
            jnp.concatenate([z_carry[n * 4 + quarter, side] for quarter in range(4)], axis=1)
            for side in range(2)
        ]
        sides = [side.astype(f32) for side in sides]
        return tuple(
            jnp.concatenate([side[8 * part : 8 * part + 8] for side in sides], axis=0).astype(bf16)
            for part in range(2)
        )

    def put(n, done):
        for side in range(2):
            lines = slice(8 * side, 8 * side + 8)
            for part in range(2):
                planes[part, side, 8 * n : 8 * n + 16, :] = jnp.concatenate(
                    [done[at][part][lines] for at in range(2)], axis=0
                ).astype(bf16)

    def gain(n):
        lines = slice(8 * n, 8 * n + 8)
        return [
            tuple(
                jnp.concatenate([gains[2 * residue + part, lines, :]] * 2, axis=0)
                for part in range(2)
            )
            for residue in range(4)
        ]

    x_sweep(GROUPS, fetch, gain, put, left_buf, cells_buf, xf, xi)
    c_send[...] = y_states(2).reshape(2, 16, QX)

    @pl.loop(1, count_py)
    def _(step):
        carry_out(step).start()

    planes_y.answer()
    y_periodic(0)
    y_periodic(1)

    def store(pair):
        rows = pl.ds(pl.multiple_of(pair * 16, 16), 16)
        return pltpu.make_async_copy(
            result.at[:, :, rows, :], field_hbm.at[:, :, rows, :], out_sem.at[pair]
        )

    @pl.loop(0, BY // 16)
    def _(pair):
        rows = pl.ds(pl.multiple_of(pair * 16, 16), 16)
        for quarter in range(4):
            lanes = slice(QX * quarter, QX * (quarter + 1))
            left, right = [
                tuple(planes[part, one, rows, lanes].astype(f32) for part in range(2))
                for one in range(2)
            ]
            for plane in range(BZ):
                first, second = (complex(one) for one in z_profile[plane])
                lines = pl.ds(pair * 16 * BZ + plane, 16, stride=BZ)
                value = tuple(solved[part, quarter, lines, :] for part in range(2))
                value = cadd(value, cmul(left, (first.real, first.imag)))
                value = cadd(value, cmul(right, (second.real, second.imag)))
                for part in range(2):
                    result[part, plane, rows, lanes] = value[part].astype(bf16)
        store(pair).start()

    @pl.loop(0, half_z)
    def _(tile):
        @pl.when(tile // tiles_z != chip)
        def _():
            z_out(tile).wait_send()

    @pl.loop(1, chips)
    def _(step):
        z_return(step).wait_send()

    @pl.loop(0, GROUPS // 2)
    def _(step):
        pair_out(step).wait_send()

    pair_back().wait_send()

    @pl.loop(1, count_py)
    def _(step):
        carry_in(step).wait_recv()

    carried = carry_solve()
    planes_y.receive()
    for quarter in range(4):
        rows = planes_y.rows((quarter, 4 + quarter)) + [carried]
        change[:, :, QX * quarter : QX * (quarter + 1)] = jnp.dot(
            turn_ref[quarter], jnp.concatenate(rows, axis=0), preferred_element_type=f32
        ).reshape(BZ, 8, QX)
    last = pltpu.make_async_copy(change, change_hbm, out_sem.at[GROUPS // 2])
    last.start()

    planes_y.close()

    @pl.loop(1, count_py)
    def _(step):
        carry_out(step).wait_send()


    @pl.loop(0, GROUPS // 2)
    def _(pair):
        store(pair).wait()

    last.wait()


PLANES = 2


def finish_kernel(
    field_hbm,
    change_hbm,
    pot_hbm,
    table_hbm,
    out_hbm,
    field,
    change,
    pot,
    table,
    out,
    in_sem,
    tab_sem,
    out_sem,
):
    steps = BZ // PLANES

    def load(step):
        planes = pl.ds(step * PLANES, PLANES)
        return (
            pltpu.make_async_copy(field_hbm.at[:, planes], field.at[:, planes], in_sem.at[0, step]),
            pltpu.make_async_copy(pot_hbm.at[planes], pot.at[planes], in_sem.at[1, step]),
        )

    def save(step):
        planes = pl.ds(step * PLANES, PLANES)
        return pltpu.make_async_copy(out.at[:, planes], out_hbm.at[:, planes], out_sem.at[step])

    tables = (
        pltpu.make_async_copy(change_hbm, change, tab_sem.at[0]),
        pltpu.make_async_copy(table_hbm, table, tab_sem.at[1]),
    )
    for copy in tables:
        copy.start()
    for step in range(steps):
        for copy in load(step):
            copy.start()
    for copy in tables:
        copy.wait()

    def finish(at, lanes):
        ends = [change[at, row : row + 1, lanes] for row in range(4)]
        for start in range(0, BY, 16):
            rows = slice(start, start + 16)
            value = tuple(field[part, at, rows, lanes].astype(f32) for part in range(2))
            for side in range(2):
                profile = (table[2 * side, rows, lanes], table[2 * side + 1, rows, lanes])
                value = cadd(value, cmul(profile, (ends[2 * side], ends[2 * side + 1])))
            new = kick(value[0], value[1], pot[at, rows, lanes])
            for part in range(2):
                out[part, at, rows, lanes] = new[part]

    @pl.loop(0, steps)
    def _(step):
        for copy in load(step):
            copy.wait()
        for one in range(PLANES):
            for side in range(2):
                finish(step * PLANES + one, slice(side * NX // 2, (side + 1) * NX // 2))
        save(step).start()

    @pl.loop(0, steps)
    def _(step):
        save(step).wait()


def shards(count_py, count_pz, wavefunction, potential):
    forward_x, inverse_x, trig = x_tables()
    z_rows, turn, z_profile, z_step = z_tables()
    forward_y, inverse_y, factor, weight, homogeneous, steps_y, add, y_table, packed = y_tables(count_py)

    def low(array):
        return jnp.asarray(array.astype(np.float32)).astype(bf16)

    def full(array):
        return jnp.asarray(array.astype(np.float32))

    chips = count_pz // 2
    tiles_z = TILES_Z // 2 // chips
    tiles_y = TILES_Y // count_py
    anywhere = pl.BlockSpec(memory_space=pl.ANY)
    inside = pl.BlockSpec(memory_space=pltpu.VMEM)
    field, change = pl.pallas_call(
        functools.partial(main_kernel, count_py, count_pz, z_step, z_profile),
        out_shape=(
            pltpu.VMEM((2, BZ, BY, NX), bf16),
            pltpu.VMEM((BZ, 8, NX), f32),
        ),
        in_specs=[anywhere] * 6 + [inside] * 9,
        out_specs=(anywhere, anywhere),
        scratch_shapes=[
            pltpu.VMEM((GROUPS, 2, BZ, 8, NX), f32),
            pltpu.VMEM((GROUPS, BZ, 8, NX), f32),
            pltpu.VMEM((4, 2 * QX, 2 * QX), bf16),
            pltpu.VMEM((4, 2 * QX, 2 * QX), bf16),
            pltpu.VMEM(weight.shape, f32),
            pltpu.VMEM(factor.shape, f32),
            pltpu.VMEM((ROWS, NX), bf16),
            pltpu.VMEM((ROWS, NX), bf16),
            pltpu.VMEM((8, BY, QX), f32),
            pltpu.VMEM((GROUPS, ROWS, NX), bf16),
            pltpu.VMEM((2, BY * BZ, NX), bf16),
            pltpu.VMEM((2, 4, BY * BZ, QX), f32),
            pltpu.VMEM((2, 2, BY, NX), bf16),
            pltpu.VMEM((2, BZ, BY, NX), bf16),
            pltpu.VMEM((4, BY * BZ, 2 * QX), bf16),
            pltpu.VMEM((4, BY * BZ, 2 * QX), f32),
            pltpu.VMEM((64, NX), f32),
            pltpu.VMEM((TILES_Z, 2, 16, QX), bf16),
            pltpu.VMEM((TILES_Z // 2, 2, 16, QX), bf16),
            pltpu.VMEM((TILES_Z // 2, 2, 16, QX), bf16),
            pltpu.VMEM((chips, tiles_z, 2, 16, QX), bf16),
            pltpu.VMEM((chips, tiles_z, 2, 16, QX), bf16),
            pltpu.VMEM((TILES_Z // 2, 2, 16, QX), bf16),
            pltpu.VMEM((TILES_Z // 2, 2, 16, QX), bf16),
            pltpu.VMEM((TILES_Z, 2, 16, QX), bf16),
            pltpu.VMEM((TILES_Y, 2, 16, QX), bf16),
            pltpu.VMEM((count_py, tiles_y, 2, 16, QX), bf16),
            pltpu.VMEM((count_py, tiles_y, 2, 16, QX), bf16),
            pltpu.VMEM((TILES_Y, 2, 16, QX), bf16),
            pltpu.VMEM((2, 16, QX), bf16),
            pltpu.VMEM((count_py, 2, 16, QX), bf16),
            pltpu.VMEM((BZ, 8, NX), f32),
            pltpu.SemaphoreType.DMA((2, GROUPS)),
            pltpu.SemaphoreType.DMA((4,)),
            pltpu.SemaphoreType.DMA((GROUPS // 2 + 1,)),
            pltpu.SemaphoreType.DMA((2, 5)),
            pltpu.SemaphoreType.DMA((2, TILES_Z // 2)),
            pltpu.SemaphoreType.DMA((2, chips)),
            pltpu.SemaphoreType.DMA((4, count_py)),
            pltpu.SemaphoreType.DMA((2, count_py)),
        ],
        compiler_params=pltpu.CompilerParams(
            collective_id=0, has_side_effects=True, vmem_limit_bytes=57 * 2**20
        ),
        cost_estimate=pl.CostEstimate(
            flops=3_000_000_000, bytes_accessed=10_000_000, transcendentals=0
        ),
        name="sweeps",
    )(
        wavefunction,
        potential,
        low(forward_x),
        low(inverse_x),
        full(weight),
        full(factor),
        full(trig),
        low(z_rows),
        low(forward_y),
        low(inverse_y),
        low(add),
        low(turn),
        full(y_table),
        full(steps_y),
        full(packed),
    )
    return pl.pallas_call(
        finish_kernel,
        out_shape=jax.ShapeDtypeStruct((2, BZ, BY, NX), f32),
        in_specs=[anywhere] * 4,
        out_specs=anywhere,
        scratch_shapes=[
            pltpu.VMEM((2, BZ, BY, NX), bf16),
            pltpu.VMEM((BZ, 8, NX), f32),
            pltpu.VMEM((BZ, BY, NX), f32),
            pltpu.VMEM(homogeneous.shape, f32),
            pltpu.VMEM((2, BZ, BY, NX), f32),
            pltpu.SemaphoreType.DMA((2, BZ // PLANES)),
            pltpu.SemaphoreType.DMA((2,)),
            pltpu.SemaphoreType.DMA((BZ // PLANES,)),
        ],
        compiler_params=pltpu.CompilerParams(vmem_limit_bytes=16 * 2**20),
        cost_estimate=pl.CostEstimate(
            flops=800_000_000, bytes_accessed=9_000_000, transcendentals=0
        ),
        name="finish",
    )(field, change, potential, full(homogeneous))


def solution(mesh):
    return jax.shard_map(
        functools.partial(shards, mesh.shape["py"], mesh.shape["pz"]),
        mesh=mesh,
        in_specs=(P(None, "pz", "py", None), P("pz", "py", None)),
        out_specs=P(None, "pz", "py", None),
        check_vma=False,
    )
```

```python
import functools

import jax
import jax.numpy as jnp
import numpy as np
from jax import lax
from jax.experimental import pallas as pl
from jax.experimental.pallas import tpu as pltpu
from jax.sharding import PartitionSpec as P

time_step = 0.005
rotation = 0.9
coupling = 100.0
grid_spacing = 0.05

NX = 512
BY = 64
BZ = 16
QX = 128
GROUPS = BY // 8
TILES_Z = GROUPS * 4
TILES_Y = 8
ROWS = 2 * BZ * 8
CARRY = 32

MESH = pl.DeviceIdType.MESH
f32 = jnp.float32
bf16 = jnp.bfloat16


def line_roots(beta):
    beta = np.asarray(beta, np.float64)
    half = (beta - 1j) / 2
    spread = np.sqrt((1 + 1j) ** 2 - (beta - 1j) * (-beta - 1j))
    first = (-(1 + 1j) + spread) / (beta - 1j)
    second = (-(1 + 1j) - spread) / (beta - 1j)
    swap = np.abs(first) > np.abs(second)
    inner = np.where(swap, second, first)
    outer = np.where(swap, first, second)
    return inner, 1 / outer, half * (inner - outer)


def real_form(matrix):
    return np.stack(
        [
            np.stack([matrix.real, -matrix.imag], 1),
            np.stack([matrix.imag, matrix.real], 1),
        ],
        0,
    )


def x_tables():
    forward, inverse = [], []
    cells = np.arange(QX)
    for residue in range(4):
        modes = 4 * np.arange(QX) + residue
        angles = 2 * np.pi * ((cells[:, None] * modes[None, :]) % NX) / NX
        cosines, sines = np.cos(angles), np.sin(angles)
        forward.append(np.block([[cosines, -sines], [sines, cosines]]))
        inverse.append(np.block([[cosines.T, sines.T], [-sines.T, cosines.T]]) / NX)
    modes = 4 * np.arange(QX)[None, :] + np.arange(4)[:, None]
    theta = 2 * np.pi * modes / NX
    trig = np.stack([1 - np.cos(theta), np.sin(theta)], 1).reshape(8, QX)
    return np.stack(forward), np.stack(inverse), trig


def z_tables():
    lam, _, scale = line_roots(0.0)
    lam, scale = complex(lam), complex(scale)
    cells = np.arange(BZ)
    local = (2 / scale) * lam ** np.abs(cells[:, None] - cells[None, :]) - np.eye(BZ)
    carry = (2 / scale) * np.stack([lam ** (cells + 1), lam ** (BZ - cells)], 1)
    states = np.stack([lam ** (BZ - 1 - cells), lam**cells], 0)
    eye = np.eye(8)
    apply_field = np.einsum("azbw,ij->aizbwj", real_form(local), eye).reshape(ROWS, ROWS)
    state_rows = np.einsum("asbz,ij->saibzj", real_form(states), eye).reshape(CARRY, ROWS)
    turn = np.zeros((4, BZ, 8, 3, 4, 8))
    fields, carries = real_form(np.eye(BZ).astype(complex)), real_form(carry)
    for end in range(2):
        for out in range(2):
            for part in range(2):
                row, column = 2 * end + out, 2 * end + part
                for half in range(2):
                    turn[:, :, row, half, column, :] = fields[
                        out, :, part, 8 * half : 8 * half + 8
                    ]
                for quarter in range(4):
                    lines = slice(2 * quarter, 2 * quarter + 2)
                    turn[quarter, :, row, 2, column, lines] = carries[out, :, part, :]
    turn = turn.reshape(4, BZ * 8, 3 * CARRY)
    return np.concatenate([apply_field, state_rows], 0), turn, carry, lam**BZ


def y_tables(blocks):
    cells = np.arange(BY)
    angles = 2 * np.pi * ((cells[:, None] * cells[None, :]) % BY) / BY
    modes = np.exp(-1j * angles)
    forward = real_form(modes).reshape(2 * BY, 2 * BY)
    inverse = real_form(np.conj(modes) / BY).reshape(2 * BY, 2 * BY)
    beta = -0.5 * time_step * rotation * (np.arange(NX) - NX // 2)
    theta = 2 * np.pi * cells / BY
    rate = (1 - np.cos(theta))[:, None] + np.sin(theta)[:, None] * beta[None, :]
    factor = (1 - 1j * rate) / (1 + 1j * rate)
    lam1, lam2, scale = line_roots(beta)
    whole1, whole2 = lam1**BY, lam2**BY
    rows = [
        whole1,
        whole2,
        1 / (1 - whole1),
        1 / (1 - whole2),
        1 / (1 - whole1**blocks),
        1 / (1 - whole2**blocks),
        2 * lam1 / scale,
        2 * lam2 / scale,
    ]
    apart = 1 - lam1 * lam2
    steps = [lam1, lam2, lam1 / apart, 2 * apart / scale]
    table = np.stack([part for row in rows for part in (row.real, row.imag)])
    down, up = np.arange(BY)[:, None], BY - 1 - np.arange(BY)[:, None]
    states = [lam1**up, lam2**down]
    homogeneous = [lam1**down, lam2**up]
    add = np.zeros((4, 4, 8, 4, 2, 8))
    for quarter in range(4):
        for plane in range(2):
            for part in range(4):
                add[quarter, part, 2 * quarter + plane, part, plane, :] = 1
    add = add.reshape(4, CARRY, 64)
    table = table.reshape(len(table), 4, QX)
    packed = np.repeat(table, 2, axis=1)
    table = table.transpose(1, 0, 2)

    def parts(values):
        return np.stack([part for value in values for part in (value.real, value.imag)])

    return (
        forward,
        inverse,
        parts([factor]),
        parts(states),
        parts(homogeneous),
        parts(steps),
        add,
        table,
        packed,
    )


def kick(real_part, imag_part, potential):
    turn = -0.5 * time_step / (2 * np.pi)
    density = real_part * real_part + imag_part * imag_part
    turns = potential * turn + density * (turn * coupling)
    rest = turns - jnp.round(turns)
    square = rest * rest
    sine = rest * (
        4.4428679 + square * (-7.30744342 + square * (3.59478806 + square * -0.78437396))
    )
    cosine = 1.4142135 + square * (
        -6.97885099 + square * (5.73946123 + square * (-1.88356328 + square * 0.31069871))
    )
    whole_cos = 1.0 - sine * sine
    whole_sin = sine * cosine
    return (
        real_part * whole_cos - imag_part * whole_sin,
        real_part * whole_sin + imag_part * whole_cos,
    )


def cmul(a, b):
    return a[0] * b[0] - a[1] * b[1], a[0] * b[1] + a[1] * b[0]


def cadd(a, b):
    return a[0] + b[0], a[1] + b[1]


def csub(a, b):
    return a[0] - b[0], a[1] - b[1]


def split_modes(real_part, imag_part):
    quarter = [
        (real_part[:, QX * p : QX * (p + 1)], imag_part[:, QX * p : QX * (p + 1)])
        for p in range(4)
    ]
    t0, t1 = cadd(quarter[0], quarter[2]), csub(quarter[0], quarter[2])
    t2, t3 = cadd(quarter[1], quarter[3]), csub(quarter[1], quarter[3])
    return [
        cadd(t0, t2),
        (t1[0] + t3[1], t1[1] - t3[0]),
        csub(t0, t2),
        (t1[0] - t3[1], t1[1] + t3[0]),
    ]


def join_modes(back):
    t0, t1 = cadd(back[0], back[2]), csub(back[0], back[2])
    t2, t3 = cadd(back[1], back[3]), csub(back[1], back[3])
    return [
        cadd(t0, t2),
        (t1[0] - t3[1], t1[1] + t3[0]),
        csub(t0, t2),
        (t1[0] + t3[1], t1[1] - t3[0]),
    ]


def x_sweep(count, load, factors, store, left, cells, forward_ref, inverse_ref):
    rows = 16 * count
    for n in range(count):
        mixed = split_modes(*load(n))
        for residue in range(4):
            left[residue, 16 * n : 16 * n + 16, :] = jnp.concatenate(mixed[residue], axis=1)
    for residue in range(4):
        modes = jnp.dot(left[residue, 0:rows, :], forward_ref[residue], preferred_element_type=f32)
        for n in range(count):
            some = modes[16 * n : 16 * n + 16]
            scaled = cmul((some[:, :QX], some[:, QX:]), factors(n)[residue])
            left[residue, 16 * n : 16 * n + 16, :] = jnp.concatenate(scaled, axis=1).astype(bf16)
    for residue in range(4):
        cells[residue, 0:rows, :] = jnp.dot(
            left[residue, 0:rows, :], inverse_ref[residue], preferred_element_type=f32
        )
    for n in range(0, count, 2):
        done = []
        for at in range(2):
            lines = slice(16 * (n + at), 16 * (n + at) + 16)
            some = [cells[residue, lines, :] for residue in range(4)]
            out = join_modes([(one[:, :QX], one[:, QX:]) for one in some])
            done.append([jnp.concatenate([one[part] for one in out], axis=1) for part in range(2)])
        store(n, done)


def main_kernel(
    count_py,
    count_pz,
    z_step,
    z_profile,
    wave_hbm,
    pot_hbm,
    xf_hbm,
    xi_hbm,
    weight_hbm,
    factor_hbm,
    trig_ref,
    z_ref,
    yf_ref,
    yi_ref,
    add_ref,
    turn_ref,
    ytab_ref,
    step_ref,
    packed_ref,
    field_hbm,
    change_hbm,
    wave,
    pot,
    xf,
    xi,
    weight,
    factor,
    fresh_a,
    fresh_b,
    gains,
    grid,
    swept,
    solved,
    planes,
    result,
    left_buf,
    cells_buf,
    sums,
    z_states,
    z_partner,
    z_send,
    z_recv,
    z_back,
    z_chip,
    z_give,
    z_carry,
    y_send,
    y_recv,
    y_back,
    y_carry,
    c_send,
    c_recv,
    change,
    in_sem,
    tab_sem,
    out_sem,
    pair_sems,
    z_sems,
    z_back_sems,
    y_sems,
    c_sems,
):
    me_y = lax.axis_index("py")
    me_z = lax.axis_index("pz")
    core = lax.rem(me_z, 2)
    chip = me_z // 2
    partner = me_z + 1 - 2 * core
    chips = count_pz // 2
    half_z = TILES_Z // 2
    tiles_z = half_z // chips
    mine = core * half_z
    theirs = half_z - mine

    def load(group):
        rows = pl.ds(pl.multiple_of(group * 8, 8), 8)
        return (
            pltpu.make_async_copy(wave_hbm.at[:, :, rows, :], wave.at[group], in_sem.at[0, group]),
            pltpu.make_async_copy(pot_hbm.at[:, rows, :], pot.at[group], in_sem.at[1, group]),
        )

    for group in range(GROUPS):
        for copy in load(group):
            copy.start()
    table_copies = (
        pltpu.make_async_copy(xf_hbm, xf, tab_sem.at[0]),
        pltpu.make_async_copy(xi_hbm, xi, tab_sem.at[1]),
        pltpu.make_async_copy(weight_hbm, weight, tab_sem.at[2]),
        pltpu.make_async_copy(factor_hbm, factor, tab_sem.at[3]),
    )
    for copy in table_copies:
        copy.start()

    barrier = pltpu.get_barrier_semaphore()

    def twin(other):
        return {"pz": other * 2 + core}

    pl.semaphore_signal(barrier, inc=1, device_id={"pz": partner}, device_id_type=MESH)

    @pl.loop(1, chips)
    def _(step):
        pl.semaphore_signal(
            barrier, inc=1, device_id=twin(lax.rem(chip + step, chips)), device_id_type=MESH
        )

    @pl.loop(1, count_py)
    def _(step):
        pl.semaphore_signal(
            barrier, inc=1, device_id={"py": lax.rem(me_y + step, count_py)}, device_id_type=MESH
        )

    for group in range(GROUPS):
        cell = lax.broadcasted_iota(jnp.int32, (8, QX), 0) + (
            me_y * BY + group * 8 - count_py * BY // 2
        )
        beta = cell.astype(f32) * (0.5 * time_step * rotation)
        for residue in range(4):
            rate = trig_ref[2 * residue : 2 * residue + 1] + beta * trig_ref[
                2 * residue + 1 : 2 * residue + 2
            ]
            scale = 1.0 / (1.0 + rate * rate)
            lines = slice(8 * group, 8 * group + 8)
            gains[2 * residue, lines, :] = (1.0 - rate * rate) * scale
            gains[2 * residue + 1, lines, :] = -2.0 * rate * scale

    def kick_group(group, fresh):
        for some in range(BZ // 2):
            rows = slice(2 * some, 2 * some + 2)
            new = kick(wave[group, 0, rows], wave[group, 1, rows], pot[group, rows])
            for part in range(2):
                start = ROWS // 2 * part + 16 * some
                fresh[start : start + 16, :] = new[part].reshape(16, NX).astype(bf16)

    def solve_group(group, fresh):
        for side in range(2):
            lanes = slice(side * NX // 2, (side + 1) * NX // 2)
            rows = jnp.dot(z_ref[...], fresh[:, lanes], preferred_element_type=f32)
            for start in range(0, ROWS, 16):
                grid[group, start : start + 16, lanes] = rows[start : start + 16].astype(bf16)
            states = rows[ROWS:].astype(bf16)
            for quarter in range(2):
                z_states[group * 4 + 2 * side + quarter] = states[
                    :, QX * quarter : QX * (quarter + 1)
                ].reshape(2, 16, QX)

    def pair_out(step):
        return pltpu.make_async_remote_copy(
            src_ref=z_states.at[pl.ds(theirs + 4 * step, 4)],
            dst_ref=z_partner.at[pl.ds(4 * step, 4)],
            send_sem=pair_sems.at[0, step],
            recv_sem=pair_sems.at[1, step],
            device_id={"pz": partner},
            device_id_type=MESH,
        )

    def pair_back():
        return pltpu.make_async_remote_copy(
            src_ref=z_give,
            dst_ref=z_carry.at[pl.ds(mine, half_z)],
            send_sem=pair_sems.at[0, 4],
            recv_sem=pair_sems.at[1, 4],
            device_id={"pz": partner},
            device_id_type=MESH,
        )

    def pair_returned():
        return pltpu.make_async_remote_copy(
            src_ref=z_give,
            dst_ref=z_carry.at[pl.ds(theirs, half_z)],
            send_sem=pair_sems.at[0, 4],
            recv_sem=pair_sems.at[1, 4],
            device_id={"pz": partner},
            device_id_type=MESH,
        )

    def z_out(tile):
        return pltpu.make_async_remote_copy(
            src_ref=z_send.at[tile],
            dst_ref=z_recv.at[chip, lax.rem(tile, tiles_z)],
            send_sem=z_sems.at[0, tile],
            recv_sem=z_sems.at[1, chip * tiles_z + lax.rem(tile, tiles_z)],
            device_id=twin(tile // tiles_z),
            device_id_type=MESH,
        )

    def z_in(step, tile):
        peer = lax.rem(chip + step, chips)
        return pltpu.make_async_remote_copy(
            src_ref=z_send.at[tile],
            dst_ref=z_recv.at[peer, tile],
            send_sem=z_sems.at[0, tile],
            recv_sem=z_sems.at[1, peer * tiles_z + tile],
            device_id=twin(peer),
            device_id_type=MESH,
        )

    def z_return(step):
        peer = lax.rem(chip + step, chips)
        return pltpu.make_async_remote_copy(
            src_ref=z_back.at[peer],
            dst_ref=z_chip.at[pl.ds(chip * tiles_z, tiles_z)],
            send_sem=z_back_sems.at[0, peer],
            recv_sem=z_back_sems.at[1, chip],
            device_id=twin(peer),
            device_id_type=MESH,
        )

    def z_returned(step):
        peer = lax.rem(chip + step, chips)
        return pltpu.make_async_remote_copy(
            src_ref=z_back.at[chip],
            dst_ref=z_chip.at[pl.ds(peer * tiles_z, tiles_z)],
            send_sem=z_back_sems.at[0, chip],
            recv_sem=z_back_sems.at[1, peer],
            device_id=twin(peer),
            device_id_type=MESH,
        )

    lead = core == 0
    block_step = (z_step.real, z_step.imag)
    chip_step = z_step * z_step

    def parts(array):
        array = array.astype(f32)
        return array[0:8], array[8:16]

    def choose(first, second):
        return jnp.where(lead, first[0], second[0]), jnp.where(lead, first[1], second[1])

    def joined(value):
        return jnp.concatenate(value, axis=0).astype(bf16)

    def order(count):
        if count < GROUPS // 2:
            return theirs // 4 + count
        return mine // 4 + lax.rem(count + chip // 4, GROUPS // 2)

    def merge(step):
        pair_out(step).wait_recv()
        for at in range(4):
            tile = step * 4 + at
            own = [parts(z_states[mine + tile, side]) for side in range(2)]
            other = [parts(z_partner[tile, side]) for side in range(2)]
            left = cadd(choose(other[0], own[0]), cmul(choose(own[0], other[0]), block_step))
            right = cadd(choose(own[1], other[1]), cmul(choose(other[1], own[1]), block_step))
            z_send[tile, 0] = joined(left)
            z_send[tile, 1] = joined(right)
        for at in range(4):
            tile = step * 4 + at
            owner = tile // tiles_z

            @pl.when(owner != chip)
            def _():
                z_out(tile).start()

            @pl.when(owner == chip)
            def _():
                z_recv[chip, lax.rem(tile, tiles_z)] = z_send[tile]

    def kicked(count, fresh):
        for copy in load(order(count)):
            copy.wait()
        kick_group(order(count), fresh)

    fresh = (fresh_a, fresh_b)
    kicked(0, fresh[0])
    for count in range(GROUPS):
        if count + 1 < GROUPS:
            for copy in load(order(count + 1)):
                copy.wait()
        solve_group(order(count), fresh[count % 2])
        if count + 1 < GROUPS:
            kick_group(order(count + 1), fresh[(count + 1) % 2])
        if count == 0:
            pl.semaphore_wait(barrier, chips + count_py - 1)
        if count < GROUPS // 2:
            pair_out(count).start()
        else:
            merge(order(count) - mine // 4)

    for copy in table_copies:
        copy.wait()

    def sweep_field():
        def fetch(n):
            group, row = n // 8, n % 8 * BZ
            return tuple(
                grid[group, start : start + BZ, :] for start in (row, row + ROWS // 2)
            )

        def gain(n):
            line = slice(n, n + 1)
            return [
                (gains[2 * residue, line, :], gains[2 * residue + 1, line, :])
                for residue in range(4)
            ]

        def put(n, done):
            for at in range(2):
                start = (n + at) * BZ
                for part in range(2):
                    swept[part, start : start + BZ, :] = done[at][part].astype(bf16)

        x_sweep(BY, fetch, gain, put, left_buf, cells_buf, xf, xi)

    steps_y = [(step_ref[2 * n : 2 * n + 1], step_ref[2 * n + 1 : 2 * n + 2]) for n in range(4)]
    forward_step, backward_step, turn_step, whole_gain = steps_y

    def y_rows(cell):
        return pl.ds(pl.multiple_of(cell * BZ, BZ), BZ)

    def save(rows, value):
        for part in range(2):
            for quarter in range(4):
                solved[part, quarter, rows, :] = value[part][
                    :, QX * quarter : QX * (quarter + 1)
                ]

    def y_forward():
        def advance(cell, totals):
            total, other = totals
            rows = y_rows(cell)
            value = tuple(swept[part, rows, :].astype(f32) for part in range(2))
            total = cadd(value, cmul(total, forward_step))
            save(rows, total)
            share = tuple(weight[2 + part, pl.ds(cell, 1), :] for part in range(2))
            return total, cadd(other, cmul(value, share))

        zero = jnp.zeros((BZ, NX), f32)
        return lax.fori_loop(0, BY, advance, ((zero, zero), (zero, zero)), unroll=4)

    def y_backward(first, last, total):
        def advance(count, total):
            rows = y_rows(BY - 1 - count)
            value = tuple(
                jnp.concatenate([solved[part, quarter, rows, :] for quarter in range(4)], axis=1)
                for part in range(2)
            )
            total = cadd(value, cmul(total, backward_step))
            out = cmul(total, whole_gain)
            save(rows, [out[part] - swept[part, rows, :].astype(f32) for part in range(2)])
            return total

        return lax.fori_loop(first, last, advance, total, unroll=4)

    def y_states(count):
        @pl.loop(0, count)
        def _(at):
            for quarter in range(4):
                lanes = slice(QX * quarter, QX * (quarter + 1))
                total = [[0.0, 0.0], [0.0, 0.0]]
                for start in range(0, BY, 16):
                    rows = slice(start, start + 16)
                    value = [planes[part, at, rows, lanes].astype(f32) for part in range(2)]
                    for side in range(2):
                        some = cmul(
                            value, (weight[2 * side, rows, lanes], weight[2 * side + 1, rows, lanes])
                        )
                        for part in range(2):
                            total[side][part] += some[part][0:8] + some[part][8:16]
                for side in range(2):
                    for part in range(2):
                        row = pl.multiple_of((side * 2 + part) * 16 + at * 8, 8)
                        sums[pl.ds(row, 8), lanes] = total[side][part]

        rows = 0.0
        for quarter in range(4):
            some = sums[:, QX * quarter : QX * (quarter + 1)].astype(bf16)
            rows += jnp.dot(add_ref[quarter], some, preferred_element_type=f32)
        return rows.astype(bf16)

    def y_periodic(plane):
        for side in range(2):
            lanes = slice(side * NX // 2, (side + 1) * NX // 2)
            block = jnp.concatenate([planes[part, plane, :, lanes] for part in range(2)], axis=0)
            modes = jnp.dot(yf_ref[...], block, preferred_element_type=f32)
            scaled = [
                cmul(
                    (modes[some : some + 32], modes[BY + some : BY + some + 32]),
                    (factor[0, some : some + 32, lanes], factor[1, some : some + 32, lanes]),
                )
                for some in range(0, BY, 32)
            ]
            block = jnp.concatenate(
                [one[part].astype(bf16) for part in range(2) for one in scaled], axis=0
            )
            cells = jnp.dot(yi_ref[...], block, preferred_element_type=f32).astype(bf16)
            for part in range(2):
                planes[part, plane, :, lanes] = cells[part * BY : (part + 1) * BY]

    class Exchange:
        def __init__(self, send, recv, back, carry, sems, tiles):
            self.send, self.recv, self.back, self.carry = send, recv, back, carry
            self.sems, self.tiles = sems, tiles

        def mine(self):
            return pl.ds(me_y * self.tiles, self.tiles)

        def out(self, peer):
            return pltpu.make_async_remote_copy(
                src_ref=self.send.at[pl.ds(peer * self.tiles, self.tiles)],
                dst_ref=self.recv.at[me_y],
                send_sem=self.sems.at[0, peer],
                recv_sem=self.sems.at[1, me_y],
                device_id={"py": peer},
                device_id_type=MESH,
            )

        def arrived(self, peer):
            return pltpu.make_async_remote_copy(
                src_ref=self.send.at[self.mine()],
                dst_ref=self.recv.at[peer],
                send_sem=self.sems.at[0, me_y],
                recv_sem=self.sems.at[1, peer],
                device_id={"py": peer},
                device_id_type=MESH,
            )

        def give(self, peer):
            return pltpu.make_async_remote_copy(
                src_ref=self.back.at[peer],
                dst_ref=self.carry.at[self.mine()],
                send_sem=self.sems.at[2, peer],
                recv_sem=self.sems.at[3, me_y],
                device_id={"py": peer},
                device_id_type=MESH,
            )

        def given(self, peer):
            return pltpu.make_async_remote_copy(
                src_ref=self.back.at[me_y],
                dst_ref=self.carry.at[pl.ds(peer * self.tiles, self.tiles)],
                send_sem=self.sems.at[2, me_y],
                recv_sem=self.sems.at[3, peer],
                device_id={"py": peer},
                device_id_type=MESH,
            )

        def post(self):
            @pl.loop(1, count_py)
            def _(step):
                self.out(lax.rem(me_y + step, count_py)).start()

        def answer(self):
            self.recv[me_y] = self.send[self.mine()]

            @pl.loop(1, count_py)
            def _(step):
                self.arrived(lax.rem(me_y + step, count_py)).wait_recv()

            for tile in range(self.tiles):
                solve_tile(self.recv, self.back, tile, lax.rem(me_y * self.tiles + tile, 4))

            @pl.loop(1, count_py)
            def _(step):
                self.give(lax.rem(me_y + step, count_py)).start()

            self.carry[self.mine()] = self.back[me_y]

        def receive(self):
            @pl.loop(1, count_py)
            def _(step):
                self.given(lax.rem(me_y + step, count_py)).wait_recv()

        def close(self):
            @pl.loop(1, count_py)
            def _(step):
                peer = lax.rem(me_y + step, count_py)
                self.out(peer).wait_send()
                self.give(peer).wait_send()

        def rows(self, tiles):
            return [self.carry[tile].reshape(CARRY, QX) for tile in tiles]

    def solve_tile(recv, back, tile, quarter):
        table = ytab_ref[quarter]
        value = [(table[2 * n : 2 * n + 1], table[2 * n + 1 : 2 * n + 2]) for n in range(8)]
        whole1, whole2, _, _, wrap1, wrap2, out1, out2 = value
        left_state = [parts(recv[block, tile, 0]) for block in range(count_py)]
        right_state = [parts(recv[block, tile, 1]) for block in range(count_py)]
        left, right = left_state[0], right_state[count_py - 1]
        for block in range(1, count_py):
            left = cadd(left_state[block], cmul(left, whole1))
            right = cadd(right_state[count_py - 1 - block], cmul(right, whole2))
        left, right = cmul(left, wrap1), cmul(right, wrap2)
        for block in range(count_py):
            other = count_py - 1 - block
            back[block, tile, 0] = joined(cmul(left, out1))
            back[other, tile, 1] = joined(cmul(right, out2))
            left = cadd(left_state[block], cmul(left, whole1))
            right = cadd(right_state[other], cmul(right, whole2))

    planes_y = Exchange(y_send, y_recv, y_back, y_carry, y_sems, TILES_Y // count_py)
    def carry_out(step):
        return pltpu.make_async_remote_copy(
            src_ref=c_send,
            dst_ref=c_recv.at[me_y],
            send_sem=c_sems.at[0, lax.rem(me_y + step, count_py)],
            recv_sem=c_sems.at[1, me_y],
            device_id={"py": lax.rem(me_y + step, count_py)},
            device_id_type=MESH,
        )

    def carry_in(step):
        peer = lax.rem(me_y + step, count_py)
        return pltpu.make_async_remote_copy(
            src_ref=c_send,
            dst_ref=c_recv.at[peer],
            send_sem=c_sems.at[0, me_y],
            recv_sem=c_sems.at[1, peer],
            device_id={"py": peer},
            device_id_type=MESH,
        )

    def carry_solve():
        value = [(packed_ref[2 * n], packed_ref[2 * n + 1]) for n in range(8)]
        whole1, whole2, own1, own2, wrap1, wrap2, out1, out2 = value
        own = [parts(c_send[side]) for side in range(2)]
        left, right = own
        for step in range(1, count_py):
            left = cadd(parts(c_recv[lax.rem(me_y + step, count_py), 0]), cmul(left, whole1))
            back = lax.rem(me_y + count_py - step, count_py)
            right = cadd(parts(c_recv[back, 1]), cmul(right, whole2))
        left = csub(cmul(left, wrap1), cmul(own[0], own1))
        right = csub(cmul(right, wrap2), cmul(own[1], own2))
        return jnp.concatenate([joined(cmul(left, out1)), joined(cmul(right, out2))], axis=0)

    def post_planes(states):
        for half in range(2):
            lines = slice(8 * half, 8 * half + 8)
            for quarter in range(4):
                lanes = slice(QX * quarter, QX * (quarter + 1))
                for side in range(2):
                    y_send[half * 4 + quarter, side] = joined(
                        [states[side][part][lines, lanes] for part in range(2)]
                    )
        planes_y.post()

    sweep_field()

    @pl.loop(1, chips)
    def _(step):
        for tile in range(tiles_z):
            z_in(step, tile).wait_recv()

    for tile in range(tiles_z):

        def state(block, side):
            return parts(z_recv[block, tile, side])

        def advance(total, value):
            return cadd(cmul(total, (chip_step.real, chip_step.imag)), value)

        def gather(step, carry):
            left, right = carry
            return (
                advance(left, state(step, 0)),
                advance(right, state(chips - 1 - step, 1)),
            )

        zero = (jnp.zeros((8, QX), f32), jnp.zeros((8, QX), f32))
        left, right = lax.fori_loop(0, chips, gather, (zero, zero), unroll=8)
        wrap = 1 / (1 - chip_step**chips)
        left = cmul(left, (wrap.real, wrap.imag))
        right = cmul(right, (wrap.real, wrap.imag))

        def hand_out(step, carry):
            left, right = carry
            last = chips - 1 - step
            z_back[step, tile, 0] = joined(left)
            z_back[last, tile, 1] = joined(right)
            return advance(left, state(step, 0)), advance(right, state(last, 1))

        lax.fori_loop(0, chips, hand_out, (left, right), unroll=8)

    @pl.loop(1, chips)
    def _(step):
        z_return(step).start()

    z_chip[pl.ds(chip * tiles_z, tiles_z)] = z_back[chip]

    forward_state, backward_state = y_forward()
    post_planes((forward_state, backward_state))
    back_total = y_backward(0, BY // 2, cmul(forward_state, turn_step))

    @pl.loop(1, chips)
    def _(step):
        z_returned(step).wait_recv()

    def split_carry(tile, _):
        own = [parts(z_states[mine + tile, side]) for side in range(2)]
        other = [parts(z_partner[tile, side]) for side in range(2)]
        whole = [parts(z_chip[tile, side]) for side in range(2)]
        inner_left = cadd(choose(own[0], other[0]), cmul(whole[0], block_step))
        inner_right = cadd(choose(other[1], own[1]), cmul(whole[1], block_step))
        z_give[tile, 0] = joined(choose(inner_left, whole[0]))
        z_give[tile, 1] = joined(choose(whole[1], inner_right))
        z_carry[mine + tile, 0] = joined(choose(whole[0], inner_left))
        z_carry[mine + tile, 1] = joined(choose(inner_right, whole[1]))
        return 0

    lax.fori_loop(0, half_z, split_carry, 0, unroll=4)
    pair_back().start()

    y_backward(BY // 2, BY, back_total)
    pair_returned().wait_recv()

    def fetch(n):
        sides = [
            jnp.concatenate([z_carry[n * 4 + quarter, side] for quarter in range(4)], axis=1)
            for side in range(2)
        ]
        sides = [side.astype(f32) for side in sides]
        return tuple(
            jnp.concatenate([side[8 * part : 8 * part + 8] for side in sides], axis=0).astype(bf16)
            for part in range(2)
        )

    def put(n, done):
        for side in range(2):
            lines = slice(8 * side, 8 * side + 8)
            for part in range(2):
                planes[part, side, 8 * n : 8 * n + 16, :] = jnp.concatenate(
                    [done[at][part][lines] for at in range(2)], axis=0
                ).astype(bf16)

    def gain(n):
        lines = slice(8 * n, 8 * n + 8)
        return [
            tuple(
                jnp.concatenate([gains[2 * residue + part, lines, :]] * 2, axis=0)
                for part in range(2)
            )
            for residue in range(4)
        ]

    x_sweep(GROUPS, fetch, gain, put, left_buf, cells_buf, xf, xi)
    c_send[...] = y_states(2).reshape(2, 16, QX)

    @pl.loop(1, count_py)
    def _(step):
        carry_out(step).start()

    planes_y.answer()
    y_periodic(0)
    y_periodic(1)

    def store(pair):
        rows = pl.ds(pl.multiple_of(pair * 16, 16), 16)
        return pltpu.make_async_copy(
            result.at[:, :, rows, :], field_hbm.at[:, :, rows, :], out_sem.at[pair]
        )

    @pl.loop(0, BY // 16)
    def _(pair):
        rows = pl.ds(pl.multiple_of(pair * 16, 16), 16)
        for quarter in range(4):
            lanes = slice(QX * quarter, QX * (quarter + 1))
            left, right = [
                tuple(planes[part, one, rows, lanes] for part in range(2)) for one in range(2)
            ]
            for plane in range(BZ):
                first, second = (complex(one) for one in z_profile[plane])
                lines = pl.ds(pair * 16 * BZ + plane, 16, stride=BZ)
                value = tuple(solved[part, quarter, lines, :].astype(bf16) for part in range(2))
                value = cadd(value, cmul(left, (first.real, first.imag)))
                value = cadd(value, cmul(right, (second.real, second.imag)))
                for part in range(2):
                    result[part, plane, rows, lanes] = value[part]
        store(pair).start()

    @pl.loop(0, half_z)
    def _(tile):
        @pl.when(tile // tiles_z != chip)
        def _():
            z_out(tile).wait_send()

    @pl.loop(1, chips)
    def _(step):
        z_return(step).wait_send()

    @pl.loop(0, GROUPS // 2)
    def _(step):
        pair_out(step).wait_send()

    pair_back().wait_send()

    @pl.loop(1, count_py)
    def _(step):
        carry_in(step).wait_recv()

    carried = carry_solve()
    planes_y.receive()
    for quarter in range(4):
        rows = planes_y.rows((quarter, 4 + quarter)) + [carried]
        change[:, :, QX * quarter : QX * (quarter + 1)] = jnp.dot(
            turn_ref[quarter], jnp.concatenate(rows, axis=0), preferred_element_type=f32
        ).reshape(BZ, 8, QX)
    last = pltpu.make_async_copy(change, change_hbm, out_sem.at[GROUPS // 2])
    last.start()

    planes_y.close()

    @pl.loop(1, count_py)
    def _(step):
        carry_out(step).wait_send()


    @pl.loop(0, GROUPS // 2)
    def _(pair):
        store(pair).wait()

    last.wait()


PLANES = 2


def finish_kernel(
    field_hbm,
    change_hbm,
    pot_hbm,
    table_hbm,
    out_hbm,
    field,
    change,
    pot,
    table,
    out,
    in_sem,
    tab_sem,
    out_sem,
):
    steps = BZ // PLANES

    def load(step):
        planes = pl.ds(step * PLANES, PLANES)
        return (
            pltpu.make_async_copy(field_hbm.at[:, planes], field.at[:, planes], in_sem.at[0, step]),
            pltpu.make_async_copy(pot_hbm.at[planes], pot.at[planes], in_sem.at[1, step]),
        )

    def save(step):
        planes = pl.ds(step * PLANES, PLANES)
        return pltpu.make_async_copy(out.at[:, planes], out_hbm.at[:, planes], out_sem.at[step])

    tables = (
        pltpu.make_async_copy(change_hbm, change, tab_sem.at[0]),
        pltpu.make_async_copy(table_hbm, table, tab_sem.at[1]),
    )
    for copy in tables:
        copy.start()
    for step in range(steps):
        for copy in load(step):
            copy.start()
    for copy in tables:
        copy.wait()

    def finish(at, lanes):
        ends = [change[at, row : row + 1, lanes].astype(bf16) for row in range(4)]
        for start in range(0, BY, 16):
            rows = slice(start, start + 16)
            value = tuple(field[part, at, rows, lanes] for part in range(2))
            for side in range(2):
                profile = (table[2 * side, rows, lanes], table[2 * side + 1, rows, lanes])
                value = cadd(value, cmul(profile, (ends[2 * side], ends[2 * side + 1])))
            new = kick(value[0].astype(f32), value[1].astype(f32), pot[at, rows, lanes])
            for part in range(2):
                out[part, at, rows, lanes] = new[part]

    @pl.loop(0, steps)
    def _(step):
        for copy in load(step):
            copy.wait()
        for one in range(PLANES):
            for side in range(2):
                finish(step * PLANES + one, slice(side * NX // 2, (side + 1) * NX // 2))
        save(step).start()

    @pl.loop(0, steps)
    def _(step):
        save(step).wait()


def shards(count_py, count_pz, wavefunction, potential):
    forward_x, inverse_x, trig = x_tables()
    z_rows, turn, z_profile, z_step = z_tables()
    forward_y, inverse_y, factor, weight, homogeneous, steps_y, add, y_table, packed = y_tables(count_py)

    def low(array):
        return jnp.asarray(array.astype(np.float32)).astype(bf16)

    def full(array):
        return jnp.asarray(array.astype(np.float32))

    chips = count_pz // 2
    tiles_z = TILES_Z // 2 // chips
    tiles_y = TILES_Y // count_py
    anywhere = pl.BlockSpec(memory_space=pl.ANY)
    inside = pl.BlockSpec(memory_space=pltpu.VMEM)
    field, change = pl.pallas_call(
        functools.partial(main_kernel, count_py, count_pz, z_step, z_profile),
        out_shape=(
            pltpu.VMEM((2, BZ, BY, NX), bf16),
            pltpu.VMEM((BZ, 8, NX), f32),
        ),
        in_specs=[anywhere] * 6 + [inside] * 9,
        out_specs=(anywhere, anywhere),
        scratch_shapes=[
            pltpu.VMEM((GROUPS, 2, BZ, 8, NX), f32),
            pltpu.VMEM((GROUPS, BZ, 8, NX), f32),
            pltpu.VMEM((4, 2 * QX, 2 * QX), bf16),
            pltpu.VMEM((4, 2 * QX, 2 * QX), bf16),
            pltpu.VMEM(weight.shape, f32),
            pltpu.VMEM(factor.shape, f32),
            pltpu.VMEM((ROWS, NX), bf16),
            pltpu.VMEM((ROWS, NX), bf16),
            pltpu.VMEM((8, BY, QX), f32),
            pltpu.VMEM((GROUPS, ROWS, NX), bf16),
            pltpu.VMEM((2, BY * BZ, NX), bf16),
            pltpu.VMEM((2, 4, BY * BZ, QX), f32),
            pltpu.VMEM((2, 2, BY, NX), bf16),
            pltpu.VMEM((2, BZ, BY, NX), bf16),
            pltpu.VMEM((4, BY * BZ, 2 * QX), bf16),
            pltpu.VMEM((4, BY * BZ, 2 * QX), f32),
            pltpu.VMEM((64, NX), f32),
            pltpu.VMEM((TILES_Z, 2, 16, QX), bf16),
            pltpu.VMEM((TILES_Z // 2, 2, 16, QX), bf16),
            pltpu.VMEM((TILES_Z // 2, 2, 16, QX), bf16),
            pltpu.VMEM((chips, tiles_z, 2, 16, QX), bf16),
            pltpu.VMEM((chips, tiles_z, 2, 16, QX), bf16),
            pltpu.VMEM((TILES_Z // 2, 2, 16, QX), bf16),
            pltpu.VMEM((TILES_Z // 2, 2, 16, QX), bf16),
            pltpu.VMEM((TILES_Z, 2, 16, QX), bf16),
            pltpu.VMEM((TILES_Y, 2, 16, QX), bf16),
            pltpu.VMEM((count_py, tiles_y, 2, 16, QX), bf16),
            pltpu.VMEM((count_py, tiles_y, 2, 16, QX), bf16),
            pltpu.VMEM((TILES_Y, 2, 16, QX), bf16),
            pltpu.VMEM((2, 16, QX), bf16),
            pltpu.VMEM((count_py, 2, 16, QX), bf16),
            pltpu.VMEM((BZ, 8, NX), f32),
            pltpu.SemaphoreType.DMA((2, GROUPS)),
            pltpu.SemaphoreType.DMA((4,)),
            pltpu.SemaphoreType.DMA((GROUPS // 2 + 1,)),
            pltpu.SemaphoreType.DMA((2, 5)),
            pltpu.SemaphoreType.DMA((2, TILES_Z // 2)),
            pltpu.SemaphoreType.DMA((2, chips)),
            pltpu.SemaphoreType.DMA((4, count_py)),
            pltpu.SemaphoreType.DMA((2, count_py)),
        ],
        compiler_params=pltpu.CompilerParams(
            collective_id=0, has_side_effects=True, vmem_limit_bytes=57 * 2**20
        ),
        cost_estimate=pl.CostEstimate(
            flops=3_000_000_000, bytes_accessed=10_000_000, transcendentals=0
        ),
        name="sweeps",
    )(
        wavefunction,
        potential,
        low(forward_x),
        low(inverse_x),
        full(weight),
        full(factor),
        full(trig),
        low(z_rows),
        low(forward_y),
        low(inverse_y),
        low(add),
        low(turn),
        full(y_table),
        full(steps_y),
        full(packed),
    )
    return pl.pallas_call(
        finish_kernel,
        out_shape=jax.ShapeDtypeStruct((2, BZ, BY, NX), f32),
        in_specs=[anywhere] * 4,
        out_specs=anywhere,
        scratch_shapes=[
            pltpu.VMEM((2, BZ, BY, NX), bf16),
            pltpu.VMEM((BZ, 8, NX), f32),
            pltpu.VMEM((BZ, BY, NX), f32),
            pltpu.VMEM(homogeneous.shape, bf16),
            pltpu.VMEM((2, BZ, BY, NX), f32),
            pltpu.SemaphoreType.DMA((2, BZ // PLANES)),
            pltpu.SemaphoreType.DMA((2,)),
            pltpu.SemaphoreType.DMA((BZ // PLANES,)),
        ],
        compiler_params=pltpu.CompilerParams(vmem_limit_bytes=16 * 2**20),
        cost_estimate=pl.CostEstimate(
            flops=800_000_000, bytes_accessed=9_000_000, transcendentals=0
        ),
        name="finish",
    )(field, change, potential, low(homogeneous))


def solution(mesh):
    return jax.shard_map(
        functools.partial(shards, mesh.shape["py"], mesh.shape["pz"]),
        mesh=mesh,
        in_specs=(P(None, "pz", "py", None), P("pz", "py", None)),
        out_specs=P(None, "pz", "py", None),
        check_vma=False,
    )
```

```python
import functools

import jax
import jax.numpy as jnp
import numpy as np
from jax import lax
from jax.experimental import pallas as pl
from jax.experimental.pallas import tpu as pltpu
from jax.sharding import PartitionSpec as P

time_step = 0.005
rotation = 0.9
coupling = 100.0
grid_spacing = 0.05

NX = 512
BY = 64
BZ = 16
QX = 128
GROUPS = BY // 8
TILES_Z = GROUPS * 4
TILES_Y = 8
ROWS = 2 * BZ * 8
CARRY = 32

MESH = pl.DeviceIdType.MESH
f32 = jnp.float32
bf16 = jnp.bfloat16


def line_roots(beta):
    beta = np.asarray(beta, np.float64)
    half = (beta - 1j) / 2
    spread = np.sqrt((1 + 1j) ** 2 - (beta - 1j) * (-beta - 1j))
    first = (-(1 + 1j) + spread) / (beta - 1j)
    second = (-(1 + 1j) - spread) / (beta - 1j)
    swap = np.abs(first) > np.abs(second)
    inner = np.where(swap, second, first)
    outer = np.where(swap, first, second)
    return inner, 1 / outer, half * (inner - outer)


def real_form(matrix):
    return np.stack(
        [
            np.stack([matrix.real, -matrix.imag], 1),
            np.stack([matrix.imag, matrix.real], 1),
        ],
        0,
    )


def x_tables():
    forward, inverse = [], []
    cells = np.arange(QX)
    for residue in range(4):
        modes = 4 * np.arange(QX) + residue
        angles = 2 * np.pi * ((cells[:, None] * modes[None, :]) % NX) / NX
        cosines, sines = np.cos(angles), np.sin(angles)
        forward.append(np.block([[cosines, -sines], [sines, cosines]]))
        inverse.append(np.block([[cosines.T, sines.T], [-sines.T, cosines.T]]) / NX)
    modes = 4 * np.arange(QX)[None, :] + np.arange(4)[:, None]
    theta = 2 * np.pi * modes / NX
    trig = np.stack([1 - np.cos(theta), np.sin(theta)], 1).reshape(8, QX)
    return np.stack(forward), np.stack(inverse), trig


def z_tables():
    lam, _, scale = line_roots(0.0)
    lam, scale = complex(lam), complex(scale)
    cells = np.arange(BZ)
    local = (2 / scale) * lam ** np.abs(cells[:, None] - cells[None, :]) - np.eye(BZ)
    carry = (2 / scale) * np.stack([lam ** (cells + 1), lam ** (BZ - cells)], 1)
    states = np.stack([lam ** (BZ - 1 - cells), lam**cells], 0)
    eye = np.eye(8)
    apply_field = np.einsum("azbw,ij->aizbwj", real_form(local), eye).reshape(ROWS, ROWS)
    state_rows = np.einsum("asbz,ij->saibzj", real_form(states), eye).reshape(CARRY, ROWS)
    turn = np.zeros((4, BZ, 8, 3, 4, 8))
    fields, carries = real_form(np.eye(BZ).astype(complex)), real_form(carry)
    for end in range(2):
        for out in range(2):
            for part in range(2):
                row, column = 2 * end + out, 2 * end + part
                for half in range(2):
                    turn[:, :, row, half, column, :] = fields[
                        out, :, part, 8 * half : 8 * half + 8
                    ]
                for quarter in range(4):
                    lines = slice(2 * quarter, 2 * quarter + 2)
                    turn[quarter, :, row, 2, column, lines] = carries[out, :, part, :]
    turn = turn.reshape(4, BZ * 8, 3 * CARRY)
    return np.concatenate([apply_field, state_rows], 0), turn, carry, lam**BZ


def y_tables(blocks):
    cells = np.arange(BY)
    angles = 2 * np.pi * ((cells[:, None] * cells[None, :]) % BY) / BY
    modes = np.exp(-1j * angles)
    forward = real_form(modes).reshape(2 * BY, 2 * BY)
    inverse = real_form(np.conj(modes) / BY).reshape(2 * BY, 2 * BY)
    beta = -0.5 * time_step * rotation * (np.arange(NX) - NX // 2)
    theta = 2 * np.pi * cells / BY
    rate = (1 - np.cos(theta))[:, None] + np.sin(theta)[:, None] * beta[None, :]
    factor = (1 - 1j * rate) / (1 + 1j * rate)
    lam1, lam2, scale = line_roots(beta)
    whole1, whole2 = lam1**BY, lam2**BY
    rows = [
        whole1,
        whole2,
        1 / (1 - whole1),
        1 / (1 - whole2),
        1 / (1 - whole1**blocks),
        1 / (1 - whole2**blocks),
        2 * lam1 / scale,
        2 * lam2 / scale,
    ]
    apart = 1 - lam1 * lam2
    steps = [lam1, lam2, lam1 / apart, 2 * apart / scale]
    table = np.stack([part for row in rows for part in (row.real, row.imag)])
    down, up = np.arange(BY)[:, None], BY - 1 - np.arange(BY)[:, None]
    states = [lam1**up, lam2**down]
    homogeneous = [lam1**down, lam2**up]
    add = np.zeros((4, 4, 8, 4, 2, 8))
    for quarter in range(4):
        for plane in range(2):
            for part in range(4):
                add[quarter, part, 2 * quarter + plane, part, plane, :] = 1
    add = add.reshape(4, CARRY, 64)
    table = table.reshape(len(table), 4, QX)
    packed = np.repeat(table, 2, axis=1)
    table = table.transpose(1, 0, 2)

    def parts(values):
        return np.stack([part for value in values for part in (value.real, value.imag)])

    return (
        forward,
        inverse,
        parts([factor]),
        parts(states),
        parts(homogeneous),
        parts(steps),
        add,
        table,
        packed,
    )


def kick(real_part, imag_part, potential):
    turn = -0.5 * time_step / (2 * np.pi)
    density = real_part * real_part + imag_part * imag_part
    turns = potential * turn + density * (turn * coupling)
    rest = turns - jnp.round(turns)
    square = rest * rest
    sine = rest * (
        4.4428679 + square * (-7.30744342 + square * (3.59478806 + square * -0.78437396))
    )
    cosine = 1.4142135 + square * (
        -6.97885099 + square * (5.73946123 + square * (-1.88356328 + square * 0.31069871))
    )
    whole_cos = 1.0 - sine * sine
    whole_sin = sine * cosine
    return (
        real_part * whole_cos - imag_part * whole_sin,
        real_part * whole_sin + imag_part * whole_cos,
    )


def cmul(a, b):
    return a[0] * b[0] - a[1] * b[1], a[0] * b[1] + a[1] * b[0]


def cadd(a, b):
    return a[0] + b[0], a[1] + b[1]


def csub(a, b):
    return a[0] - b[0], a[1] - b[1]


def split_modes(real_part, imag_part):
    quarter = [
        (real_part[:, QX * p : QX * (p + 1)], imag_part[:, QX * p : QX * (p + 1)])
        for p in range(4)
    ]
    t0, t1 = cadd(quarter[0], quarter[2]), csub(quarter[0], quarter[2])
    t2, t3 = cadd(quarter[1], quarter[3]), csub(quarter[1], quarter[3])
    return [
        cadd(t0, t2),
        (t1[0] + t3[1], t1[1] - t3[0]),
        csub(t0, t2),
        (t1[0] - t3[1], t1[1] + t3[0]),
    ]


def join_modes(back):
    t0, t1 = cadd(back[0], back[2]), csub(back[0], back[2])
    t2, t3 = cadd(back[1], back[3]), csub(back[1], back[3])
    return [
        cadd(t0, t2),
        (t1[0] - t3[1], t1[1] + t3[0]),
        csub(t0, t2),
        (t1[0] + t3[1], t1[1] - t3[0]),
    ]


def x_sweep(count, load, factors, store, left, cells, forward_ref, inverse_ref):
    rows = 16 * count
    for n in range(count):
        mixed = split_modes(*load(n))
        for residue in range(4):
            left[residue, 16 * n : 16 * n + 16, :] = jnp.concatenate(mixed[residue], axis=1)
    for residue in range(4):
        modes = jnp.dot(left[residue, 0:rows, :], forward_ref[residue], preferred_element_type=f32)
        for n in range(count):
            some = modes[16 * n : 16 * n + 16]
            scaled = cmul((some[:, :QX], some[:, QX:]), factors(n)[residue])
            left[residue, 16 * n : 16 * n + 16, :] = jnp.concatenate(scaled, axis=1).astype(bf16)
    for residue in range(4):
        cells[residue, 0:rows, :] = jnp.dot(
            left[residue, 0:rows, :], inverse_ref[residue], preferred_element_type=f32
        )
    for n in range(0, count, 2):
        done = []
        for at in range(2):
            lines = slice(16 * (n + at), 16 * (n + at) + 16)
            some = [cells[residue, lines, :] for residue in range(4)]
            out = join_modes([(one[:, :QX], one[:, QX:]) for one in some])
            done.append([jnp.concatenate([one[part] for one in out], axis=1) for part in range(2)])
        store(n, done)


def main_kernel(
    count_py,
    count_pz,
    z_step,
    z_profile,
    wave_hbm,
    pot_hbm,
    xf_hbm,
    xi_hbm,
    weight_hbm,
    factor_hbm,
    trig_ref,
    z_ref,
    yf_ref,
    yi_ref,
    add_ref,
    turn_ref,
    ytab_ref,
    step_ref,
    packed_ref,
    field_hbm,
    change_hbm,
    wave,
    pot,
    xf,
    xi,
    weight,
    factor,
    fresh_a,
    fresh_b,
    gains,
    grid,
    swept,
    solved,
    planes,
    result,
    left_buf,
    cells_buf,
    sums,
    z_states,
    z_partner,
    z_send,
    z_recv,
    z_back,
    z_chip,
    z_give,
    z_carry,
    y_send,
    y_recv,
    y_back,
    y_carry,
    c_send,
    c_recv,
    change,
    in_sem,
    tab_sem,
    out_sem,
    pair_sems,
    z_sems,
    z_back_sems,
    y_sems,
    c_sems,
):
    me_y = lax.axis_index("py")
    me_z = lax.axis_index("pz")
    core = lax.rem(me_z, 2)
    chip = me_z // 2
    partner = me_z + 1 - 2 * core
    chips = count_pz // 2
    half_z = TILES_Z // 2
    tiles_z = half_z // chips
    mine = core * half_z
    theirs = half_z - mine

    def load(group):
        rows = pl.ds(pl.multiple_of(group * 8, 8), 8)
        return (
            pltpu.make_async_copy(wave_hbm.at[:, :, rows, :], wave.at[group], in_sem.at[0, group]),
            pltpu.make_async_copy(pot_hbm.at[:, rows, :], pot.at[group], in_sem.at[1, group]),
        )

    for group in range(GROUPS):
        for copy in load(group):
            copy.start()
    table_copies = (
        pltpu.make_async_copy(xf_hbm, xf, tab_sem.at[0]),
        pltpu.make_async_copy(xi_hbm, xi, tab_sem.at[1]),
        pltpu.make_async_copy(weight_hbm, weight, tab_sem.at[2]),
        pltpu.make_async_copy(factor_hbm, factor, tab_sem.at[3]),
    )
    for copy in table_copies:
        copy.start()

    barrier = pltpu.get_barrier_semaphore()

    def twin(other):
        return {"pz": other * 2 + core}

    pl.semaphore_signal(barrier, inc=1, device_id={"pz": partner}, device_id_type=MESH)

    @pl.loop(1, chips)
    def _(step):
        pl.semaphore_signal(
            barrier, inc=1, device_id=twin(lax.rem(chip + step, chips)), device_id_type=MESH
        )

    @pl.loop(1, count_py)
    def _(step):
        pl.semaphore_signal(
            barrier, inc=1, device_id={"py": lax.rem(me_y + step, count_py)}, device_id_type=MESH
        )

    for group in range(GROUPS):
        cell = lax.broadcasted_iota(jnp.int32, (8, QX), 0) + (
            me_y * BY + group * 8 - count_py * BY // 2
        )
        beta = cell.astype(f32) * (0.5 * time_step * rotation)
        for residue in range(4):
            rate = trig_ref[2 * residue : 2 * residue + 1] + beta * trig_ref[
                2 * residue + 1 : 2 * residue + 2
            ]
            scale = 1.0 / (1.0 + rate * rate)
            lines = slice(8 * group, 8 * group + 8)
            gains[2 * residue, lines, :] = (1.0 - rate * rate) * scale
            gains[2 * residue + 1, lines, :] = -2.0 * rate * scale

    def kick_group(group, fresh):
        for some in range(BZ // 2):
            rows = slice(2 * some, 2 * some + 2)
            new = kick(wave[group, 0, rows], wave[group, 1, rows], pot[group, rows])
            for part in range(2):
                start = ROWS // 2 * part + 16 * some
                fresh[start : start + 16, :] = new[part].reshape(16, NX).astype(bf16)

    def solve_group(group, fresh):
        for side in range(2):
            lanes = slice(side * NX // 2, (side + 1) * NX // 2)
            rows = jnp.dot(z_ref[...], fresh[:, lanes], preferred_element_type=f32)
            for start in range(0, ROWS, 16):
                grid[group, start : start + 16, lanes] = rows[start : start + 16].astype(bf16)
            states = rows[ROWS:].astype(bf16)
            for quarter in range(2):
                z_states[group * 4 + 2 * side + quarter] = states[
                    :, QX * quarter : QX * (quarter + 1)
                ].reshape(2, 16, QX)

    def pair_out(step):
        return pltpu.make_async_remote_copy(
            src_ref=z_states.at[pl.ds(theirs + 4 * step, 4)],
            dst_ref=z_partner.at[pl.ds(4 * step, 4)],
            send_sem=pair_sems.at[0, step],
            recv_sem=pair_sems.at[1, step],
            device_id={"pz": partner},
            device_id_type=MESH,
        )

    def pair_back():
        return pltpu.make_async_remote_copy(
            src_ref=z_give,
            dst_ref=z_carry.at[pl.ds(mine, half_z)],
            send_sem=pair_sems.at[0, 4],
            recv_sem=pair_sems.at[1, 4],
            device_id={"pz": partner},
            device_id_type=MESH,
        )

    def pair_returned():
        return pltpu.make_async_remote_copy(
            src_ref=z_give,
            dst_ref=z_carry.at[pl.ds(theirs, half_z)],
            send_sem=pair_sems.at[0, 4],
            recv_sem=pair_sems.at[1, 4],
            device_id={"pz": partner},
            device_id_type=MESH,
        )

    def z_out(tile):
        return pltpu.make_async_remote_copy(
            src_ref=z_send.at[tile],
            dst_ref=z_recv.at[chip, lax.rem(tile, tiles_z)],
            send_sem=z_sems.at[0, tile],
            recv_sem=z_sems.at[1, chip * tiles_z + lax.rem(tile, tiles_z)],
            device_id=twin(tile // tiles_z),
            device_id_type=MESH,
        )

    def z_in(step, tile):
        peer = lax.rem(chip + step, chips)
        return pltpu.make_async_remote_copy(
            src_ref=z_send.at[tile],
            dst_ref=z_recv.at[peer, tile],
            send_sem=z_sems.at[0, tile],
            recv_sem=z_sems.at[1, peer * tiles_z + tile],
            device_id=twin(peer),
            device_id_type=MESH,
        )

    def z_return(step):
        peer = lax.rem(chip + step, chips)
        return pltpu.make_async_remote_copy(
            src_ref=z_back.at[peer],
            dst_ref=z_chip.at[pl.ds(chip * tiles_z, tiles_z)],
            send_sem=z_back_sems.at[0, peer],
            recv_sem=z_back_sems.at[1, chip],
            device_id=twin(peer),
            device_id_type=MESH,
        )

    def z_returned(step):
        peer = lax.rem(chip + step, chips)
        return pltpu.make_async_remote_copy(
            src_ref=z_back.at[chip],
            dst_ref=z_chip.at[pl.ds(peer * tiles_z, tiles_z)],
            send_sem=z_back_sems.at[0, chip],
            recv_sem=z_back_sems.at[1, peer],
            device_id=twin(peer),
            device_id_type=MESH,
        )

    lead = core == 0
    block_step = (z_step.real, z_step.imag)
    chip_step = z_step * z_step

    def parts(array):
        array = array.astype(f32)
        return array[0:8], array[8:16]

    def choose(first, second):
        return jnp.where(lead, first[0], second[0]), jnp.where(lead, first[1], second[1])

    def joined(value):
        return jnp.concatenate(value, axis=0).astype(bf16)

    def order(count):
        if count < GROUPS // 2:
            return theirs // 4 + count
        return mine // 4 + lax.rem(count + chip // 4, GROUPS // 2)

    def merge(step):
        pair_out(step).wait_recv()
        for at in range(4):
            tile = step * 4 + at
            own = [parts(z_states[mine + tile, side]) for side in range(2)]
            other = [parts(z_partner[tile, side]) for side in range(2)]
            left = cadd(choose(other[0], own[0]), cmul(choose(own[0], other[0]), block_step))
            right = cadd(choose(own[1], other[1]), cmul(choose(other[1], own[1]), block_step))
            z_send[tile, 0] = joined(left)
            z_send[tile, 1] = joined(right)
        for at in range(4):
            tile = step * 4 + at
            owner = tile // tiles_z

            @pl.when(owner != chip)
            def _():
                z_out(tile).start()

            @pl.when(owner == chip)
            def _():
                z_recv[chip, lax.rem(tile, tiles_z)] = z_send[tile]

    def kicked(count, fresh):
        for copy in load(order(count)):
            copy.wait()
        kick_group(order(count), fresh)

    fresh = (fresh_a, fresh_b)
    kicked(0, fresh[0])
    for count in range(GROUPS):
        if count + 1 < GROUPS:
            for copy in load(order(count + 1)):
                copy.wait()
        solve_group(order(count), fresh[count % 2])
        if count + 1 < GROUPS:
            kick_group(order(count + 1), fresh[(count + 1) % 2])
        if count == 0:
            pl.semaphore_wait(barrier, chips + count_py - 1)
        if count < GROUPS // 2:
            pair_out(count).start()
        else:
            merge(order(count) - mine // 4)

    for copy in table_copies:
        copy.wait()

    def sweep_field():
        def fetch(n):
            group, row = n // 8, n % 8 * BZ
            return tuple(
                grid[group, start : start + BZ, :] for start in (row, row + ROWS // 2)
            )

        def gain(n):
            line = slice(n, n + 1)
            return [
                (gains[2 * residue, line, :], gains[2 * residue + 1, line, :])
                for residue in range(4)
            ]

        def put(n, done):
            for at in range(2):
                start = (n + at) * BZ
                for part in range(2):
                    swept[part, start : start + BZ, :] = done[at][part].astype(bf16)

        x_sweep(BY, fetch, gain, put, left_buf, cells_buf, xf, xi)

    steps_y = [(step_ref[2 * n : 2 * n + 1], step_ref[2 * n + 1 : 2 * n + 2]) for n in range(4)]
    forward_step, backward_step, turn_step, whole_gain = steps_y

    def y_rows(cell):
        return pl.ds(pl.multiple_of(cell * BZ, BZ), BZ)

    def save(rows, value):
        for part in range(2):
            for quarter in range(4):
                solved[part, quarter, rows, :] = value[part][
                    :, QX * quarter : QX * (quarter + 1)
                ]

    def y_forward():
        def advance(cell, totals):
            total, other = totals
            rows = y_rows(cell)
            value = tuple(swept[part, rows, :].astype(f32) for part in range(2))
            total = cadd(value, cmul(total, forward_step))
            save(rows, total)
            share = tuple(weight[2 + part, pl.ds(cell, 1), :] for part in range(2))
            return total, cadd(other, cmul(value, share))

        zero = jnp.zeros((BZ, NX), f32)
        return lax.fori_loop(0, BY, advance, ((zero, zero), (zero, zero)), unroll=4)

    def y_backward(first, last, total):
        def advance(count, total):
            rows = y_rows(BY - 1 - count)
            value = tuple(
                jnp.concatenate([solved[part, quarter, rows, :] for quarter in range(4)], axis=1)
                for part in range(2)
            )
            total = cadd(value, cmul(total, backward_step))
            out = cmul(total, whole_gain)
            save(rows, [out[part] - swept[part, rows, :].astype(f32) for part in range(2)])
            return total

        return lax.fori_loop(first, last, advance, total, unroll=4)

    def y_states(count):
        @pl.loop(0, count)
        def _(at):
            for quarter in range(4):
                lanes = slice(QX * quarter, QX * (quarter + 1))
                total = [[0.0, 0.0], [0.0, 0.0]]
                for start in range(0, BY, 16):
                    rows = slice(start, start + 16)
                    value = [planes[part, at, rows, lanes].astype(f32) for part in range(2)]
                    for side in range(2):
                        some = cmul(
                            value, (weight[2 * side, rows, lanes], weight[2 * side + 1, rows, lanes])
                        )
                        for part in range(2):
                            total[side][part] += some[part][0:8] + some[part][8:16]
                for side in range(2):
                    for part in range(2):
                        row = pl.multiple_of((side * 2 + part) * 16 + at * 8, 8)
                        sums[pl.ds(row, 8), lanes] = total[side][part]

        rows = 0.0
        for quarter in range(4):
            some = sums[:, QX * quarter : QX * (quarter + 1)].astype(bf16)
            rows += jnp.dot(add_ref[quarter], some, preferred_element_type=f32)
        return rows.astype(bf16)

    def y_periodic(plane):
        for side in range(2):
            lanes = slice(side * NX // 2, (side + 1) * NX // 2)
            block = jnp.concatenate([planes[part, plane, :, lanes] for part in range(2)], axis=0)
            modes = jnp.dot(yf_ref[...], block, preferred_element_type=f32)
            scaled = [
                cmul(
                    (modes[some : some + 32], modes[BY + some : BY + some + 32]),
                    (factor[0, some : some + 32, lanes], factor[1, some : some + 32, lanes]),
                )
                for some in range(0, BY, 32)
            ]
            block = jnp.concatenate(
                [one[part].astype(bf16) for part in range(2) for one in scaled], axis=0
            )
            cells = jnp.dot(yi_ref[...], block, preferred_element_type=f32).astype(bf16)
            for part in range(2):
                planes[part, plane, :, lanes] = cells[part * BY : (part + 1) * BY]

    class Exchange:
        def __init__(self, send, recv, back, carry, sems, tiles):
            self.send, self.recv, self.back, self.carry = send, recv, back, carry
            self.sems, self.tiles = sems, tiles

        def mine(self):
            return pl.ds(me_y * self.tiles, self.tiles)

        def out(self, peer):
            return pltpu.make_async_remote_copy(
                src_ref=self.send.at[pl.ds(peer * self.tiles, self.tiles)],
                dst_ref=self.recv.at[me_y],
                send_sem=self.sems.at[0, peer],
                recv_sem=self.sems.at[1, me_y],
                device_id={"py": peer},
                device_id_type=MESH,
            )

        def arrived(self, peer):
            return pltpu.make_async_remote_copy(
                src_ref=self.send.at[self.mine()],
                dst_ref=self.recv.at[peer],
                send_sem=self.sems.at[0, me_y],
                recv_sem=self.sems.at[1, peer],
                device_id={"py": peer},
                device_id_type=MESH,
            )

        def give(self, peer):
            return pltpu.make_async_remote_copy(
                src_ref=self.back.at[peer],
                dst_ref=self.carry.at[self.mine()],
                send_sem=self.sems.at[2, peer],
                recv_sem=self.sems.at[3, me_y],
                device_id={"py": peer},
                device_id_type=MESH,
            )

        def given(self, peer):
            return pltpu.make_async_remote_copy(
                src_ref=self.back.at[me_y],
                dst_ref=self.carry.at[pl.ds(peer * self.tiles, self.tiles)],
                send_sem=self.sems.at[2, me_y],
                recv_sem=self.sems.at[3, peer],
                device_id={"py": peer},
                device_id_type=MESH,
            )

        def post(self):
            @pl.loop(1, count_py)
            def _(step):
                self.out(lax.rem(me_y + step, count_py)).start()

        def answer(self):
            self.recv[me_y] = self.send[self.mine()]

            @pl.loop(1, count_py)
            def _(step):
                self.arrived(lax.rem(me_y + step, count_py)).wait_recv()

            for tile in range(self.tiles):
                solve_tile(self.recv, self.back, tile, lax.rem(me_y * self.tiles + tile, 4))

            @pl.loop(1, count_py)
            def _(step):
                self.give(lax.rem(me_y + step, count_py)).start()

            self.carry[self.mine()] = self.back[me_y]

        def receive(self):
            @pl.loop(1, count_py)
            def _(step):
                self.given(lax.rem(me_y + step, count_py)).wait_recv()

        def close(self):
            @pl.loop(1, count_py)
            def _(step):
                peer = lax.rem(me_y + step, count_py)
                self.out(peer).wait_send()
                self.give(peer).wait_send()

        def rows(self, tiles):
            return [self.carry[tile].reshape(CARRY, QX) for tile in tiles]

    def solve_tile(recv, back, tile, quarter):
        table = ytab_ref[quarter]
        value = [(table[2 * n : 2 * n + 1], table[2 * n + 1 : 2 * n + 2]) for n in range(8)]
        whole1, whole2, _, _, wrap1, wrap2, out1, out2 = value
        left_state = [parts(recv[block, tile, 0]) for block in range(count_py)]
        right_state = [parts(recv[block, tile, 1]) for block in range(count_py)]
        left, right = left_state[0], right_state[count_py - 1]
        for block in range(1, count_py):
            left = cadd(left_state[block], cmul(left, whole1))
            right = cadd(right_state[count_py - 1 - block], cmul(right, whole2))
        left, right = cmul(left, wrap1), cmul(right, wrap2)
        for block in range(count_py):
            other = count_py - 1 - block
            back[block, tile, 0] = joined(cmul(left, out1))
            back[other, tile, 1] = joined(cmul(right, out2))
            left = cadd(left_state[block], cmul(left, whole1))
            right = cadd(right_state[other], cmul(right, whole2))

    planes_y = Exchange(y_send, y_recv, y_back, y_carry, y_sems, TILES_Y // count_py)
    def carry_out(step):
        return pltpu.make_async_remote_copy(
            src_ref=c_send,
            dst_ref=c_recv.at[me_y],
            send_sem=c_sems.at[0, lax.rem(me_y + step, count_py)],
            recv_sem=c_sems.at[1, me_y],
            device_id={"py": lax.rem(me_y + step, count_py)},
            device_id_type=MESH,
        )

    def carry_in(step):
        peer = lax.rem(me_y + step, count_py)
        return pltpu.make_async_remote_copy(
            src_ref=c_send,
            dst_ref=c_recv.at[peer],
            send_sem=c_sems.at[0, me_y],
            recv_sem=c_sems.at[1, peer],
            device_id={"py": peer},
            device_id_type=MESH,
        )

    def carry_solve():
        value = [(packed_ref[2 * n], packed_ref[2 * n + 1]) for n in range(8)]
        whole1, whole2, own1, own2, wrap1, wrap2, out1, out2 = value
        own = [parts(c_send[side]) for side in range(2)]
        left, right = own
        for step in range(1, count_py):
            left = cadd(parts(c_recv[lax.rem(me_y + step, count_py), 0]), cmul(left, whole1))
            back = lax.rem(me_y + count_py - step, count_py)
            right = cadd(parts(c_recv[back, 1]), cmul(right, whole2))
        left = csub(cmul(left, wrap1), cmul(own[0], own1))
        right = csub(cmul(right, wrap2), cmul(own[1], own2))
        return jnp.concatenate([joined(cmul(left, out1)), joined(cmul(right, out2))], axis=0)

    def post_planes(states):
        for half in range(2):
            lines = slice(8 * half, 8 * half + 8)
            for quarter in range(4):
                lanes = slice(QX * quarter, QX * (quarter + 1))
                for side in range(2):
                    y_send[half * 4 + quarter, side] = joined(
                        [states[side][part][lines, lanes] for part in range(2)]
                    )
        planes_y.post()

    sweep_field()

    @pl.loop(1, chips)
    def _(step):
        for tile in range(tiles_z):
            z_in(step, tile).wait_recv()

    for tile in range(tiles_z):

        def state(block, side):
            return parts(z_recv[block, tile, side])

        def advance(total, value):
            return cadd(cmul(total, (chip_step.real, chip_step.imag)), value)

        def gather(step, carry):
            left, right = carry
            return (
                advance(left, state(step, 0)),
                advance(right, state(chips - 1 - step, 1)),
            )

        zero = (jnp.zeros((8, QX), f32), jnp.zeros((8, QX), f32))
        left, right = lax.fori_loop(0, chips, gather, (zero, zero), unroll=8)
        wrap = 1 / (1 - chip_step**chips)
        left = cmul(left, (wrap.real, wrap.imag))
        right = cmul(right, (wrap.real, wrap.imag))

        def hand_out(step, carry):
            left, right = carry
            last = chips - 1 - step
            z_back[step, tile, 0] = joined(left)
            z_back[last, tile, 1] = joined(right)
            return advance(left, state(step, 0)), advance(right, state(last, 1))

        lax.fori_loop(0, chips, hand_out, (left, right), unroll=8)

    @pl.loop(1, chips)
    def _(step):
        z_return(step).start()

    z_chip[pl.ds(chip * tiles_z, tiles_z)] = z_back[chip]

    forward_state, backward_state = y_forward()
    post_planes((forward_state, backward_state))
    back_total = y_backward(0, BY // 2, cmul(forward_state, turn_step))

    @pl.loop(1, chips)
    def _(step):
        z_returned(step).wait_recv()

    def split_carry(tile, _):
        own = [parts(z_states[mine + tile, side]) for side in range(2)]
        other = [parts(z_partner[tile, side]) for side in range(2)]
        whole = [parts(z_chip[tile, side]) for side in range(2)]
        inner_left = cadd(choose(own[0], other[0]), cmul(whole[0], block_step))
        inner_right = cadd(choose(other[1], own[1]), cmul(whole[1], block_step))
        z_give[tile, 0] = joined(choose(inner_left, whole[0]))
        z_give[tile, 1] = joined(choose(whole[1], inner_right))
        z_carry[mine + tile, 0] = joined(choose(whole[0], inner_left))
        z_carry[mine + tile, 1] = joined(choose(inner_right, whole[1]))
        return 0

    lax.fori_loop(0, half_z, split_carry, 0, unroll=4)
    pair_back().start()

    def carry_planes(first):
        def fetch(n):
            sides = [
                jnp.concatenate(
                    [z_carry[(first + n) * 4 + quarter, side] for quarter in range(4)], axis=1
                ).astype(f32)
                for side in range(2)
            ]
            return tuple(
                jnp.concatenate(
                    [side[8 * part : 8 * part + 8] for side in sides], axis=0
                ).astype(bf16)
                for part in range(2)
            )

        def gain(n):
            lines = pl.ds(pl.multiple_of((first + n) * 8, 8), 8)
            return [
                tuple(
                    jnp.concatenate([gains[2 * residue + part, lines, :]] * 2, axis=0)
                    for part in range(2)
                )
                for residue in range(4)
            ]

        def put(n, done):
            rows = pl.ds(pl.multiple_of((first + n) * 8, 16), 16)
            for side in range(2):
                lines = slice(8 * side, 8 * side + 8)
                for part in range(2):
                    planes[part, side, rows, :] = jnp.concatenate(
                        [done[at][part][lines] for at in range(2)], axis=0
                    ).astype(bf16)

        x_sweep(GROUPS // 2, fetch, gain, put, left_buf, cells_buf, xf, xi)

    carry_planes(mine // 4)
    pair_returned().wait_recv()
    carry_planes(theirs // 4)
    c_send[...] = y_states(2).reshape(2, 16, QX)

    @pl.loop(1, count_py)
    def _(step):
        carry_out(step).start()

    planes_y.answer()
    y_backward(BY // 2, BY, back_total)
    y_periodic(0)
    y_periodic(1)

    def store(pair):
        rows = pl.ds(pl.multiple_of(pair * 16, 16), 16)
        return pltpu.make_async_copy(
            result.at[:, :, rows, :], field_hbm.at[:, :, rows, :], out_sem.at[pair]
        )

    @pl.loop(0, BY // 16)
    def _(pair):
        rows = pl.ds(pl.multiple_of(pair * 16, 16), 16)
        for quarter in range(4):
            lanes = slice(QX * quarter, QX * (quarter + 1))
            left, right = [
                tuple(planes[part, one, rows, lanes] for part in range(2)) for one in range(2)
            ]
            for plane in range(BZ):
                first, second = (complex(one) for one in z_profile[plane])
                lines = pl.ds(pair * 16 * BZ + plane, 16, stride=BZ)
                value = tuple(solved[part, quarter, lines, :].astype(bf16) for part in range(2))
                value = cadd(value, cmul(left, (first.real, first.imag)))
                value = cadd(value, cmul(right, (second.real, second.imag)))
                for part in range(2):
                    result[part, plane, rows, lanes] = value[part]
        store(pair).start()

    @pl.loop(0, half_z)
    def _(tile):
        @pl.when(tile // tiles_z != chip)
        def _():
            z_out(tile).wait_send()

    @pl.loop(1, chips)
    def _(step):
        z_return(step).wait_send()

    @pl.loop(0, GROUPS // 2)
    def _(step):
        pair_out(step).wait_send()

    pair_back().wait_send()

    @pl.loop(1, count_py)
    def _(step):
        carry_in(step).wait_recv()

    carried = carry_solve()
    planes_y.receive()
    for quarter in range(4):
        rows = planes_y.rows((quarter, 4 + quarter)) + [carried]
        change[:, :, QX * quarter : QX * (quarter + 1)] = jnp.dot(
            turn_ref[quarter], jnp.concatenate(rows, axis=0), preferred_element_type=f32
        ).reshape(BZ, 8, QX)
    last = pltpu.make_async_copy(change, change_hbm, out_sem.at[GROUPS // 2])
    last.start()

    planes_y.close()

    @pl.loop(1, count_py)
    def _(step):
        carry_out(step).wait_send()


    @pl.loop(0, GROUPS // 2)
    def _(pair):
        store(pair).wait()

    last.wait()


PLANES = 2


def finish_kernel(
    field_hbm,
    change_hbm,
    pot_hbm,
    table_hbm,
    out_hbm,
    field,
    change,
    pot,
    table,
    out,
    in_sem,
    tab_sem,
    out_sem,
):
    steps = BZ // PLANES

    def load(step):
        planes = pl.ds(step * PLANES, PLANES)
        return (
            pltpu.make_async_copy(field_hbm.at[:, planes], field.at[:, planes], in_sem.at[0, step]),
            pltpu.make_async_copy(pot_hbm.at[planes], pot.at[planes], in_sem.at[1, step]),
        )

    def save(step):
        planes = pl.ds(step * PLANES, PLANES)
        return pltpu.make_async_copy(out.at[:, planes], out_hbm.at[:, planes], out_sem.at[step])

    tables = (
        pltpu.make_async_copy(change_hbm, change, tab_sem.at[0]),
        pltpu.make_async_copy(table_hbm, table, tab_sem.at[1]),
    )
    for copy in tables:
        copy.start()
    for step in range(steps):
        for copy in load(step):
            copy.start()
    for copy in tables:
        copy.wait()

    def finish(at, lanes):
        ends = [change[at, row : row + 1, lanes].astype(bf16) for row in range(4)]
        for start in range(0, BY, 16):
            rows = slice(start, start + 16)
            value = tuple(field[part, at, rows, lanes] for part in range(2))
            for side in range(2):
                profile = (table[2 * side, rows, lanes], table[2 * side + 1, rows, lanes])
                value = cadd(value, cmul(profile, (ends[2 * side], ends[2 * side + 1])))
            new = kick(value[0].astype(f32), value[1].astype(f32), pot[at, rows, lanes])
            for part in range(2):
                out[part, at, rows, lanes] = new[part]

    @pl.loop(0, steps)
    def _(step):
        for copy in load(step):
            copy.wait()
        for one in range(PLANES):
            for side in range(2):
                finish(step * PLANES + one, slice(side * NX // 2, (side + 1) * NX // 2))
        save(step).start()

    @pl.loop(0, steps)
    def _(step):
        save(step).wait()


def shards(count_py, count_pz, wavefunction, potential):
    forward_x, inverse_x, trig = x_tables()
    z_rows, turn, z_profile, z_step = z_tables()
    forward_y, inverse_y, factor, weight, homogeneous, steps_y, add, y_table, packed = y_tables(count_py)

    def low(array):
        return jnp.asarray(array.astype(np.float32)).astype(bf16)

    def full(array):
        return jnp.asarray(array.astype(np.float32))

    chips = count_pz // 2
    tiles_z = TILES_Z // 2 // chips
    tiles_y = TILES_Y // count_py
    anywhere = pl.BlockSpec(memory_space=pl.ANY)
    inside = pl.BlockSpec(memory_space=pltpu.VMEM)
    field, change = pl.pallas_call(
        functools.partial(main_kernel, count_py, count_pz, z_step, z_profile),
        out_shape=(
            pltpu.VMEM((2, BZ, BY, NX), bf16),
            pltpu.VMEM((BZ, 8, NX), f32),
        ),
        in_specs=[anywhere] * 6 + [inside] * 9,
        out_specs=(anywhere, anywhere),
        scratch_shapes=[
            pltpu.VMEM((GROUPS, 2, BZ, 8, NX), f32),
            pltpu.VMEM((GROUPS, BZ, 8, NX), f32),
            pltpu.VMEM((4, 2 * QX, 2 * QX), bf16),
            pltpu.VMEM((4, 2 * QX, 2 * QX), bf16),
            pltpu.VMEM(weight.shape, f32),
            pltpu.VMEM(factor.shape, f32),
            pltpu.VMEM((ROWS, NX), bf16),
            pltpu.VMEM((ROWS, NX), bf16),
            pltpu.VMEM((8, BY, QX), f32),
            pltpu.VMEM((GROUPS, ROWS, NX), bf16),
            pltpu.VMEM((2, BY * BZ, NX), bf16),
            pltpu.VMEM((2, 4, BY * BZ, QX), f32),
            pltpu.VMEM((2, 2, BY, NX), bf16),
            pltpu.VMEM((2, BZ, BY, NX), bf16),
            pltpu.VMEM((4, BY * BZ, 2 * QX), bf16),
            pltpu.VMEM((4, BY * BZ, 2 * QX), f32),
            pltpu.VMEM((64, NX), f32),
            pltpu.VMEM((TILES_Z, 2, 16, QX), bf16),
            pltpu.VMEM((TILES_Z // 2, 2, 16, QX), bf16),
            pltpu.VMEM((TILES_Z // 2, 2, 16, QX), bf16),
            pltpu.VMEM((chips, tiles_z, 2, 16, QX), bf16),
            pltpu.VMEM((chips, tiles_z, 2, 16, QX), bf16),
            pltpu.VMEM((TILES_Z // 2, 2, 16, QX), bf16),
            pltpu.VMEM((TILES_Z // 2, 2, 16, QX), bf16),
            pltpu.VMEM((TILES_Z, 2, 16, QX), bf16),
            pltpu.VMEM((TILES_Y, 2, 16, QX), bf16),
            pltpu.VMEM((count_py, tiles_y, 2, 16, QX), bf16),
            pltpu.VMEM((count_py, tiles_y, 2, 16, QX), bf16),
            pltpu.VMEM((TILES_Y, 2, 16, QX), bf16),
            pltpu.VMEM((2, 16, QX), bf16),
            pltpu.VMEM((count_py, 2, 16, QX), bf16),
            pltpu.VMEM((BZ, 8, NX), f32),
            pltpu.SemaphoreType.DMA((2, GROUPS)),
            pltpu.SemaphoreType.DMA((4,)),
            pltpu.SemaphoreType.DMA((GROUPS // 2 + 1,)),
            pltpu.SemaphoreType.DMA((2, 5)),
            pltpu.SemaphoreType.DMA((2, TILES_Z // 2)),
            pltpu.SemaphoreType.DMA((2, chips)),
            pltpu.SemaphoreType.DMA((4, count_py)),
            pltpu.SemaphoreType.DMA((2, count_py)),
        ],
        compiler_params=pltpu.CompilerParams(
            collective_id=0, has_side_effects=True, vmem_limit_bytes=57 * 2**20
        ),
        cost_estimate=pl.CostEstimate(
            flops=3_000_000_000, bytes_accessed=10_000_000, transcendentals=0
        ),
        name="sweeps",
    )(
        wavefunction,
        potential,
        low(forward_x),
        low(inverse_x),
        full(weight),
        full(factor),
        full(trig),
        low(z_rows),
        low(forward_y),
        low(inverse_y),
        low(add),
        low(turn),
        full(y_table),
        full(steps_y),
        full(packed),
    )
    return pl.pallas_call(
        finish_kernel,
        out_shape=jax.ShapeDtypeStruct((2, BZ, BY, NX), f32),
        in_specs=[anywhere] * 4,
        out_specs=anywhere,
        scratch_shapes=[
            pltpu.VMEM((2, BZ, BY, NX), bf16),
            pltpu.VMEM((BZ, 8, NX), f32),
            pltpu.VMEM((BZ, BY, NX), f32),
            pltpu.VMEM(homogeneous.shape, bf16),
            pltpu.VMEM((2, BZ, BY, NX), f32),
            pltpu.SemaphoreType.DMA((2, BZ // PLANES)),
            pltpu.SemaphoreType.DMA((2,)),
            pltpu.SemaphoreType.DMA((BZ // PLANES,)),
        ],
        compiler_params=pltpu.CompilerParams(vmem_limit_bytes=16 * 2**20),
        cost_estimate=pl.CostEstimate(
            flops=800_000_000, bytes_accessed=9_000_000, transcendentals=0
        ),
        name="finish",
    )(field, change, potential, low(homogeneous))


def solution(mesh):
    return jax.shard_map(
        functools.partial(shards, mesh.shape["py"], mesh.shape["pz"]),
        mesh=mesh,
        in_specs=(P(None, "pz", "py", None), P("pz", "py", None)),
        out_specs=P(None, "pz", "py", None),
        check_vma=False,
    )
```

```python
import functools

import jax
import jax.numpy as jnp
import numpy as np
from jax import lax
from jax.experimental import pallas as pl
from jax.experimental.pallas import tpu as pltpu
from jax.sharding import PartitionSpec as P

time_step = 0.005
rotation = 0.9
coupling = 100.0
grid_spacing = 0.05

NX = 512
BY = 64
BZ = 16
QX = 128
GROUPS = BY // 8
TILES_Z = GROUPS * 4
TILES_Y = 8
ROWS = 2 * BZ * 8
CARRY = 32

MESH = pl.DeviceIdType.MESH
f32 = jnp.float32
bf16 = jnp.bfloat16


def line_roots(beta):
    beta = np.asarray(beta, np.float64)
    half = (beta - 1j) / 2
    spread = np.sqrt((1 + 1j) ** 2 - (beta - 1j) * (-beta - 1j))
    first = (-(1 + 1j) + spread) / (beta - 1j)
    second = (-(1 + 1j) - spread) / (beta - 1j)
    swap = np.abs(first) > np.abs(second)
    inner = np.where(swap, second, first)
    outer = np.where(swap, first, second)
    return inner, 1 / outer, half * (inner - outer)


def real_form(matrix):
    return np.stack(
        [
            np.stack([matrix.real, -matrix.imag], 1),
            np.stack([matrix.imag, matrix.real], 1),
        ],
        0,
    )


def x_tables():
    forward, inverse = [], []
    cells = np.arange(QX)
    for residue in range(4):
        modes = 4 * np.arange(QX) + residue
        angles = 2 * np.pi * ((cells[:, None] * modes[None, :]) % NX) / NX
        cosines, sines = np.cos(angles), np.sin(angles)
        forward.append(np.block([[cosines, -sines], [sines, cosines]]))
        inverse.append(np.block([[cosines.T, sines.T], [-sines.T, cosines.T]]) / NX)
    modes = 4 * np.arange(QX)[None, :] + np.arange(4)[:, None]
    theta = 2 * np.pi * modes / NX
    trig = np.stack([1 - np.cos(theta), np.sin(theta)], 1).reshape(8, QX)
    return np.stack(forward), np.stack(inverse), trig


def z_tables():
    lam, _, scale = line_roots(0.0)
    lam, scale = complex(lam), complex(scale)
    cells = np.arange(BZ)
    local = (2 / scale) * lam ** np.abs(cells[:, None] - cells[None, :]) - np.eye(BZ)
    carry = (2 / scale) * np.stack([lam ** (cells + 1), lam ** (BZ - cells)], 1)
    states = np.stack([lam ** (BZ - 1 - cells), lam**cells], 0)
    eye = np.eye(8)
    apply_field = np.einsum("azbw,ij->aizbwj", real_form(local), eye).reshape(ROWS, ROWS)
    state_rows = np.einsum("asbz,ij->saibzj", real_form(states), eye).reshape(CARRY, ROWS)
    turn = np.zeros((4, BZ, 8, 3, 4, 8))
    fields, carries = real_form(np.eye(BZ).astype(complex)), real_form(carry)
    for end in range(2):
        for out in range(2):
            for part in range(2):
                row, column = 2 * end + out, 2 * end + part
                for half in range(2):
                    turn[:, :, row, half, column, :] = fields[
                        out, :, part, 8 * half : 8 * half + 8
                    ]
                for quarter in range(4):
                    lines = slice(2 * quarter, 2 * quarter + 2)
                    turn[quarter, :, row, 2, column, lines] = carries[out, :, part, :]
    turn = turn.reshape(4, BZ * 8, 3 * CARRY)
    return np.concatenate([apply_field, state_rows], 0), turn, carry, lam**BZ


def y_tables(blocks):
    cells = np.arange(BY)
    angles = 2 * np.pi * ((cells[:, None] * cells[None, :]) % BY) / BY
    modes = np.exp(-1j * angles)
    forward = real_form(modes).reshape(2 * BY, 2 * BY)
    inverse = real_form(np.conj(modes) / BY).reshape(2 * BY, 2 * BY)
    beta = -0.5 * time_step * rotation * (np.arange(NX) - NX // 2)
    theta = 2 * np.pi * cells / BY
    rate = (1 - np.cos(theta))[:, None] + np.sin(theta)[:, None] * beta[None, :]
    factor = (1 - 1j * rate) / (1 + 1j * rate)
    lam1, lam2, scale = line_roots(beta)
    whole1, whole2 = lam1**BY, lam2**BY
    rows = [
        whole1,
        whole2,
        1 / (1 - whole1),
        1 / (1 - whole2),
        1 / (1 - whole1**blocks),
        1 / (1 - whole2**blocks),
        2 * lam1 / scale,
        2 * lam2 / scale,
    ]
    apart = 1 - lam1 * lam2
    steps = [lam1, lam2, lam1 / apart, 2 * apart / scale]
    table = np.stack([part for row in rows for part in (row.real, row.imag)])
    down, up = np.arange(BY)[:, None], BY - 1 - np.arange(BY)[:, None]
    states = [lam1**up, lam2**down]
    homogeneous = [lam1**down, lam2**up]
    add = np.zeros((4, 4, 8, 4, 2, 8))
    for quarter in range(4):
        for plane in range(2):
            for part in range(4):
                add[quarter, part, 2 * quarter + plane, part, plane, :] = 1
    add = add.reshape(4, CARRY, 64)
    table = table.reshape(len(table), 4, QX)
    packed = np.repeat(table, 2, axis=1)
    table = table.transpose(1, 0, 2)

    def parts(values):
        return np.stack([part for value in values for part in (value.real, value.imag)])

    return (
        forward,
        inverse,
        parts([factor]),
        parts(states),
        parts(homogeneous),
        parts(steps),
        add,
        table,
        packed,
    )


def kick(real_part, imag_part, potential):
    turn = -0.5 * time_step / (2 * np.pi)
    density = real_part * real_part + imag_part * imag_part
    turns = potential * turn + density * (turn * coupling)
    rest = turns - jnp.round(turns)
    square = rest * rest
    sine = rest * (
        4.4428679 + square * (-7.30744342 + square * (3.59478806 + square * -0.78437396))
    )
    cosine = 1.4142135 + square * (
        -6.97885099 + square * (5.73946123 + square * (-1.88356328 + square * 0.31069871))
    )
    whole_cos = 1.0 - sine * sine
    whole_sin = sine * cosine
    return (
        real_part * whole_cos - imag_part * whole_sin,
        real_part * whole_sin + imag_part * whole_cos,
    )


def cmul(a, b):
    return a[0] * b[0] - a[1] * b[1], a[0] * b[1] + a[1] * b[0]


def cadd(a, b):
    return a[0] + b[0], a[1] + b[1]


def csub(a, b):
    return a[0] - b[0], a[1] - b[1]


def split_modes(real_part, imag_part):
    quarter = [
        (real_part[:, QX * p : QX * (p + 1)], imag_part[:, QX * p : QX * (p + 1)])
        for p in range(4)
    ]
    t0, t1 = cadd(quarter[0], quarter[2]), csub(quarter[0], quarter[2])
    t2, t3 = cadd(quarter[1], quarter[3]), csub(quarter[1], quarter[3])
    return [
        cadd(t0, t2),
        (t1[0] + t3[1], t1[1] - t3[0]),
        csub(t0, t2),
        (t1[0] - t3[1], t1[1] + t3[0]),
    ]


def join_modes(back):
    t0, t1 = cadd(back[0], back[2]), csub(back[0], back[2])
    t2, t3 = cadd(back[1], back[3]), csub(back[1], back[3])
    return [
        cadd(t0, t2),
        (t1[0] - t3[1], t1[1] + t3[0]),
        csub(t0, t2),
        (t1[0] + t3[1], t1[1] - t3[0]),
    ]


def x_sweep(count, load, factors, store, left, cells, forward_ref, inverse_ref):
    rows = 16 * count
    for n in range(count):
        mixed = split_modes(*load(n))
        for residue in range(4):
            left[residue, 16 * n : 16 * n + 16, :] = jnp.concatenate(mixed[residue], axis=1)
    for residue in range(4):
        modes = jnp.dot(left[residue, 0:rows, :], forward_ref[residue], preferred_element_type=f32)
        for n in range(count):
            some = modes[16 * n : 16 * n + 16]
            scaled = cmul((some[:, :QX], some[:, QX:]), factors(n)[residue])
            left[residue, 16 * n : 16 * n + 16, :] = jnp.concatenate(scaled, axis=1).astype(bf16)
    for residue in range(4):
        cells[residue, 0:rows, :] = jnp.dot(
            left[residue, 0:rows, :], inverse_ref[residue], preferred_element_type=f32
        )
    for n in range(0, count, 2):
        done = []
        for at in range(2):
            lines = slice(16 * (n + at), 16 * (n + at) + 16)
            some = [cells[residue, lines, :] for residue in range(4)]
            out = join_modes([(one[:, :QX], one[:, QX:]) for one in some])
            done.append([jnp.concatenate([one[part] for one in out], axis=1) for part in range(2)])
        store(n, done)


def main_kernel(
    count_py,
    count_pz,
    z_step,
    z_profile,
    wave_hbm,
    pot_hbm,
    xf_hbm,
    xi_hbm,
    weight_hbm,
    factor_hbm,
    trig_ref,
    z_ref,
    yf_ref,
    yi_ref,
    add_ref,
    turn_ref,
    ytab_ref,
    step_ref,
    packed_ref,
    field_hbm,
    change_hbm,
    wave,
    pot,
    xf,
    xi,
    weight,
    factor,
    fresh_a,
    fresh_b,
    gains,
    grid,
    swept,
    solved,
    planes,
    result,
    left_buf,
    cells_buf,
    sums,
    z_states,
    z_partner,
    z_send,
    z_recv,
    z_back,
    z_chip,
    z_give,
    z_carry,
    y_send,
    y_recv,
    y_back,
    y_carry,
    c_send,
    c_recv,
    change,
    in_sem,
    tab_sem,
    out_sem,
    pair_sems,
    z_sems,
    z_back_sems,
    y_sems,
    c_sems,
):
    me_y = lax.axis_index("py")
    me_z = lax.axis_index("pz")
    core = lax.rem(me_z, 2)
    chip = me_z // 2
    partner = me_z + 1 - 2 * core
    chips = count_pz // 2
    half_z = TILES_Z // 2
    tiles_z = half_z // chips
    mine = core * half_z
    theirs = half_z - mine

    def load(group):
        rows = pl.ds(pl.multiple_of(group * 8, 8), 8)
        return (
            pltpu.make_async_copy(wave_hbm.at[:, :, rows, :], wave.at[group], in_sem.at[0, group]),
            pltpu.make_async_copy(pot_hbm.at[:, rows, :], pot.at[group], in_sem.at[1, group]),
        )

    for group in range(GROUPS):
        for copy in load(group):
            copy.start()
    table_copies = (
        pltpu.make_async_copy(xf_hbm, xf, tab_sem.at[0]),
        pltpu.make_async_copy(xi_hbm, xi, tab_sem.at[1]),
        pltpu.make_async_copy(weight_hbm, weight, tab_sem.at[2]),
        pltpu.make_async_copy(factor_hbm, factor, tab_sem.at[3]),
    )
    for copy in table_copies:
        copy.start()

    barrier = pltpu.get_barrier_semaphore()

    def twin(other):
        return {"pz": other * 2 + core}

    pl.semaphore_signal(barrier, inc=1, device_id={"pz": partner}, device_id_type=MESH)

    @pl.loop(1, chips)
    def _(step):
        pl.semaphore_signal(
            barrier, inc=1, device_id=twin(lax.rem(chip + step, chips)), device_id_type=MESH
        )

    @pl.loop(1, count_py)
    def _(step):
        pl.semaphore_signal(
            barrier, inc=1, device_id={"py": lax.rem(me_y + step, count_py)}, device_id_type=MESH
        )

    for group in range(GROUPS):
        cell = lax.broadcasted_iota(jnp.int32, (8, QX), 0) + (
            me_y * BY + group * 8 - count_py * BY // 2
        )
        beta = cell.astype(f32) * (0.5 * time_step * rotation)
        for residue in range(4):
            rate = trig_ref[2 * residue : 2 * residue + 1] + beta * trig_ref[
                2 * residue + 1 : 2 * residue + 2
            ]
            scale = 1.0 / (1.0 + rate * rate)
            lines = slice(8 * group, 8 * group + 8)
            gains[2 * residue, lines, :] = (1.0 - rate * rate) * scale
            gains[2 * residue + 1, lines, :] = -2.0 * rate * scale

    def kick_group(group, fresh):
        for some in range(BZ // 2):
            rows = slice(2 * some, 2 * some + 2)
            new = kick(wave[group, 0, rows], wave[group, 1, rows], pot[group, rows])
            for part in range(2):
                start = ROWS // 2 * part + 16 * some
                fresh[start : start + 16, :] = new[part].reshape(16, NX).astype(bf16)

    def solve_group(group, fresh):
        for side in range(2):
            lanes = slice(side * NX // 2, (side + 1) * NX // 2)
            rows = jnp.dot(z_ref[...], fresh[:, lanes], preferred_element_type=f32)
            for start in range(0, ROWS, 16):
                grid[group, start : start + 16, lanes] = rows[start : start + 16].astype(bf16)
            states = rows[ROWS:].astype(bf16)
            for quarter in range(2):
                z_states[group * 4 + 2 * side + quarter] = states[
                    :, QX * quarter : QX * (quarter + 1)
                ].reshape(2, 16, QX)

    def pair_out(step):
        return pltpu.make_async_remote_copy(
            src_ref=z_states.at[pl.ds(theirs + 4 * step, 4)],
            dst_ref=z_partner.at[pl.ds(4 * step, 4)],
            send_sem=pair_sems.at[0, step],
            recv_sem=pair_sems.at[1, step],
            device_id={"pz": partner},
            device_id_type=MESH,
        )

    def pair_back():
        return pltpu.make_async_remote_copy(
            src_ref=z_give,
            dst_ref=z_carry.at[pl.ds(mine, half_z)],
            send_sem=pair_sems.at[0, 4],
            recv_sem=pair_sems.at[1, 4],
            device_id={"pz": partner},
            device_id_type=MESH,
        )

    def pair_returned():
        return pltpu.make_async_remote_copy(
            src_ref=z_give,
            dst_ref=z_carry.at[pl.ds(theirs, half_z)],
            send_sem=pair_sems.at[0, 4],
            recv_sem=pair_sems.at[1, 4],
            device_id={"pz": partner},
            device_id_type=MESH,
        )

    def z_out(tile):
        return pltpu.make_async_remote_copy(
            src_ref=z_send.at[tile],
            dst_ref=z_recv.at[chip, lax.rem(tile, tiles_z)],
            send_sem=z_sems.at[0, tile],
            recv_sem=z_sems.at[1, chip * tiles_z + lax.rem(tile, tiles_z)],
            device_id=twin(tile // tiles_z),
            device_id_type=MESH,
        )

    def z_in(step, tile):
        peer = lax.rem(chip + step, chips)
        return pltpu.make_async_remote_copy(
            src_ref=z_send.at[tile],
            dst_ref=z_recv.at[peer, tile],
            send_sem=z_sems.at[0, tile],
            recv_sem=z_sems.at[1, peer * tiles_z + tile],
            device_id=twin(peer),
            device_id_type=MESH,
        )

    def z_return(step):
        peer = lax.rem(chip + step, chips)
        return pltpu.make_async_remote_copy(
            src_ref=z_back.at[peer],
            dst_ref=z_chip.at[pl.ds(chip * tiles_z, tiles_z)],
            send_sem=z_back_sems.at[0, peer],
            recv_sem=z_back_sems.at[1, chip],
            device_id=twin(peer),
            device_id_type=MESH,
        )

    def z_returned(step):
        peer = lax.rem(chip + step, chips)
        return pltpu.make_async_remote_copy(
            src_ref=z_back.at[chip],
            dst_ref=z_chip.at[pl.ds(peer * tiles_z, tiles_z)],
            send_sem=z_back_sems.at[0, chip],
            recv_sem=z_back_sems.at[1, peer],
            device_id=twin(peer),
            device_id_type=MESH,
        )

    lead = core == 0
    block_step = (z_step.real, z_step.imag)
    chip_step = z_step * z_step

    def parts(array):
        array = array.astype(f32)
        return array[0:8], array[8:16]

    def choose(first, second):
        return jnp.where(lead, first[0], second[0]), jnp.where(lead, first[1], second[1])

    def joined(value):
        return jnp.concatenate(value, axis=0).astype(bf16)

    def order(count):
        if count < GROUPS // 2:
            return theirs // 4 + count
        return mine // 4 + lax.rem(count + chip // 4, GROUPS // 2)

    def merge(step):
        pair_out(step).wait_recv()
        for at in range(4):
            tile = step * 4 + at
            own = [parts(z_states[mine + tile, side]) for side in range(2)]
            other = [parts(z_partner[tile, side]) for side in range(2)]
            left = cadd(choose(other[0], own[0]), cmul(choose(own[0], other[0]), block_step))
            right = cadd(choose(own[1], other[1]), cmul(choose(other[1], own[1]), block_step))
            z_send[tile, 0] = joined(left)
            z_send[tile, 1] = joined(right)
        for at in range(4):
            tile = step * 4 + at
            owner = tile // tiles_z

            @pl.when(owner != chip)
            def _():
                z_out(tile).start()

            @pl.when(owner == chip)
            def _():
                z_recv[chip, lax.rem(tile, tiles_z)] = z_send[tile]

    def kicked(count, fresh):
        for copy in load(order(count)):
            copy.wait()
        kick_group(order(count), fresh)

    fresh = (fresh_a, fresh_b)
    kicked(0, fresh[0])
    for count in range(GROUPS):
        if count + 1 < GROUPS:
            for copy in load(order(count + 1)):
                copy.wait()
        solve_group(order(count), fresh[count % 2])
        if count + 1 < GROUPS:
            kick_group(order(count + 1), fresh[(count + 1) % 2])
        if count == 0:
            pl.semaphore_wait(barrier, chips + count_py - 1)
        if count < GROUPS // 2:
            pair_out(count).start()
        else:
            merge(order(count) - mine // 4)

    for copy in table_copies:
        copy.wait()

    def sweep_field():
        def fetch(n):
            group, row = n // 8, n % 8 * BZ
            return tuple(
                grid[group, start : start + BZ, :] for start in (row, row + ROWS // 2)
            )

        def gain(n):
            line = slice(n, n + 1)
            return [
                (gains[2 * residue, line, :], gains[2 * residue + 1, line, :])
                for residue in range(4)
            ]

        def put(n, done):
            for at in range(2):
                start = (n + at) * BZ
                for part in range(2):
                    swept[part, start : start + BZ, :] = done[at][part].astype(bf16)

        x_sweep(BY, fetch, gain, put, left_buf, cells_buf, xf, xi)

    steps_y = [(step_ref[2 * n : 2 * n + 1], step_ref[2 * n + 1 : 2 * n + 2]) for n in range(4)]
    forward_step, backward_step, turn_step, whole_gain = steps_y

    def y_rows(cell):
        return pl.ds(pl.multiple_of(cell * BZ, BZ), BZ)

    def save(rows, value):
        for part in range(2):
            for quarter in range(4):
                solved[part, quarter, rows, :] = value[part][
                    :, QX * quarter : QX * (quarter + 1)
                ]

    def y_forward():
        def advance(cell, totals):
            total, other = totals
            rows = y_rows(cell)
            value = tuple(swept[part, rows, :].astype(f32) for part in range(2))
            total = cadd(value, cmul(total, forward_step))
            save(rows, total)
            share = tuple(weight[2 + part, pl.ds(cell, 1), :] for part in range(2))
            return total, cadd(other, cmul(value, share))

        zero = jnp.zeros((BZ, NX), f32)
        return lax.fori_loop(0, BY, advance, ((zero, zero), (zero, zero)), unroll=4)

    def y_backward(first, last, total):
        def advance(count, total):
            rows = y_rows(BY - 1 - count)
            value = tuple(
                jnp.concatenate([solved[part, quarter, rows, :] for quarter in range(4)], axis=1)
                for part in range(2)
            )
            total = cadd(value, cmul(total, backward_step))
            out = cmul(total, whole_gain)
            save(rows, [out[part] - swept[part, rows, :].astype(f32) for part in range(2)])
            return total

        return lax.fori_loop(first, last, advance, total, unroll=4)

    def y_states(count):
        @pl.loop(0, count)
        def _(at):
            for quarter in range(4):
                lanes = slice(QX * quarter, QX * (quarter + 1))
                total = [[0.0, 0.0], [0.0, 0.0]]
                for start in range(0, BY, 16):
                    rows = slice(start, start + 16)
                    value = [planes[part, at, rows, lanes].astype(f32) for part in range(2)]
                    for side in range(2):
                        some = cmul(
                            value, (weight[2 * side, rows, lanes], weight[2 * side + 1, rows, lanes])
                        )
                        for part in range(2):
                            total[side][part] += some[part][0:8] + some[part][8:16]
                for side in range(2):
                    for part in range(2):
                        row = pl.multiple_of((side * 2 + part) * 16 + at * 8, 8)
                        sums[pl.ds(row, 8), lanes] = total[side][part]

        rows = 0.0
        for quarter in range(4):
            some = sums[:, QX * quarter : QX * (quarter + 1)].astype(bf16)
            rows += jnp.dot(add_ref[quarter], some, preferred_element_type=f32)
        return rows.astype(bf16)

    def y_periodic(plane):
        for side in range(2):
            lanes = slice(side * NX // 2, (side + 1) * NX // 2)
            block = jnp.concatenate([planes[part, plane, :, lanes] for part in range(2)], axis=0)
            modes = jnp.dot(yf_ref[...], block, preferred_element_type=f32)
            scaled = [
                cmul(
                    (modes[some : some + 32], modes[BY + some : BY + some + 32]),
                    (factor[0, some : some + 32, lanes], factor[1, some : some + 32, lanes]),
                )
                for some in range(0, BY, 32)
            ]
            block = jnp.concatenate(
                [one[part].astype(bf16) for part in range(2) for one in scaled], axis=0
            )
            cells = jnp.dot(yi_ref[...], block, preferred_element_type=f32).astype(bf16)
            for part in range(2):
                planes[part, plane, :, lanes] = cells[part * BY : (part + 1) * BY]

    class Exchange:
        def __init__(self, send, recv, back, carry, sems, tiles):
            self.send, self.recv, self.back, self.carry = send, recv, back, carry
            self.sems, self.tiles = sems, tiles

        def mine(self):
            return pl.ds(me_y * self.tiles, self.tiles)

        def out(self, peer):
            return pltpu.make_async_remote_copy(
                src_ref=self.send.at[pl.ds(peer * self.tiles, self.tiles)],
                dst_ref=self.recv.at[me_y],
                send_sem=self.sems.at[0, peer],
                recv_sem=self.sems.at[1, me_y],
                device_id={"py": peer},
                device_id_type=MESH,
            )

        def arrived(self, peer):
            return pltpu.make_async_remote_copy(
                src_ref=self.send.at[self.mine()],
                dst_ref=self.recv.at[peer],
                send_sem=self.sems.at[0, me_y],
                recv_sem=self.sems.at[1, peer],
                device_id={"py": peer},
                device_id_type=MESH,
            )

        def give(self, peer):
            return pltpu.make_async_remote_copy(
                src_ref=self.back.at[peer],
                dst_ref=self.carry.at[self.mine()],
                send_sem=self.sems.at[2, peer],
                recv_sem=self.sems.at[3, me_y],
                device_id={"py": peer},
                device_id_type=MESH,
            )

        def given(self, peer):
            return pltpu.make_async_remote_copy(
                src_ref=self.back.at[me_y],
                dst_ref=self.carry.at[pl.ds(peer * self.tiles, self.tiles)],
                send_sem=self.sems.at[2, me_y],
                recv_sem=self.sems.at[3, peer],
                device_id={"py": peer},
                device_id_type=MESH,
            )

        def post(self):
            @pl.loop(1, count_py)
            def _(step):
                self.out(lax.rem(me_y + step, count_py)).start()

        def answer(self):
            self.recv[me_y] = self.send[self.mine()]

            @pl.loop(1, count_py)
            def _(step):
                self.arrived(lax.rem(me_y + step, count_py)).wait_recv()

            for tile in range(self.tiles):
                solve_tile(self.recv, self.back, tile, lax.rem(me_y * self.tiles + tile, 4))

            @pl.loop(1, count_py)
            def _(step):
                self.give(lax.rem(me_y + step, count_py)).start()

            self.carry[self.mine()] = self.back[me_y]

        def receive(self):
            @pl.loop(1, count_py)
            def _(step):
                self.given(lax.rem(me_y + step, count_py)).wait_recv()

        def close(self):
            @pl.loop(1, count_py)
            def _(step):
                peer = lax.rem(me_y + step, count_py)
                self.out(peer).wait_send()
                self.give(peer).wait_send()

        def rows(self, tiles):
            return [self.carry[tile].reshape(CARRY, QX) for tile in tiles]

    def solve_tile(recv, back, tile, quarter):
        table = ytab_ref[quarter]
        value = [(table[2 * n : 2 * n + 1], table[2 * n + 1 : 2 * n + 2]) for n in range(8)]
        whole1, whole2, _, _, wrap1, wrap2, out1, out2 = value
        left_state = [parts(recv[block, tile, 0]) for block in range(count_py)]
        right_state = [parts(recv[block, tile, 1]) for block in range(count_py)]
        left, right = left_state[0], right_state[count_py - 1]
        for block in range(1, count_py):
            left = cadd(left_state[block], cmul(left, whole1))
            right = cadd(right_state[count_py - 1 - block], cmul(right, whole2))
        left, right = cmul(left, wrap1), cmul(right, wrap2)
        for block in range(count_py):
            other = count_py - 1 - block
            back[block, tile, 0] = joined(cmul(left, out1))
            back[other, tile, 1] = joined(cmul(right, out2))
            left = cadd(left_state[block], cmul(left, whole1))
            right = cadd(right_state[other], cmul(right, whole2))

    planes_y = Exchange(y_send, y_recv, y_back, y_carry, y_sems, TILES_Y // count_py)
    def carry_out(step):
        return pltpu.make_async_remote_copy(
            src_ref=c_send,
            dst_ref=c_recv.at[me_y],
            send_sem=c_sems.at[0, lax.rem(me_y + step, count_py)],
            recv_sem=c_sems.at[1, me_y],
            device_id={"py": lax.rem(me_y + step, count_py)},
            device_id_type=MESH,
        )

    def carry_in(step):
        peer = lax.rem(me_y + step, count_py)
        return pltpu.make_async_remote_copy(
            src_ref=c_send,
            dst_ref=c_recv.at[peer],
            send_sem=c_sems.at[0, me_y],
            recv_sem=c_sems.at[1, peer],
            device_id={"py": peer},
            device_id_type=MESH,
        )

    def carry_solve():
        value = [(packed_ref[2 * n], packed_ref[2 * n + 1]) for n in range(8)]
        whole1, whole2, own1, own2, wrap1, wrap2, out1, out2 = value
        own = [parts(c_send[side]) for side in range(2)]
        left, right = own
        for step in range(1, count_py):
            left = cadd(parts(c_recv[lax.rem(me_y + step, count_py), 0]), cmul(left, whole1))
            back = lax.rem(me_y + count_py - step, count_py)
            right = cadd(parts(c_recv[back, 1]), cmul(right, whole2))
        left = csub(cmul(left, wrap1), cmul(own[0], own1))
        right = csub(cmul(right, wrap2), cmul(own[1], own2))
        return jnp.concatenate([joined(cmul(left, out1)), joined(cmul(right, out2))], axis=0)

    def post_planes(states):
        for half in range(2):
            lines = slice(8 * half, 8 * half + 8)
            for quarter in range(4):
                lanes = slice(QX * quarter, QX * (quarter + 1))
                for side in range(2):
                    y_send[half * 4 + quarter, side] = joined(
                        [states[side][part][lines, lanes] for part in range(2)]
                    )
        planes_y.post()

    sweep_field()

    @pl.loop(1, chips)
    def _(step):
        for tile in range(tiles_z):
            z_in(step, tile).wait_recv()

    for tile in range(tiles_z):

        def state(block, side):
            return parts(z_recv[block, tile, side])

        def advance(total, value):
            return cadd(cmul(total, (chip_step.real, chip_step.imag)), value)

        def gather(step, carry):
            left, right = carry
            return (
                advance(left, state(step, 0)),
                advance(right, state(chips - 1 - step, 1)),
            )

        zero = (jnp.zeros((8, QX), f32), jnp.zeros((8, QX), f32))
        left, right = lax.fori_loop(0, chips, gather, (zero, zero), unroll=8)
        wrap = 1 / (1 - chip_step**chips)
        left = cmul(left, (wrap.real, wrap.imag))
        right = cmul(right, (wrap.real, wrap.imag))

        def hand_out(step, carry):
            left, right = carry
            last = chips - 1 - step
            z_back[step, tile, 0] = joined(left)
            z_back[last, tile, 1] = joined(right)
            return advance(left, state(step, 0)), advance(right, state(last, 1))

        lax.fori_loop(0, chips, hand_out, (left, right), unroll=8)

    @pl.loop(1, chips)
    def _(step):
        z_return(step).start()

    z_chip[pl.ds(chip * tiles_z, tiles_z)] = z_back[chip]

    forward_state, backward_state = y_forward()
    post_planes((forward_state, backward_state))
    back_total = y_backward(0, BY // 2, cmul(forward_state, turn_step))

    @pl.loop(1, chips)
    def _(step):
        z_returned(step).wait_recv()

    def split_carry(tile, _):
        own = [parts(z_states[mine + tile, side]) for side in range(2)]
        other = [parts(z_partner[tile, side]) for side in range(2)]
        whole = [parts(z_chip[tile, side]) for side in range(2)]
        inner_left = cadd(choose(own[0], other[0]), cmul(whole[0], block_step))
        inner_right = cadd(choose(other[1], own[1]), cmul(whole[1], block_step))
        z_give[tile, 0] = joined(choose(inner_left, whole[0]))
        z_give[tile, 1] = joined(choose(whole[1], inner_right))
        z_carry[mine + tile, 0] = joined(choose(whole[0], inner_left))
        z_carry[mine + tile, 1] = joined(choose(inner_right, whole[1]))
        return 0

    lax.fori_loop(0, half_z, split_carry, 0, unroll=4)
    pair_back().start()

    def carry_planes(first):
        def fetch(n):
            sides = [
                jnp.concatenate(
                    [z_carry[(first + n) * 4 + quarter, side] for quarter in range(4)], axis=1
                ).astype(f32)
                for side in range(2)
            ]
            return tuple(
                jnp.concatenate(
                    [side[8 * part : 8 * part + 8] for side in sides], axis=0
                ).astype(bf16)
                for part in range(2)
            )

        def gain(n):
            lines = pl.ds(pl.multiple_of((first + n) * 8, 8), 8)
            return [
                tuple(
                    jnp.concatenate([gains[2 * residue + part, lines, :]] * 2, axis=0)
                    for part in range(2)
                )
                for residue in range(4)
            ]

        def put(n, done):
            rows = pl.ds(pl.multiple_of((first + n) * 8, 16), 16)
            for side in range(2):
                lines = slice(8 * side, 8 * side + 8)
                for part in range(2):
                    planes[part, side, rows, :] = jnp.concatenate(
                        [done[at][part][lines] for at in range(2)], axis=0
                    ).astype(bf16)

        x_sweep(GROUPS // 2, fetch, gain, put, left_buf, cells_buf, xf, xi)

    carry_planes(mine // 4)
    planes_y.answer()
    pair_returned().wait_recv()
    carry_planes(theirs // 4)
    c_send[...] = y_states(2).reshape(2, 16, QX)

    @pl.loop(1, count_py)
    def _(step):
        carry_out(step).start()

    y_backward(BY // 2, BY, back_total)
    y_periodic(0)
    y_periodic(1)

    def store(pair):
        rows = pl.ds(pl.multiple_of(pair * 16, 16), 16)
        return pltpu.make_async_copy(
            result.at[:, :, rows, :], field_hbm.at[:, :, rows, :], out_sem.at[pair]
        )

    @pl.loop(0, BY // 16)
    def _(pair):
        rows = pl.ds(pl.multiple_of(pair * 16, 16), 16)
        for quarter in range(4):
            lanes = slice(QX * quarter, QX * (quarter + 1))
            left, right = [
                tuple(planes[part, one, rows, lanes] for part in range(2)) for one in range(2)
            ]
            for plane in range(BZ):
                first, second = (complex(one) for one in z_profile[plane])
                lines = pl.ds(pair * 16 * BZ + plane, 16, stride=BZ)
                value = tuple(solved[part, quarter, lines, :].astype(bf16) for part in range(2))
                value = cadd(value, cmul(left, (first.real, first.imag)))
                value = cadd(value, cmul(right, (second.real, second.imag)))
                for part in range(2):
                    result[part, plane, rows, lanes] = value[part]
        store(pair).start()

    @pl.loop(0, half_z)
    def _(tile):
        @pl.when(tile // tiles_z != chip)
        def _():
            z_out(tile).wait_send()

    @pl.loop(1, chips)
    def _(step):
        z_return(step).wait_send()

    @pl.loop(0, GROUPS // 2)
    def _(step):
        pair_out(step).wait_send()

    pair_back().wait_send()

    @pl.loop(1, count_py)
    def _(step):
        carry_in(step).wait_recv()

    carried = carry_solve()
    planes_y.receive()
    for quarter in range(4):
        rows = planes_y.rows((quarter, 4 + quarter)) + [carried]
        change[:, :, QX * quarter : QX * (quarter + 1)] = jnp.dot(
            turn_ref[quarter], jnp.concatenate(rows, axis=0), preferred_element_type=f32
        ).reshape(BZ, 8, QX)
    last = pltpu.make_async_copy(change, change_hbm, out_sem.at[GROUPS // 2])
    last.start()

    planes_y.close()

    @pl.loop(1, count_py)
    def _(step):
        carry_out(step).wait_send()


    @pl.loop(0, GROUPS // 2)
    def _(pair):
        store(pair).wait()

    last.wait()


PLANES = 2


def finish_kernel(
    field_hbm,
    change_hbm,
    pot_hbm,
    table_hbm,
    out_hbm,
    field,
    change,
    pot,
    table,
    out,
    in_sem,
    tab_sem,
    out_sem,
):
    steps = BZ // PLANES

    def load(step):
        planes = pl.ds(step * PLANES, PLANES)
        return (
            pltpu.make_async_copy(field_hbm.at[:, planes], field.at[:, planes], in_sem.at[0, step]),
            pltpu.make_async_copy(pot_hbm.at[planes], pot.at[planes], in_sem.at[1, step]),
        )

    def save(step):
        planes = pl.ds(step * PLANES, PLANES)
        return pltpu.make_async_copy(out.at[:, planes], out_hbm.at[:, planes], out_sem.at[step])

    tables = (
        pltpu.make_async_copy(change_hbm, change, tab_sem.at[0]),
        pltpu.make_async_copy(table_hbm, table, tab_sem.at[1]),
    )
    for copy in tables:
        copy.start()
    for step in range(steps):
        for copy in load(step):
            copy.start()
    for copy in tables:
        copy.wait()

    def finish(at, lanes):
        ends = [change[at, row : row + 1, lanes].astype(bf16) for row in range(4)]
        for start in range(0, BY, 16):
            rows = slice(start, start + 16)
            value = tuple(field[part, at, rows, lanes] for part in range(2))
            for side in range(2):
                profile = (table[2 * side, rows, lanes], table[2 * side + 1, rows, lanes])
                value = cadd(value, cmul(profile, (ends[2 * side], ends[2 * side + 1])))
            new = kick(value[0].astype(f32), value[1].astype(f32), pot[at, rows, lanes])
            for part in range(2):
                out[part, at, rows, lanes] = new[part]

    @pl.loop(0, steps)
    def _(step):
        for copy in load(step):
            copy.wait()
        for one in range(PLANES):
            for side in range(2):
                finish(step * PLANES + one, slice(side * NX // 2, (side + 1) * NX // 2))
        save(step).start()

    @pl.loop(0, steps)
    def _(step):
        save(step).wait()


def shards(count_py, count_pz, wavefunction, potential):
    forward_x, inverse_x, trig = x_tables()
    z_rows, turn, z_profile, z_step = z_tables()
    forward_y, inverse_y, factor, weight, homogeneous, steps_y, add, y_table, packed = y_tables(count_py)

    def low(array):
        return jnp.asarray(array.astype(np.float32)).astype(bf16)

    def full(array):
        return jnp.asarray(array.astype(np.float32))

    chips = count_pz // 2
    tiles_z = TILES_Z // 2 // chips
    tiles_y = TILES_Y // count_py
    anywhere = pl.BlockSpec(memory_space=pl.ANY)
    inside = pl.BlockSpec(memory_space=pltpu.VMEM)
    field, change = pl.pallas_call(
        functools.partial(main_kernel, count_py, count_pz, z_step, z_profile),
        out_shape=(
            pltpu.VMEM((2, BZ, BY, NX), bf16),
            pltpu.VMEM((BZ, 8, NX), f32),
        ),
        in_specs=[anywhere] * 6 + [inside] * 9,
        out_specs=(anywhere, anywhere),
        scratch_shapes=[
            pltpu.VMEM((GROUPS, 2, BZ, 8, NX), f32),
            pltpu.VMEM((GROUPS, BZ, 8, NX), f32),
            pltpu.VMEM((4, 2 * QX, 2 * QX), bf16),
            pltpu.VMEM((4, 2 * QX, 2 * QX), bf16),
            pltpu.VMEM(weight.shape, f32),
            pltpu.VMEM(factor.shape, f32),
            pltpu.VMEM((ROWS, NX), bf16),
            pltpu.VMEM((ROWS, NX), bf16),
            pltpu.VMEM((8, BY, QX), f32),
            pltpu.VMEM((GROUPS, ROWS, NX), bf16),
            pltpu.VMEM((2, BY * BZ, NX), bf16),
            pltpu.VMEM((2, 4, BY * BZ, QX), f32),
            pltpu.VMEM((2, 2, BY, NX), bf16),
            pltpu.VMEM((2, BZ, BY, NX), bf16),
            pltpu.VMEM((4, BY * BZ, 2 * QX), bf16),
            pltpu.VMEM((4, BY * BZ, 2 * QX), f32),
            pltpu.VMEM((64, NX), f32),
            pltpu.VMEM((TILES_Z, 2, 16, QX), bf16),
            pltpu.VMEM((TILES_Z // 2, 2, 16, QX), bf16),
            pltpu.VMEM((TILES_Z // 2, 2, 16, QX), bf16),
            pltpu.VMEM((chips, tiles_z, 2, 16, QX), bf16),
            pltpu.VMEM((chips, tiles_z, 2, 16, QX), bf16),
            pltpu.VMEM((TILES_Z // 2, 2, 16, QX), bf16),
            pltpu.VMEM((TILES_Z // 2, 2, 16, QX), bf16),
            pltpu.VMEM((TILES_Z, 2, 16, QX), bf16),
            pltpu.VMEM((TILES_Y, 2, 16, QX), bf16),
            pltpu.VMEM((count_py, tiles_y, 2, 16, QX), bf16),
            pltpu.VMEM((count_py, tiles_y, 2, 16, QX), bf16),
            pltpu.VMEM((TILES_Y, 2, 16, QX), bf16),
            pltpu.VMEM((2, 16, QX), bf16),
            pltpu.VMEM((count_py, 2, 16, QX), bf16),
            pltpu.VMEM((BZ, 8, NX), f32),
            pltpu.SemaphoreType.DMA((2, GROUPS)),
            pltpu.SemaphoreType.DMA((4,)),
            pltpu.SemaphoreType.DMA((GROUPS // 2 + 1,)),
            pltpu.SemaphoreType.DMA((2, 5)),
            pltpu.SemaphoreType.DMA((2, TILES_Z // 2)),
            pltpu.SemaphoreType.DMA((2, chips)),
            pltpu.SemaphoreType.DMA((4, count_py)),
            pltpu.SemaphoreType.DMA((2, count_py)),
        ],
        compiler_params=pltpu.CompilerParams(
            collective_id=0, has_side_effects=True, vmem_limit_bytes=57 * 2**20
        ),
        cost_estimate=pl.CostEstimate(
            flops=3_000_000_000, bytes_accessed=10_000_000, transcendentals=0
        ),
        name="sweeps",
    )(
        wavefunction,
        potential,
        low(forward_x),
        low(inverse_x),
        full(weight),
        full(factor),
        full(trig),
        low(z_rows),
        low(forward_y),
        low(inverse_y),
        low(add),
        low(turn),
        full(y_table),
        full(steps_y),
        full(packed),
    )
    return pl.pallas_call(
        finish_kernel,
        out_shape=jax.ShapeDtypeStruct((2, BZ, BY, NX), f32),
        in_specs=[anywhere] * 4,
        out_specs=anywhere,
        scratch_shapes=[
            pltpu.VMEM((2, BZ, BY, NX), bf16),
            pltpu.VMEM((BZ, 8, NX), f32),
            pltpu.VMEM((BZ, BY, NX), f32),
            pltpu.VMEM(homogeneous.shape, bf16),
            pltpu.VMEM((2, BZ, BY, NX), f32),
            pltpu.SemaphoreType.DMA((2, BZ // PLANES)),
            pltpu.SemaphoreType.DMA((2,)),
            pltpu.SemaphoreType.DMA((BZ // PLANES,)),
        ],
        compiler_params=pltpu.CompilerParams(vmem_limit_bytes=16 * 2**20),
        cost_estimate=pl.CostEstimate(
            flops=800_000_000, bytes_accessed=9_000_000, transcendentals=0
        ),
        name="finish",
    )(field, change, potential, low(homogeneous))


def solution(mesh):
    return jax.shard_map(
        functools.partial(shards, mesh.shape["py"], mesh.shape["pz"]),
        mesh=mesh,
        in_specs=(P(None, "pz", "py", None), P("pz", "py", None)),
        out_specs=P(None, "pz", "py", None),
        check_vma=False,
    )
```

```python
import functools

import jax
import jax.numpy as jnp
import numpy as np
from jax import lax
from jax.experimental import pallas as pl
from jax.experimental.pallas import tpu as pltpu
from jax.sharding import PartitionSpec as P

time_step = 0.005
rotation = 0.9
coupling = 100.0
grid_spacing = 0.05

NX = 512
BY = 64
BZ = 16
QX = 128
GROUPS = BY // 8
TILES_Z = GROUPS * 4
TILES_Y = 8
ROWS = 2 * BZ * 8
CARRY = 32

MESH = pl.DeviceIdType.MESH
f32 = jnp.float32
bf16 = jnp.bfloat16


def line_roots(beta):
    beta = np.asarray(beta, np.float64)
    half = (beta - 1j) / 2
    spread = np.sqrt((1 + 1j) ** 2 - (beta - 1j) * (-beta - 1j))
    first = (-(1 + 1j) + spread) / (beta - 1j)
    second = (-(1 + 1j) - spread) / (beta - 1j)
    swap = np.abs(first) > np.abs(second)
    inner = np.where(swap, second, first)
    outer = np.where(swap, first, second)
    return inner, 1 / outer, half * (inner - outer)


def real_form(matrix):
    return np.stack(
        [
            np.stack([matrix.real, -matrix.imag], 1),
            np.stack([matrix.imag, matrix.real], 1),
        ],
        0,
    )


def x_tables():
    forward, inverse = [], []
    cells = np.arange(QX)
    for residue in range(4):
        modes = 4 * np.arange(QX) + residue
        angles = 2 * np.pi * ((cells[:, None] * modes[None, :]) % NX) / NX
        cosines, sines = np.cos(angles), np.sin(angles)
        forward.append(np.block([[cosines, -sines], [sines, cosines]]))
        inverse.append(np.block([[cosines.T, sines.T], [-sines.T, cosines.T]]) / NX)
    modes = 4 * np.arange(QX)[None, :] + np.arange(4)[:, None]
    theta = 2 * np.pi * modes / NX
    trig = np.stack([1 - np.cos(theta), np.sin(theta)], 1).reshape(8, QX)
    return np.stack(forward), np.stack(inverse), trig


def z_tables():
    lam, _, scale = line_roots(0.0)
    lam, scale = complex(lam), complex(scale)
    cells = np.arange(BZ)
    local = (2 / scale) * lam ** np.abs(cells[:, None] - cells[None, :]) - np.eye(BZ)
    carry = (2 / scale) * np.stack([lam ** (cells + 1), lam ** (BZ - cells)], 1)
    states = np.stack([lam ** (BZ - 1 - cells), lam**cells], 0)
    eye = np.eye(8)
    apply_field = np.einsum("azbw,ij->aizbwj", real_form(local), eye).reshape(ROWS, ROWS)
    state_rows = np.einsum("asbz,ij->saibzj", real_form(states), eye).reshape(CARRY, ROWS)
    turn = np.zeros((4, BZ, 8, 3, 4, 8))
    fields, carries = real_form(np.eye(BZ).astype(complex)), real_form(carry)
    for end in range(2):
        for out in range(2):
            for part in range(2):
                row, column = 2 * end + out, 2 * end + part
                for half in range(2):
                    turn[:, :, row, half, column, :] = fields[
                        out, :, part, 8 * half : 8 * half + 8
                    ]
                for quarter in range(4):
                    lines = slice(2 * quarter, 2 * quarter + 2)
                    turn[quarter, :, row, 2, column, lines] = carries[out, :, part, :]
    turn = turn.reshape(4, BZ * 8, 3 * CARRY)
    return np.concatenate([apply_field, state_rows], 0), turn, carry, lam**BZ


def y_tables(blocks):
    cells = np.arange(BY)
    angles = 2 * np.pi * ((cells[:, None] * cells[None, :]) % BY) / BY
    modes = np.exp(-1j * angles)
    forward = real_form(modes).reshape(2 * BY, 2 * BY)
    inverse = real_form(np.conj(modes) / BY).reshape(2 * BY, 2 * BY)
    beta = -0.5 * time_step * rotation * (np.arange(NX) - NX // 2)
    theta = 2 * np.pi * cells / BY
    rate = (1 - np.cos(theta))[:, None] + np.sin(theta)[:, None] * beta[None, :]
    factor = (1 - 1j * rate) / (1 + 1j * rate)
    lam1, lam2, scale = line_roots(beta)
    whole1, whole2 = lam1**BY, lam2**BY
    rows = [
        whole1,
        whole2,
        1 / (1 - whole1),
        1 / (1 - whole2),
        1 / (1 - whole1**blocks),
        1 / (1 - whole2**blocks),
        2 * lam1 / scale,
        2 * lam2 / scale,
    ]
    apart = 1 - lam1 * lam2
    steps = [lam1, lam2, lam1 / apart, 2 * apart / scale]
    table = np.stack([part for row in rows for part in (row.real, row.imag)])
    down, up = np.arange(BY)[:, None], BY - 1 - np.arange(BY)[:, None]
    states = [lam1**up, lam2**down]
    homogeneous = [lam1**down, lam2**up]
    add = np.zeros((4, 4, 8, 4, 2, 8))
    for quarter in range(4):
        for plane in range(2):
            for part in range(4):
                add[quarter, part, 2 * quarter + plane, part, plane, :] = 1
    add = add.reshape(4, CARRY, 64)
    table = table.reshape(len(table), 4, QX)
    packed = np.repeat(table, 2, axis=1)
    table = table.transpose(1, 0, 2)

    def parts(values):
        return np.stack([part for value in values for part in (value.real, value.imag)])

    return (
        forward,
        inverse,
        parts([factor]),
        parts(states),
        parts(homogeneous),
        parts(steps),
        add,
        table,
        packed,
    )


def kick(real_part, imag_part, potential):
    turn = -0.5 * time_step / (2 * np.pi)
    density = real_part * real_part + imag_part * imag_part
    turns = potential * turn + density * (turn * coupling)
    rest = turns - jnp.round(turns)
    square = rest * rest
    sine = rest * (
        4.4428679 + square * (-7.30744342 + square * (3.59478806 + square * -0.78437396))
    )
    cosine = 1.4142135 + square * (
        -6.97885099 + square * (5.73946123 + square * (-1.88356328 + square * 0.31069871))
    )
    whole_cos = 1.0 - sine * sine
    whole_sin = sine * cosine
    return (
        real_part * whole_cos - imag_part * whole_sin,
        real_part * whole_sin + imag_part * whole_cos,
    )


def cmul(a, b):
    return a[0] * b[0] - a[1] * b[1], a[0] * b[1] + a[1] * b[0]


def cadd(a, b):
    return a[0] + b[0], a[1] + b[1]


def csub(a, b):
    return a[0] - b[0], a[1] - b[1]


def split_modes(real_part, imag_part):
    quarter = [
        (real_part[:, QX * p : QX * (p + 1)], imag_part[:, QX * p : QX * (p + 1)])
        for p in range(4)
    ]
    t0, t1 = cadd(quarter[0], quarter[2]), csub(quarter[0], quarter[2])
    t2, t3 = cadd(quarter[1], quarter[3]), csub(quarter[1], quarter[3])
    return [
        cadd(t0, t2),
        (t1[0] + t3[1], t1[1] - t3[0]),
        csub(t0, t2),
        (t1[0] - t3[1], t1[1] + t3[0]),
    ]


def join_modes(back):
    t0, t1 = cadd(back[0], back[2]), csub(back[0], back[2])
    t2, t3 = cadd(back[1], back[3]), csub(back[1], back[3])
    return [
        cadd(t0, t2),
        (t1[0] - t3[1], t1[1] + t3[0]),
        csub(t0, t2),
        (t1[0] + t3[1], t1[1] - t3[0]),
    ]


def x_sweep(count, load, factors, store, left, cells, forward_ref, inverse_ref):
    rows = 16 * count
    for n in range(count):
        mixed = split_modes(*load(n))
        for residue in range(4):
            left[residue, 16 * n : 16 * n + 16, :] = jnp.concatenate(mixed[residue], axis=1)
    for residue in range(4):
        modes = jnp.dot(left[residue, 0:rows, :], forward_ref[residue], preferred_element_type=f32)
        for n in range(count):
            some = modes[16 * n : 16 * n + 16]
            scaled = cmul((some[:, :QX], some[:, QX:]), factors(n)[residue])
            left[residue, 16 * n : 16 * n + 16, :] = jnp.concatenate(scaled, axis=1).astype(bf16)
    for residue in range(4):
        cells[residue, 0:rows, :] = jnp.dot(
            left[residue, 0:rows, :], inverse_ref[residue], preferred_element_type=f32
        )
    for n in range(0, count, 2):
        done = []
        for at in range(2):
            lines = slice(16 * (n + at), 16 * (n + at) + 16)
            some = [cells[residue, lines, :] for residue in range(4)]
            out = join_modes([(one[:, :QX], one[:, QX:]) for one in some])
            done.append([jnp.concatenate([one[part] for one in out], axis=1) for part in range(2)])
        store(n, done)


def main_kernel(
    count_py,
    count_pz,
    z_step,
    z_profile,
    wave_hbm,
    pot_hbm,
    xf_hbm,
    xi_hbm,
    weight_hbm,
    factor_hbm,
    trig_ref,
    z_ref,
    yf_ref,
    yi_ref,
    add_ref,
    turn_ref,
    ytab_ref,
    step_ref,
    packed_ref,
    field_hbm,
    change_hbm,
    wave,
    pot,
    xf,
    xi,
    weight,
    factor,
    fresh_a,
    fresh_b,
    gains,
    grid,
    swept,
    solved,
    planes,
    result,
    left_buf,
    cells_buf,
    sums,
    z_states,
    z_partner,
    z_send,
    z_recv,
    z_back,
    z_chip,
    z_give,
    z_carry,
    y_send,
    y_recv,
    y_back,
    y_carry,
    c_send,
    c_recv,
    change,
    in_sem,
    tab_sem,
    out_sem,
    pair_sems,
    z_sems,
    z_back_sems,
    y_sems,
    c_sems,
):
    me_y = lax.axis_index("py")
    me_z = lax.axis_index("pz")
    core = lax.rem(me_z, 2)
    chip = me_z // 2
    partner = me_z + 1 - 2 * core
    chips = count_pz // 2
    half_z = TILES_Z // 2
    tiles_z = half_z // chips
    mine = core * half_z
    theirs = half_z - mine

    def load(group):
        rows = pl.ds(pl.multiple_of(group * 8, 8), 8)
        return (
            pltpu.make_async_copy(wave_hbm.at[:, :, rows, :], wave.at[group], in_sem.at[0, group]),
            pltpu.make_async_copy(pot_hbm.at[:, rows, :], pot.at[group], in_sem.at[1, group]),
        )

    for group in range(GROUPS):
        for copy in load(group):
            copy.start()
    table_copies = (
        pltpu.make_async_copy(xf_hbm, xf, tab_sem.at[0]),
        pltpu.make_async_copy(xi_hbm, xi, tab_sem.at[1]),
        pltpu.make_async_copy(weight_hbm, weight, tab_sem.at[2]),
        pltpu.make_async_copy(factor_hbm, factor, tab_sem.at[3]),
    )
    for copy in table_copies:
        copy.start()

    barrier = pltpu.get_barrier_semaphore()

    def twin(other):
        return {"pz": other * 2 + core}

    pl.semaphore_signal(barrier, inc=1, device_id={"pz": partner}, device_id_type=MESH)

    @pl.loop(1, chips)
    def _(step):
        pl.semaphore_signal(
            barrier, inc=1, device_id=twin(lax.rem(chip + step, chips)), device_id_type=MESH
        )

    @pl.loop(1, count_py)
    def _(step):
        pl.semaphore_signal(
            barrier, inc=1, device_id={"py": lax.rem(me_y + step, count_py)}, device_id_type=MESH
        )

    for group in range(GROUPS):
        cell = lax.broadcasted_iota(jnp.int32, (8, QX), 0) + (
            me_y * BY + group * 8 - count_py * BY // 2
        )
        beta = cell.astype(f32) * (0.5 * time_step * rotation)
        for residue in range(4):
            rate = trig_ref[2 * residue : 2 * residue + 1] + beta * trig_ref[
                2 * residue + 1 : 2 * residue + 2
            ]
            scale = 1.0 / (1.0 + rate * rate)
            lines = slice(8 * group, 8 * group + 8)
            gains[2 * residue, lines, :] = (1.0 - rate * rate) * scale
            gains[2 * residue + 1, lines, :] = -2.0 * rate * scale

    def kick_group(group, fresh):
        for some in range(BZ // 2):
            rows = slice(2 * some, 2 * some + 2)
            new = kick(wave[group, 0, rows], wave[group, 1, rows], pot[group, rows])
            for part in range(2):
                start = ROWS // 2 * part + 16 * some
                fresh[start : start + 16, :] = new[part].reshape(16, NX).astype(bf16)

    def solve_group(group, fresh):
        for side in range(2):
            lanes = slice(side * NX // 2, (side + 1) * NX // 2)
            rows = jnp.dot(z_ref[...], fresh[:, lanes], preferred_element_type=f32)
            for start in range(0, ROWS, 16):
                grid[group, start : start + 16, lanes] = rows[start : start + 16].astype(bf16)
            states = rows[ROWS:].astype(bf16)
            for quarter in range(2):
                z_states[group * 4 + 2 * side + quarter] = states[
                    :, QX * quarter : QX * (quarter + 1)
                ].reshape(2, 16, QX)

    def pair_out(step):
        return pltpu.make_async_remote_copy(
            src_ref=z_states.at[pl.ds(theirs + 4 * step, 4)],
            dst_ref=z_partner.at[pl.ds(4 * step, 4)],
            send_sem=pair_sems.at[0, step],
            recv_sem=pair_sems.at[1, step],
            device_id={"pz": partner},
            device_id_type=MESH,
        )

    def pair_back():
        return pltpu.make_async_remote_copy(
            src_ref=z_give,
            dst_ref=z_carry.at[pl.ds(mine, half_z)],
            send_sem=pair_sems.at[0, 4],
            recv_sem=pair_sems.at[1, 4],
            device_id={"pz": partner},
            device_id_type=MESH,
        )

    def pair_returned():
        return pltpu.make_async_remote_copy(
            src_ref=z_give,
            dst_ref=z_carry.at[pl.ds(theirs, half_z)],
            send_sem=pair_sems.at[0, 4],
            recv_sem=pair_sems.at[1, 4],
            device_id={"pz": partner},
            device_id_type=MESH,
        )

    def z_out(tile):
        return pltpu.make_async_remote_copy(
            src_ref=z_send.at[tile],
            dst_ref=z_recv.at[chip, lax.rem(tile, tiles_z)],
            send_sem=z_sems.at[0, tile],
            recv_sem=z_sems.at[1, chip * tiles_z + lax.rem(tile, tiles_z)],
            device_id=twin(tile // tiles_z),
            device_id_type=MESH,
        )

    def z_in(step, tile):
        peer = lax.rem(chip + step, chips)
        return pltpu.make_async_remote_copy(
            src_ref=z_send.at[tile],
            dst_ref=z_recv.at[peer, tile],
            send_sem=z_sems.at[0, tile],
            recv_sem=z_sems.at[1, peer * tiles_z + tile],
            device_id=twin(peer),
            device_id_type=MESH,
        )

    def z_return(step):
        peer = lax.rem(chip + step, chips)
        return pltpu.make_async_remote_copy(
            src_ref=z_back.at[peer],
            dst_ref=z_chip.at[pl.ds(chip * tiles_z, tiles_z)],
            send_sem=z_back_sems.at[0, peer],
            recv_sem=z_back_sems.at[1, chip],
            device_id=twin(peer),
            device_id_type=MESH,
        )

    def z_returned(step):
        peer = lax.rem(chip + step, chips)
        return pltpu.make_async_remote_copy(
            src_ref=z_back.at[chip],
            dst_ref=z_chip.at[pl.ds(peer * tiles_z, tiles_z)],
            send_sem=z_back_sems.at[0, chip],
            recv_sem=z_back_sems.at[1, peer],
            device_id=twin(peer),
            device_id_type=MESH,
        )

    lead = core == 0
    block_step = (z_step.real, z_step.imag)
    chip_step = z_step * z_step

    def parts(array):
        array = array.astype(f32)
        return array[0:8], array[8:16]

    def choose(first, second):
        return jnp.where(lead, first[0], second[0]), jnp.where(lead, first[1], second[1])

    def joined(value):
        return jnp.concatenate(value, axis=0).astype(bf16)

    def order(count):
        if count < GROUPS // 2:
            return theirs // 4 + count
        return mine // 4 + lax.rem(count + chip // 4, GROUPS // 2)

    def merge(step):
        pair_out(step).wait_recv()
        for at in range(4):
            tile = step * 4 + at
            own = [parts(z_states[mine + tile, side]) for side in range(2)]
            other = [parts(z_partner[tile, side]) for side in range(2)]
            left = cadd(choose(other[0], own[0]), cmul(choose(own[0], other[0]), block_step))
            right = cadd(choose(own[1], other[1]), cmul(choose(other[1], own[1]), block_step))
            z_send[tile, 0] = joined(left)
            z_send[tile, 1] = joined(right)
        for at in range(4):
            tile = step * 4 + at
            owner = tile // tiles_z

            @pl.when(owner != chip)
            def _():
                z_out(tile).start()

            @pl.when(owner == chip)
            def _():
                z_recv[chip, lax.rem(tile, tiles_z)] = z_send[tile]

    def kicked(count, fresh):
        for copy in load(order(count)):
            copy.wait()
        kick_group(order(count), fresh)

    fresh = (fresh_a, fresh_b)
    kicked(0, fresh[0])
    for count in range(GROUPS):
        if count + 1 < GROUPS:
            for copy in load(order(count + 1)):
                copy.wait()
        solve_group(order(count), fresh[count % 2])
        if count + 1 < GROUPS:
            kick_group(order(count + 1), fresh[(count + 1) % 2])
        if count == 0:
            pl.semaphore_wait(barrier, chips + count_py - 1)
        if count < GROUPS // 2:
            pair_out(count).start()
        else:
            merge(order(count) - mine // 4)

    for copy in table_copies:
        copy.wait()

    def sweep_field():
        def fetch(n):
            group, row = n // 8, n % 8 * BZ
            return tuple(
                grid[group, start : start + BZ, :] for start in (row, row + ROWS // 2)
            )

        def gain(n):
            line = slice(n, n + 1)
            return [
                (gains[2 * residue, line, :], gains[2 * residue + 1, line, :])
                for residue in range(4)
            ]

        def put(n, done):
            for at in range(2):
                start = (n + at) * BZ
                for part in range(2):
                    swept[part, start : start + BZ, :] = done[at][part].astype(bf16)

        x_sweep(BY, fetch, gain, put, left_buf, cells_buf, xf, xi)

    steps_y = [(step_ref[2 * n : 2 * n + 1], step_ref[2 * n + 1 : 2 * n + 2]) for n in range(4)]
    forward_step, backward_step, turn_step, whole_gain = steps_y

    def y_rows(cell):
        return pl.ds(pl.multiple_of(cell * BZ, BZ), BZ)

    def save(rows, value):
        for part in range(2):
            for quarter in range(4):
                solved[part, quarter, rows, :] = value[part][
                    :, QX * quarter : QX * (quarter + 1)
                ]

    def y_forward():
        def advance(cell, totals):
            total, other = totals
            rows = y_rows(cell)
            value = tuple(swept[part, rows, :].astype(f32) for part in range(2))
            total = cadd(value, cmul(total, forward_step))
            save(rows, total)
            share = tuple(weight[2 + part, pl.ds(cell, 1), :] for part in range(2))
            return total, cadd(other, cmul(value, share))

        zero = jnp.zeros((BZ, NX), f32)
        return lax.fori_loop(0, BY, advance, ((zero, zero), (zero, zero)), unroll=4)

    def y_backward(first, last, total):
        def advance(count, total):
            rows = y_rows(BY - 1 - count)
            value = tuple(
                jnp.concatenate([solved[part, quarter, rows, :] for quarter in range(4)], axis=1)
                for part in range(2)
            )
            total = cadd(value, cmul(total, backward_step))
            out = cmul(total, whole_gain)
            save(rows, [out[part] - swept[part, rows, :].astype(f32) for part in range(2)])
            return total

        return lax.fori_loop(first, last, advance, total, unroll=4)

    def y_states(count):
        @pl.loop(0, count)
        def _(at):
            for quarter in range(4):
                lanes = slice(QX * quarter, QX * (quarter + 1))
                total = [[0.0, 0.0], [0.0, 0.0]]
                for start in range(0, BY, 16):
                    rows = slice(start, start + 16)
                    value = [planes[part, at, rows, lanes].astype(f32) for part in range(2)]
                    for side in range(2):
                        some = cmul(
                            value, (weight[2 * side, rows, lanes], weight[2 * side + 1, rows, lanes])
                        )
                        for part in range(2):
                            total[side][part] += some[part][0:8] + some[part][8:16]
                for side in range(2):
                    for part in range(2):
                        row = pl.multiple_of((side * 2 + part) * 16 + at * 8, 8)
                        sums[pl.ds(row, 8), lanes] = total[side][part]

        rows = 0.0
        for quarter in range(4):
            some = sums[:, QX * quarter : QX * (quarter + 1)].astype(bf16)
            rows += jnp.dot(add_ref[quarter], some, preferred_element_type=f32)
        return rows.astype(bf16)

    def y_periodic(plane):
        for side in range(2):
            lanes = slice(side * NX // 2, (side + 1) * NX // 2)
            block = jnp.concatenate([planes[part, plane, :, lanes] for part in range(2)], axis=0)
            modes = jnp.dot(yf_ref[...], block, preferred_element_type=f32)
            scaled = [
                cmul(
                    (modes[some : some + 32], modes[BY + some : BY + some + 32]),
                    (factor[0, some : some + 32, lanes], factor[1, some : some + 32, lanes]),
                )
                for some in range(0, BY, 32)
            ]
            block = jnp.concatenate(
                [one[part].astype(bf16) for part in range(2) for one in scaled], axis=0
            )
            cells = jnp.dot(yi_ref[...], block, preferred_element_type=f32).astype(bf16)
            for part in range(2):
                planes[part, plane, :, lanes] = cells[part * BY : (part + 1) * BY]

    class Exchange:
        def __init__(self, send, recv, back, carry, sems, tiles):
            self.send, self.recv, self.back, self.carry = send, recv, back, carry
            self.sems, self.tiles = sems, tiles

        def mine(self):
            return pl.ds(me_y * self.tiles, self.tiles)

        def out(self, peer):
            return pltpu.make_async_remote_copy(
                src_ref=self.send.at[pl.ds(peer * self.tiles, self.tiles)],
                dst_ref=self.recv.at[me_y],
                send_sem=self.sems.at[0, peer],
                recv_sem=self.sems.at[1, me_y],
                device_id={"py": peer},
                device_id_type=MESH,
            )

        def arrived(self, peer):
            return pltpu.make_async_remote_copy(
                src_ref=self.send.at[self.mine()],
                dst_ref=self.recv.at[peer],
                send_sem=self.sems.at[0, me_y],
                recv_sem=self.sems.at[1, peer],
                device_id={"py": peer},
                device_id_type=MESH,
            )

        def give(self, peer):
            return pltpu.make_async_remote_copy(
                src_ref=self.back.at[peer],
                dst_ref=self.carry.at[self.mine()],
                send_sem=self.sems.at[2, peer],
                recv_sem=self.sems.at[3, me_y],
                device_id={"py": peer},
                device_id_type=MESH,
            )

        def given(self, peer):
            return pltpu.make_async_remote_copy(
                src_ref=self.back.at[me_y],
                dst_ref=self.carry.at[pl.ds(peer * self.tiles, self.tiles)],
                send_sem=self.sems.at[2, me_y],
                recv_sem=self.sems.at[3, peer],
                device_id={"py": peer},
                device_id_type=MESH,
            )

        def post(self):
            @pl.loop(1, count_py)
            def _(step):
                self.out(lax.rem(me_y + step, count_py)).start()

        def answer(self):
            self.recv[me_y] = self.send[self.mine()]

            @pl.loop(1, count_py)
            def _(step):
                self.arrived(lax.rem(me_y + step, count_py)).wait_recv()

            for tile in range(self.tiles):
                solve_tile(self.recv, self.back, tile, lax.rem(me_y * self.tiles + tile, 4))

            @pl.loop(1, count_py)
            def _(step):
                self.give(lax.rem(me_y + step, count_py)).start()

            self.carry[self.mine()] = self.back[me_y]

        def receive(self):
            @pl.loop(1, count_py)
            def _(step):
                self.given(lax.rem(me_y + step, count_py)).wait_recv()

        def close(self):
            @pl.loop(1, count_py)
            def _(step):
                peer = lax.rem(me_y + step, count_py)
                self.out(peer).wait_send()
                self.give(peer).wait_send()

        def rows(self, tiles):
            return [self.carry[tile].reshape(CARRY, QX) for tile in tiles]

    def solve_tile(recv, back, tile, quarter):
        table = ytab_ref[quarter]
        value = [(table[2 * n : 2 * n + 1], table[2 * n + 1 : 2 * n + 2]) for n in range(8)]
        whole1, whole2, _, _, wrap1, wrap2, out1, out2 = value
        left_state = [parts(recv[block, tile, 0]) for block in range(count_py)]
        right_state = [parts(recv[block, tile, 1]) for block in range(count_py)]
        left, right = left_state[0], right_state[count_py - 1]
        for block in range(1, count_py):
            left = cadd(left_state[block], cmul(left, whole1))
            right = cadd(right_state[count_py - 1 - block], cmul(right, whole2))
        left, right = cmul(left, wrap1), cmul(right, wrap2)
        for block in range(count_py):
            other = count_py - 1 - block
            back[block, tile, 0] = joined(cmul(left, out1))
            back[other, tile, 1] = joined(cmul(right, out2))
            left = cadd(left_state[block], cmul(left, whole1))
            right = cadd(right_state[other], cmul(right, whole2))

    planes_y = Exchange(y_send, y_recv, y_back, y_carry, y_sems, TILES_Y // count_py)
    def carry_out(step):
        return pltpu.make_async_remote_copy(
            src_ref=c_send,
            dst_ref=c_recv.at[me_y],
            send_sem=c_sems.at[0, lax.rem(me_y + step, count_py)],
            recv_sem=c_sems.at[1, me_y],
            device_id={"py": lax.rem(me_y + step, count_py)},
            device_id_type=MESH,
        )

    def carry_in(step):
        peer = lax.rem(me_y + step, count_py)
        return pltpu.make_async_remote_copy(
            src_ref=c_send,
            dst_ref=c_recv.at[peer],
            send_sem=c_sems.at[0, me_y],
            recv_sem=c_sems.at[1, peer],
            device_id={"py": peer},
            device_id_type=MESH,
        )

    def carry_solve():
        value = [(packed_ref[2 * n], packed_ref[2 * n + 1]) for n in range(8)]
        whole1, whole2, own1, own2, wrap1, wrap2, out1, out2 = value
        own = [parts(c_send[side]) for side in range(2)]
        left, right = own
        for step in range(1, count_py):
            left = cadd(parts(c_recv[lax.rem(me_y + step, count_py), 0]), cmul(left, whole1))
            back = lax.rem(me_y + count_py - step, count_py)
            right = cadd(parts(c_recv[back, 1]), cmul(right, whole2))
        left = csub(cmul(left, wrap1), cmul(own[0], own1))
        right = csub(cmul(right, wrap2), cmul(own[1], own2))
        return jnp.concatenate([joined(cmul(left, out1)), joined(cmul(right, out2))], axis=0)

    def post_planes(states):
        for half in range(2):
            lines = slice(8 * half, 8 * half + 8)
            for quarter in range(4):
                lanes = slice(QX * quarter, QX * (quarter + 1))
                for side in range(2):
                    y_send[half * 4 + quarter, side] = joined(
                        [states[side][part][lines, lanes] for part in range(2)]
                    )
        planes_y.post()

    sweep_field()
    forward_state, backward_state = y_forward()
    post_planes((forward_state, backward_state))

    @pl.loop(1, chips)
    def _(step):
        for tile in range(tiles_z):
            z_in(step, tile).wait_recv()

    for tile in range(tiles_z):

        def state(block, side):
            return parts(z_recv[block, tile, side])

        def advance(total, value):
            return cadd(cmul(total, (chip_step.real, chip_step.imag)), value)

        def gather(step, carry):
            left, right = carry
            return (
                advance(left, state(step, 0)),
                advance(right, state(chips - 1 - step, 1)),
            )

        zero = (jnp.zeros((8, QX), f32), jnp.zeros((8, QX), f32))
        left, right = lax.fori_loop(0, chips, gather, (zero, zero), unroll=8)
        wrap = 1 / (1 - chip_step**chips)
        left = cmul(left, (wrap.real, wrap.imag))
        right = cmul(right, (wrap.real, wrap.imag))

        def hand_out(step, carry):
            left, right = carry
            last = chips - 1 - step
            z_back[step, tile, 0] = joined(left)
            z_back[last, tile, 1] = joined(right)
            return advance(left, state(step, 0)), advance(right, state(last, 1))

        lax.fori_loop(0, chips, hand_out, (left, right), unroll=8)

    @pl.loop(1, chips)
    def _(step):
        z_return(step).start()

    z_chip[pl.ds(chip * tiles_z, tiles_z)] = z_back[chip]

    back_total = y_backward(0, BY // 2, cmul(forward_state, turn_step))

    @pl.loop(1, chips)
    def _(step):
        z_returned(step).wait_recv()

    def split_carry(tile, _):
        own = [parts(z_states[mine + tile, side]) for side in range(2)]
        other = [parts(z_partner[tile, side]) for side in range(2)]
        whole = [parts(z_chip[tile, side]) for side in range(2)]
        inner_left = cadd(choose(own[0], other[0]), cmul(whole[0], block_step))
        inner_right = cadd(choose(other[1], own[1]), cmul(whole[1], block_step))
        z_give[tile, 0] = joined(choose(inner_left, whole[0]))
        z_give[tile, 1] = joined(choose(whole[1], inner_right))
        z_carry[mine + tile, 0] = joined(choose(whole[0], inner_left))
        z_carry[mine + tile, 1] = joined(choose(inner_right, whole[1]))
        return 0

    lax.fori_loop(0, half_z, split_carry, 0, unroll=4)
    pair_back().start()

    y_backward(BY // 2, BY, back_total)
    pair_returned().wait_recv()

    def fetch(n):
        sides = [
            jnp.concatenate([z_carry[n * 4 + quarter, side] for quarter in range(4)], axis=1)
            for side in range(2)
        ]
        sides = [side.astype(f32) for side in sides]
        return tuple(
            jnp.concatenate([side[8 * part : 8 * part + 8] for side in sides], axis=0).astype(bf16)
            for part in range(2)
        )

    def put(n, done):
        for side in range(2):
            lines = slice(8 * side, 8 * side + 8)
            for part in range(2):
                planes[part, side, 8 * n : 8 * n + 16, :] = jnp.concatenate(
                    [done[at][part][lines] for at in range(2)], axis=0
                ).astype(bf16)

    def gain(n):
        lines = slice(8 * n, 8 * n + 8)
        return [
            tuple(
                jnp.concatenate([gains[2 * residue + part, lines, :]] * 2, axis=0)
                for part in range(2)
            )
            for residue in range(4)
        ]

    x_sweep(GROUPS, fetch, gain, put, left_buf, cells_buf, xf, xi)
    c_send[...] = y_states(2).reshape(2, 16, QX)

    @pl.loop(1, count_py)
    def _(step):
        carry_out(step).start()

    planes_y.answer()
    y_periodic(0)
    y_periodic(1)

    def store(pair):
        rows = pl.ds(pl.multiple_of(pair * 16, 16), 16)
        return pltpu.make_async_copy(
            result.at[:, :, rows, :], field_hbm.at[:, :, rows, :], out_sem.at[pair]
        )

    @pl.loop(0, BY // 16)
    def _(pair):
        rows = pl.ds(pl.multiple_of(pair * 16, 16), 16)
        for quarter in range(4):
            lanes = slice(QX * quarter, QX * (quarter + 1))
            left, right = [
                tuple(planes[part, one, rows, lanes] for part in range(2)) for one in range(2)
            ]
            for plane in range(BZ):
                first, second = (complex(one) for one in z_profile[plane])
                lines = pl.ds(pair * 16 * BZ + plane, 16, stride=BZ)
                value = tuple(solved[part, quarter, lines, :].astype(bf16) for part in range(2))
                value = cadd(value, cmul(left, (first.real, first.imag)))
                value = cadd(value, cmul(right, (second.real, second.imag)))
                for part in range(2):
                    result[part, plane, rows, lanes] = value[part]
        store(pair).start()

    @pl.loop(0, half_z)
    def _(tile):
        @pl.when(tile // tiles_z != chip)
        def _():
            z_out(tile).wait_send()

    @pl.loop(1, chips)
    def _(step):
        z_return(step).wait_send()

    @pl.loop(0, GROUPS // 2)
    def _(step):
        pair_out(step).wait_send()

    pair_back().wait_send()

    @pl.loop(1, count_py)
    def _(step):
        carry_in(step).wait_recv()

    carried = carry_solve()
    planes_y.receive()
    for quarter in range(4):
        rows = planes_y.rows((quarter, 4 + quarter)) + [carried]
        change[:, :, QX * quarter : QX * (quarter + 1)] = jnp.dot(
            turn_ref[quarter], jnp.concatenate(rows, axis=0), preferred_element_type=f32
        ).reshape(BZ, 8, QX)
    last = pltpu.make_async_copy(change, change_hbm, out_sem.at[GROUPS // 2])
    last.start()

    planes_y.close()

    @pl.loop(1, count_py)
    def _(step):
        carry_out(step).wait_send()


    @pl.loop(0, GROUPS // 2)
    def _(pair):
        store(pair).wait()

    last.wait()


PLANES = 2


def finish_kernel(
    field_hbm,
    change_hbm,
    pot_hbm,
    table_hbm,
    out_hbm,
    field,
    change,
    pot,
    table,
    out,
    in_sem,
    tab_sem,
    out_sem,
):
    steps = BZ // PLANES

    def load(step):
        planes = pl.ds(step * PLANES, PLANES)
        return (
            pltpu.make_async_copy(field_hbm.at[:, planes], field.at[:, planes], in_sem.at[0, step]),
            pltpu.make_async_copy(pot_hbm.at[planes], pot.at[planes], in_sem.at[1, step]),
        )

    def save(step):
        planes = pl.ds(step * PLANES, PLANES)
        return pltpu.make_async_copy(out.at[:, planes], out_hbm.at[:, planes], out_sem.at[step])

    tables = (
        pltpu.make_async_copy(change_hbm, change, tab_sem.at[0]),
        pltpu.make_async_copy(table_hbm, table, tab_sem.at[1]),
    )
    for copy in tables:
        copy.start()
    for step in range(steps):
        for copy in load(step):
            copy.start()
    for copy in tables:
        copy.wait()

    def finish(at, lanes):
        ends = [change[at, row : row + 1, lanes].astype(bf16) for row in range(4)]
        for start in range(0, BY, 16):
            rows = slice(start, start + 16)
            value = tuple(field[part, at, rows, lanes] for part in range(2))
            for side in range(2):
                profile = (table[2 * side, rows, lanes], table[2 * side + 1, rows, lanes])
                value = cadd(value, cmul(profile, (ends[2 * side], ends[2 * side + 1])))
            new = kick(value[0].astype(f32), value[1].astype(f32), pot[at, rows, lanes])
            for part in range(2):
                out[part, at, rows, lanes] = new[part]

    @pl.loop(0, steps)
    def _(step):
        for copy in load(step):
            copy.wait()
        for one in range(PLANES):
            for side in range(2):
                finish(step * PLANES + one, slice(side * NX // 2, (side + 1) * NX // 2))
        save(step).start()

    @pl.loop(0, steps)
    def _(step):
        save(step).wait()


def shards(count_py, count_pz, wavefunction, potential):
    forward_x, inverse_x, trig = x_tables()
    z_rows, turn, z_profile, z_step = z_tables()
    forward_y, inverse_y, factor, weight, homogeneous, steps_y, add, y_table, packed = y_tables(count_py)

    def low(array):
        return jnp.asarray(array.astype(np.float32)).astype(bf16)

    def full(array):
        return jnp.asarray(array.astype(np.float32))

    chips = count_pz // 2
    tiles_z = TILES_Z // 2 // chips
    tiles_y = TILES_Y // count_py
    anywhere = pl.BlockSpec(memory_space=pl.ANY)
    inside = pl.BlockSpec(memory_space=pltpu.VMEM)
    field, change = pl.pallas_call(
        functools.partial(main_kernel, count_py, count_pz, z_step, z_profile),
        out_shape=(
            pltpu.VMEM((2, BZ, BY, NX), bf16),
            pltpu.VMEM((BZ, 8, NX), f32),
        ),
        in_specs=[anywhere] * 6 + [inside] * 9,
        out_specs=(anywhere, anywhere),
        scratch_shapes=[
            pltpu.VMEM((GROUPS, 2, BZ, 8, NX), f32),
            pltpu.VMEM((GROUPS, BZ, 8, NX), f32),
            pltpu.VMEM((4, 2 * QX, 2 * QX), bf16),
            pltpu.VMEM((4, 2 * QX, 2 * QX), bf16),
            pltpu.VMEM(weight.shape, f32),
            pltpu.VMEM(factor.shape, f32),
            pltpu.VMEM((ROWS, NX), bf16),
            pltpu.VMEM((ROWS, NX), bf16),
            pltpu.VMEM((8, BY, QX), f32),
            pltpu.VMEM((GROUPS, ROWS, NX), bf16),
            pltpu.VMEM((2, BY * BZ, NX), bf16),
            pltpu.VMEM((2, 4, BY * BZ, QX), f32),
            pltpu.VMEM((2, 2, BY, NX), bf16),
            pltpu.VMEM((2, BZ, BY, NX), bf16),
            pltpu.VMEM((4, BY * BZ, 2 * QX), bf16),
            pltpu.VMEM((4, BY * BZ, 2 * QX), f32),
            pltpu.VMEM((64, NX), f32),
            pltpu.VMEM((TILES_Z, 2, 16, QX), bf16),
            pltpu.VMEM((TILES_Z // 2, 2, 16, QX), bf16),
            pltpu.VMEM((TILES_Z // 2, 2, 16, QX), bf16),
            pltpu.VMEM((chips, tiles_z, 2, 16, QX), bf16),
            pltpu.VMEM((chips, tiles_z, 2, 16, QX), bf16),
            pltpu.VMEM((TILES_Z // 2, 2, 16, QX), bf16),
            pltpu.VMEM((TILES_Z // 2, 2, 16, QX), bf16),
            pltpu.VMEM((TILES_Z, 2, 16, QX), bf16),
            pltpu.VMEM((TILES_Y, 2, 16, QX), bf16),
            pltpu.VMEM((count_py, tiles_y, 2, 16, QX), bf16),
            pltpu.VMEM((count_py, tiles_y, 2, 16, QX), bf16),
            pltpu.VMEM((TILES_Y, 2, 16, QX), bf16),
            pltpu.VMEM((2, 16, QX), bf16),
            pltpu.VMEM((count_py, 2, 16, QX), bf16),
            pltpu.VMEM((BZ, 8, NX), f32),
            pltpu.SemaphoreType.DMA((2, GROUPS)),
            pltpu.SemaphoreType.DMA((4,)),
            pltpu.SemaphoreType.DMA((GROUPS // 2 + 1,)),
            pltpu.SemaphoreType.DMA((2, 5)),
            pltpu.SemaphoreType.DMA((2, TILES_Z // 2)),
            pltpu.SemaphoreType.DMA((2, chips)),
            pltpu.SemaphoreType.DMA((4, count_py)),
            pltpu.SemaphoreType.DMA((2, count_py)),
        ],
        compiler_params=pltpu.CompilerParams(
            collective_id=0, has_side_effects=True, vmem_limit_bytes=57 * 2**20
        ),
        cost_estimate=pl.CostEstimate(
            flops=3_000_000_000, bytes_accessed=10_000_000, transcendentals=0
        ),
        name="sweeps",
    )(
        wavefunction,
        potential,
        low(forward_x),
        low(inverse_x),
        full(weight),
        full(factor),
        full(trig),
        low(z_rows),
        low(forward_y),
        low(inverse_y),
        low(add),
        low(turn),
        full(y_table),
        full(steps_y),
        full(packed),
    )
    return pl.pallas_call(
        finish_kernel,
        out_shape=jax.ShapeDtypeStruct((2, BZ, BY, NX), f32),
        in_specs=[anywhere] * 4,
        out_specs=anywhere,
        scratch_shapes=[
            pltpu.VMEM((2, BZ, BY, NX), bf16),
            pltpu.VMEM((BZ, 8, NX), f32),
            pltpu.VMEM((BZ, BY, NX), f32),
            pltpu.VMEM(homogeneous.shape, bf16),
            pltpu.VMEM((2, BZ, BY, NX), f32),
            pltpu.SemaphoreType.DMA((2, BZ // PLANES)),
            pltpu.SemaphoreType.DMA((2,)),
            pltpu.SemaphoreType.DMA((BZ // PLANES,)),
        ],
        compiler_params=pltpu.CompilerParams(vmem_limit_bytes=16 * 2**20),
        cost_estimate=pl.CostEstimate(
            flops=800_000_000, bytes_accessed=9_000_000, transcendentals=0
        ),
        name="finish",
    )(field, change, potential, low(homogeneous))


def solution(mesh):
    return jax.shard_map(
        functools.partial(shards, mesh.shape["py"], mesh.shape["pz"]),
        mesh=mesh,
        in_specs=(P(None, "pz", "py", None), P("pz", "py", None)),
        out_specs=P(None, "pz", "py", None),
        check_vma=False,
    )
```
